32 devices in a mesh: vocab: 4 (over y, x), ctx: 8 (over z, core).
Axes of the slice: x: 2, y: 2, z: 4, core: 2. Of those that a mesh axis runs over, the one named last changes fastest.
Arguments:
- hidden: bfloat16 [1024, 8192], P('ctx', 'vocab'), may hold values from -20 to 20
- norm_gain: float32 [8192], replicated, may hold values from 0.5 to 1.5
- head_weight: bfloat16 [152064, 8192], P(('vocab', 'ctx')), may hold values from -16 to 16
- targets: int32 [64], replicated, may hold values from 0 to 152063
- loss_rows: int32 [64], replicated, may hold values from 0 to 127, as said below
- stretch_of_slot: int32 [16], replicated, may hold values from 0 to 15, as said below
- queries: bfloat16 [1024, 8192], P('ctx', 'vocab'), may hold values from -20 to 20
- key_states: bfloat16 [1024, 1024], P('ctx', 'vocab'), may hold values from -20 to 20
- attention_values: bfloat16 [1024, 1024], P('ctx', 'vocab'), may hold values from -6 to 6
- output_weight: bfloat16 [8192, 8192], P('vocab', 'ctx'), may hold values from -0.0625 to 0.0625
Outputs:
- mean_loss: float32 [], replicated
- query_grad: bfloat16 [64, 8192], P('ctx', 'vocab')
- key_gradient: bfloat16 [1024, 1024], P('ctx', 'vocab')
- value_gradient: bfloat16 [1024, 1024], P('ctx', 'vocab')
- resid_grad: bfloat16 [8192, 64], P('ctx')
The draws below stay inside these ranges and needn't reach their ends.
Inputs may be any that keep to these rules, and one draw needn't show every extreme that they name: `loss_rows`: within each block of 8 entries, entry j lies in rows j * 16 to (j + 1) * 16 - 1. `stretch_of_slot`: A permutation of the stretches in which slots 2c and 2c+1 hold stretches that sum to 15.
All inputs are finite; a program needn't handle non-finite values.
Results may differ from the reference program's by a relative error of at most 0.023.
Values may be sent and summed in bfloat16 or wider, within the bound.
No kernel may reach another device: no remote copies, remote signals or barrier semaphores. Data moves between devices by JAX's collectives and lax.ppermute only.
A program may use at most 128 MiB of HBM per device.

```python
import math
import jax
import jax.numpy as jnp
import numpy as np
from jax import lax

D = 8192
QUERY_HEAD_COUNT = 64
KEY_VALUE_HEADS = 8
HEAD_SIZE = 128
VOCAB = 152064
CH = 64
STRIDE = 16
T_DEV = 128
LPD = 8
STRETCHES = 16
SEQUENCE_TOKENS = 1024
LOSS = 64


def index_tables(key):
    half_count = STRETCHES // 2
    order_perm = jax.random.permutation(jax.random.fold_in(key, 101), half_count).astype(jnp.int32)
    flip_bits = jax.random.randint(jax.random.fold_in(key, 102), (half_count,), 0, 2).astype(jnp.int32)
    mirror = STRETCHES - 1 - order_perm
    leading = jnp.where(flip_bits == 1, mirror, order_perm)
    trailing = jnp.where(flip_bits == 1, order_perm, mirror)
    stretch_table = jnp.stack([leading, trailing], axis=1).reshape(STRETCHES).astype(jnp.int32)
    offsets = jax.random.randint(jax.random.fold_in(key, 103), (half_count, LPD), 0, STRIDE).astype(jnp.int32)
    offsets = offsets.at[0, 0].set(0).at[0, LPD - 1].set(STRIDE - 1)
    local_rows = offsets + STRIDE * jnp.arange(LPD, dtype=jnp.int32)[None, :]
    return (local_rows.reshape(LOSS).astype(jnp.int32), stretch_table)


def draw_loss_rows(key, part):
    return index_tables(key)[0]


def draw_stretch_of_slot(key, part):
    return index_tables(key)[1]


def hidden_field(key):
    normal_part = jnp.clip(jax.random.normal(jax.random.fold_in(key, 201), (SEQUENCE_TOKENS, D), jnp.float32), -6.0, 6.0)
    return normal_part.astype(jnp.bfloat16)


def draw_hidden(key, part):
    return hidden_field(key)


def draw_head_weight(key, part):
    weights = 3.0 * D ** (-0.5) * jnp.clip(jax.random.normal(jax.random.fold_in(key, 301), (VOCAB, D), jnp.float32), -6.0, 6.0)
    return weights.astype(jnp.bfloat16)


def draw_queries(key, part):
    value_rows_full = jnp.clip(jax.random.normal(jax.random.fold_in(key, 411), (SEQUENCE_TOKENS, QUERY_HEAD_COUNT * HEAD_SIZE), jnp.float32), -6.0, 6.0)
    return value_rows_full.astype(jnp.bfloat16)


def draw_key_states(key, part):
    value_rows_full = jnp.clip(jax.random.normal(jax.random.fold_in(key, 421), (SEQUENCE_TOKENS, KEY_VALUE_HEADS * HEAD_SIZE), jnp.float32), -6.0, 6.0)
    return value_rows_full.astype(jnp.bfloat16)


def set_ends(drawn, key, low, largest):
    extent = drawn.shape
    index_at = [jax.random.randint(jax.random.fold_in(key, axis), (), 0, extent[axis]) for axis in range(len(extent))]
    drawn = drawn.at[tuple(index_at)].set(low)
    longest = extent.index(max(extent))
    index_at[longest] = (index_at[longest] + 1) % extent[longest]
    return drawn.at[tuple(index_at)].set(largest)


def levels(own_key, extent, pieces, least, top_value):
    def one(dim, blocks):
        steps = jax.random.uniform(jax.random.fold_in(jax.random.fold_in(own_key, 6), dim), (blocks,), jnp.float32, least / len(pieces), top_value / len(pieces))
        return jnp.repeat(jnp.exp(steps), extent[dim] // blocks).reshape((-1,) + (1,) * (len(extent) - dim - 1))

    gain = one(*pieces[0])
    for cut in pieces[1:]:
        gain = gain * one(*cut)
    return gain


def wide_ids(stream_key, shape, amount, skew):
    weights = [min(1 << octave, amount + 1 - (1 << octave)) * (1 << 20) // math.isqrt((1 << octave) ** skew) + 1 for octave in range((amount + 1).bit_length()) if 1 << octave <= amount]
    deviation = 1 + sum(weights) // (1 << 30)
    listing = np.cumsum(np.array([max(1, weight // deviation) for weight in weights]))
    pick = jax.random.randint(jax.random.fold_in(stream_key, 1), shape, 0, int(listing[len(weights) - 1]))
    start = jnp.left_shift(1, jnp.searchsorted(jnp.asarray(listing, jnp.int32), pick, side="right").astype(jnp.int32))
    standing = start - 1 + jax.random.randint(jax.random.fold_in(stream_key, 4), shape, 0, 1 << 30) % jnp.minimum(start, amount + 1 - start)
    return jax.random.permutation(jax.random.fold_in(stream_key, 2), amount)[standing].astype(jnp.int32)


def normal_values(stream_key, extent, scale, most, split=(), kind=jnp.bfloat16):
    array = scale * jax.random.normal(stream_key, extent, jnp.float32)
    if split:
        array = array * levels(stream_key, extent, split, -0.22, 0.18)
    return jnp.clip(array, -most, most).astype(kind)


def setup_inputs(seed: int = 0) -> dict:
    keys = jax.random.split(jax.random.key(seed), 11)
    hidden = draw_hidden(jax.random.fold_in(keys[10], 71), 0)
    norm_gain = jnp.clip(1.0 + 0.1 * jax.random.normal(keys[1], (D,), jnp.float32), 0.5, 1.5)
    head_weight = draw_head_weight(jax.random.fold_in(keys[10], 71), 0)
    targets = set_ends(wide_ids(keys[3], (LOSS,), VOCAB, 2), jax.random.fold_in(keys[3], 3), 0, VOCAB - 1).astype(jnp.int32)
    loss_rows = draw_loss_rows(jax.random.fold_in(keys[10], 71), 0)
    stretch_of_slot = draw_stretch_of_slot(jax.random.fold_in(keys[10], 71), 0)
    queries = draw_queries(jax.random.fold_in(keys[10], 71), 0)
    key_states = draw_key_states(jax.random.fold_in(keys[10], 71), 0)
    attention_values = normal_values(keys[8], (SEQUENCE_TOKENS, KEY_VALUE_HEADS * HEAD_SIZE), 1.0, 6.0, ((0, 8), (1, 4)))
    output_weight = normal_values(keys[9], (QUERY_HEAD_COUNT * HEAD_SIZE, D), (QUERY_HEAD_COUNT * HEAD_SIZE) ** -0.5, 0.0625, ((0, 4), (1, 8)))
    return dict(hidden=hidden, norm_gain=norm_gain, head_weight=head_weight, targets=targets, loss_rows=loss_rows, stretch_of_slot=stretch_of_slot, queries=queries, key_states=key_states, attention_values=attention_values, output_weight=output_weight)


norm_eps = 1e-06
grad_weight = 16.0
masked_fill = -1e+30

def head_attention(query_heads, grad_heads, query_pos, key_heads, value_heads, key_pos):
    score_scale = HEAD_SIZE ** (-0.5)
    highest = lax.Precision.HIGHEST
    query_f = query_heads.astype(jnp.float32)
    grad_f = grad_heads.astype(jnp.float32)
    key_f = key_heads.astype(jnp.float32)
    value_f = value_heads.astype(jnp.float32)
    scores = jnp.einsum('tgd,sd->gts', query_f, key_f, precision=highest) * score_scale
    visible = key_pos[None, None, :] <= query_pos[None, :, None]
    masked = jnp.where(visible, scores, masked_fill)
    top_score = lax.optimization_barrier(jnp.max(masked, axis=2, keepdims=True))
    raw_weights = jnp.where(visible, jnp.exp(masked - top_score), 0.0)
    prob_full = raw_weights / lax.optimization_barrier(jnp.sum(raw_weights, axis=2, keepdims=True))
    output = jnp.einsum('gts,sd->gtd', prob_full, value_f, precision=highest)
    row_delta = lax.optimization_barrier(jnp.sum(output * jnp.transpose(grad_f, (1, 0, 2)), axis=2))
    prob_half = prob_full.astype(jnp.bfloat16).astype(jnp.float32)
    prob_grad = jnp.einsum('tgd,sd->gts', grad_f, value_f, precision=highest)
    score_grad = (prob_full * (prob_grad - row_delta[:, :, None])).astype(jnp.bfloat16).astype(jnp.float32)
    query_term = jnp.einsum('gts,sd->tgd', score_grad, key_f, precision=highest) * score_scale
    key_term = jnp.einsum('gts,tgd->sd', score_grad, query_f, precision=highest) * score_scale
    value_term = jnp.einsum('gts,tgd->sd', prob_half, grad_f, precision=highest)
    return (query_term, key_term, value_term)

def reference(hidden, norm_gain, head_weight, targets, loss_rows, stretch_of_slot, queries, key_states, attention_values, output_weight):
    owner_dev = jnp.arange(LOSS, dtype=jnp.int32) // LPD
    row_ids = (owner_dev * T_DEV + loss_rows).astype(jnp.int32)
    picked = hidden[row_ids].astype(jnp.float32)
    inv_rms = lax.rsqrt(lax.optimization_barrier(jnp.mean(picked * picked, axis=1)) + norm_eps)
    normed = (picked * inv_rms[:, None] * norm_gain[None, :]).astype(jnp.bfloat16)
    logits = jnp.dot(normed, head_weight.T, preferred_element_type=jnp.float32)
    top_score = lax.optimization_barrier(jnp.max(logits, axis=1))
    row_total = lax.optimization_barrier(jnp.sum(jnp.exp(logits - top_score[:, None]), axis=1))
    log_total = top_score + jnp.log(row_total)
    vocab_ids = jnp.arange(VOCAB, dtype=jnp.int32)
    is_target = vocab_ids[None, :] == targets[:, None]
    target_logit = lax.optimization_barrier(jnp.sum(jnp.where(is_target, logits, 0.0), axis=1))
    mean_loss = jnp.mean(log_total - target_logit)
    logit_grad = (grad_weight * (jnp.exp(logits - log_total[:, None]) - is_target.astype(jnp.float32))).astype(jnp.bfloat16)
    normed_grad = jnp.dot(logit_grad, head_weight, preferred_element_type=jnp.float32)
    scaled = normed_grad * norm_gain[None, :]
    unit_rows = picked * inv_rms[:, None]
    inner = lax.optimization_barrier(jnp.sum(scaled * unit_rows, axis=1)) / D
    resid_grad = (inv_rms[:, None] * (scaled - unit_rows * inner[:, None])).astype(jnp.bfloat16)
    attn_grad = jnp.dot(resid_grad, output_weight.T, preferred_element_type=jnp.float32).astype(jnp.bfloat16)
    slot_ids = jnp.arange(SEQUENCE_TOKENS, dtype=jnp.int32)
    key_pos = (stretch_of_slot[slot_ids // CH] * CH + slot_ids % CH).astype(jnp.int32)
    query_pos = key_pos[row_ids]
    query_loss = queries[row_ids]
    query_group_size = QUERY_HEAD_COUNT // KEY_VALUE_HEADS

    def each_head_rows(head_index):
        start = (head_index * query_group_size * HEAD_SIZE).astype(jnp.int32)
        query_heads = lax.dynamic_slice_in_dim(query_loss, start, query_group_size * HEAD_SIZE, 1).reshape(LOSS, query_group_size, HEAD_SIZE)
        grad_heads = lax.dynamic_slice_in_dim(attn_grad, start, query_group_size * HEAD_SIZE, 1).reshape(LOSS, query_group_size, HEAD_SIZE)
        key_start = (head_index * HEAD_SIZE).astype(jnp.int32)
        key_heads = lax.dynamic_slice_in_dim(key_states, key_start, HEAD_SIZE, 1)
        value_heads = lax.dynamic_slice_in_dim(attention_values, key_start, HEAD_SIZE, 1)
        return head_attention(query_heads, grad_heads, query_pos, key_heads, value_heads, key_pos)
    gathered_queries, gathered_keys, gathered_values = lax.map(each_head_rows, jnp.arange(KEY_VALUE_HEADS, dtype=jnp.int32))
    query_grad = jnp.transpose(gathered_queries, (1, 0, 2, 3)).reshape(LOSS, QUERY_HEAD_COUNT * HEAD_SIZE).astype(jnp.bfloat16)
    key_gradient = jnp.transpose(gathered_keys, (1, 0, 2)).reshape(SEQUENCE_TOKENS, KEY_VALUE_HEADS * HEAD_SIZE).astype(jnp.bfloat16)
    value_gradient = jnp.transpose(gathered_values, (1, 0, 2)).reshape(SEQUENCE_TOKENS, KEY_VALUE_HEADS * HEAD_SIZE).astype(jnp.bfloat16)
    return (mean_loss, query_grad, key_gradient, value_gradient, resid_grad.T)
```

```python
import functools

import jax
import jax.numpy as jnp
from jax import lax
from jax.experimental import pallas as pl
from jax.experimental.pallas import tpu as pltpu
from jax.sharding import PartitionSpec as P

HEAD_SIZE = 128
CORES = 2
CHUNK = 512
SLOTS = 3
LANES = 128

norm_eps = 1e-06
grad_weight = 16.0
masked_fill = -1e30

f32 = jnp.float32
bf16 = jnp.bfloat16

NT = (((1,), (1,)), ((), ()))
NN = (((1,), (0,)), ((), ()))
TN = (((0,), (0,)), ((), ()))


def dot(a, b, dims):
    return lax.dot_general(a, b, dims, preferred_element_type=f32)


def smem():
    return pl.BlockSpec(memory_space=pltpu.SMEM)


def vmem():
    return pl.BlockSpec(memory_space=pltpu.VMEM)


def shape(dims, dtype):
    return jax.ShapeDtypeStruct(dims, dtype)


def call(body, outs, ins, scratch=(), limit=48, flops=0, moved=0, exps=0):
    return pl.pallas_call(
        body,
        out_shape=outs,
        in_specs=ins,
        out_specs=jax.tree.map(lambda _: vmem(), outs),
        scratch_shapes=list(scratch),
        compiler_params=pltpu.CompilerParams(vmem_limit_bytes=limit * 2**20),
        cost_estimate=pl.CostEstimate(flops=flops, bytes_accessed=moved, transcendentals=exps),
    )


def shifted(value, axis, step, inner=1, ring=None):
    size = lax.axis_size(axis)
    outer = size // inner
    pairs = [(i, ((i // inner + step) % outer) * inner + i % inner) for i in range(size)]
    return lax.ppermute(value, axis, pairs)


def swapped(value):
    size = lax.axis_size("ctx")
    return lax.ppermute(value, "ctx", [(i, i ^ 1) for i in range(size)])


def pick_body(loss_per, place, rows, hidden, queries, keys, values, picked, packed):
    base = place[3] * loss_per
    tokens, width = hidden.shape
    row_iota = lax.broadcasted_iota(jnp.int32, (loss_per, tokens), 0)
    col_iota = lax.broadcasted_iota(jnp.int32, (loss_per, tokens), 1)
    sel = jnp.zeros((loss_per, tokens), f32)
    for j in range(loss_per):
        sel = jnp.where((row_iota == j) & (col_iota == rows[base + j]), 1.0, sel)
    sel = sel.astype(bf16)
    mine = dot(sel, hidden[...], NN)
    half = width // 2
    picked[...] = jnp.concatenate([mine[:, :half], mine[:, half:]], axis=0).astype(bf16)
    mine = dot(sel, queries[...], NN)
    key_width = keys.shape[1]
    packed[0:tokens, 0:key_width] = keys[...]
    packed[0:tokens, key_width : 2 * key_width] = values[...]
    parts = queries.shape[1] // (2 * key_width)
    stacked = [mine[:, b * 2 * key_width : (b + 1) * 2 * key_width] for b in range(parts)]
    packed[tokens : tokens + parts * loss_per, :] = jnp.concatenate(stacked, axis=0).astype(bf16)


def flash_body(
    first,
    place,
    own,
    other,
    gain,
    targets,
    weight,
    keep,
    send,
    stats,
    unit,
    normed,
    raw,
    acc,
    probs,
    state,
    head_buf,
    buf,
    head_sem,
    sems,
):
    vocab_at, z_at, core_at, ctx_at, first_id = (place[k] for k in range(5))
    nv, nz = own.shape[0], own.shape[1]
    loss, width = normed.shape
    half = own.shape[3]
    total_rows = weight.shape[0]
    chunks = (total_rows - first) // CHUNK
    blocks = acc.shape[0]
    block_width = width // blocks

    def head_copy():
        return pltpu.make_async_copy(weight.at[pl.ds(0, first), :], head_buf, head_sem)

    def body_copy(c):
        slot = lax.rem(c, SLOTS)
        start = pl.multiple_of(first + c * CHUNK, 16)
        return pltpu.make_async_copy(
            weight.at[pl.ds(start, CHUNK), :], buf.at[slot], sems.at[slot]
        )

    head_copy().start()
    for c in range(min(SLOTS, chunks)):
        body_copy(c).start()

    is_even = core_at == 0
    for zr in range(nz):
        z_src = lax.rem(z_at - zr + nz, nz)
        square_own = jnp.zeros((8, 1), f32)
        square_other = jnp.zeros((8, 1), f32)
        for vr in range(nv):
            a = own[vr, zr].astype(f32)
            b = other[vr, zr].astype(f32)
            square_a = jnp.sum(a * a, axis=1, keepdims=True)
            square_b = jnp.sum(b * b, axis=1, keepdims=True)
            square_own += square_a[:8] + square_a[8:]
            square_other += square_b[:8] + square_b[8:]
        square = jnp.concatenate(
            [
                jnp.where(is_even, square_own, square_other),
                jnp.where(is_even, square_other, square_own),
            ],
            axis=0,
        )
        inv = lax.rsqrt(square / width + norm_eps)
        row_at = pl.multiple_of(z_src * 16, 16)
        state[pl.ds(row_at, 16), :] = jnp.broadcast_to(inv, (16, LANES))
        for vr in range(nv):
            v_src = lax.rem(vocab_at - vr + nv, nv)
            a = own[vr, zr].astype(f32)
            b = other[vr, zr].astype(f32)
            low = jnp.where(is_even, a, b)
            high = jnp.where(is_even, b, a)
            for k in range(2):
                x = jnp.concatenate([low[8 * k : 8 * k + 8], high[8 * k : 8 * k + 8]], axis=0)
                lane_at = pl.multiple_of((v_src * 2 + k) * half, half)
                raw[pl.ds(row_at, 16), pl.ds(lane_at, half)] = x.astype(bf16)
                normed[pl.ds(row_at, 16), pl.ds(lane_at, half)] = (
                    x * inv * gain[:, pl.ds(lane_at, half)]
                ).astype(bf16)

    per_vocab = loss // nv
    mine_at = pl.multiple_of(vocab_at * per_vocab, per_vocab)
    feature_at = pl.multiple_of(ctx_at * block_width, block_width)
    unit[...] = (
        raw[pl.ds(mine_at, per_vocab), pl.ds(feature_at, block_width)].astype(f32)
        * state[pl.ds(mine_at, per_vocab), 0:1]
    )

    target_col = targets[...]

    def softmax(scores, base, before):
        cols = scores.shape[1]
        ids = base + lax.broadcasted_iota(jnp.int32, (loss, cols), 1)
        hit = ids == target_col
        top = jnp.max(scores, axis=1, keepdims=True)
        if before is not None:
            top = jnp.maximum(top, before[0])
        shifted_scores = scores - top
        weights = jnp.exp(shifted_scores)
        total = jnp.sum(weights, axis=1, keepdims=True)
        moment = jnp.sum(weights * shifted_scores, axis=1, keepdims=True)
        logit = jnp.sum(jnp.where(hit, scores, 0.0), axis=1, keepdims=True)
        scale = None
        if before is not None:
            gap = before[0] - top
            scale = jnp.exp(gap)
            total = total + before[1] * scale
            moment = moment + scale * (before[2] + gap * before[1])
            logit = logit + before[3]
        masked = jnp.where(hit, 0.0, weights).astype(bf16)
        return masked, scale, (top, total, moment, logit)

    def scores_of(block):
        return dot(normed[...], block, NT)

    def add_product(p, scale, read):
        for b in range(blocks):
            part = dot(p, read(b * block_width, block_width), NN)
            if scale is None:
                acc[b] = part
            else:
                acc[b] = acc[b] * scale + part

    head_copy().wait()
    p, _, run = softmax(scores_of(head_buf[...]), first_id, None)
    add_product(p, None, lambda at, n: head_buf[:, at : at + n])
    if chunks:
        body_copy(0).wait()
        p, scale, run = softmax(scores_of(buf[0]), first_id + first, run)
        probs[...] = p

        def step(c, carry):
            scale, run = carry
            body_copy(c).wait()
            here = lax.rem(c, SLOTS)
            there = lax.rem(c - 1, SLOTS)
            scores = scores_of(buf[here])
            add_product(probs[...], scale, lambda at, n: buf[there, :, at : at + n])

            @pl.when(c + SLOTS - 1 < chunks)
            def _():
                body_copy(c + SLOTS - 1).start()

            p, scale, run = softmax(scores, first_id + first + c * CHUNK, run)
            probs[...] = p
            return scale, run

        scale, run = lax.fori_loop(1, chunks, step, (scale, run))
        last = (chunks - 1) % SLOTS
        add_product(probs[...], scale, lambda at, n: buf[last, :, at : at + n])

    for z in range(nz):
        keep[z] = acc[CORES * z + core_at]
        send[z] = acc[CORES * z + 1 - core_at].astype(bf16)
    lane = lax.broadcasted_iota(jnp.int32, (loss, LANES), 1)
    table = state[...]
    for k in range(4):
        table = jnp.where(lane == k, run[k], table)
    stats[...] = table


def merge_stats(tables):
    columns = [[t[:, k : k + 1] for k in range(4)] for t in tables]
    top = functools.reduce(jnp.maximum, [c[0] for c in columns])
    gaps = [c[0] - top for c in columns]
    scales = [jnp.exp(g) for g in gaps]
    total = sum(s * c[1] for s, c in zip(scales, columns))
    moment = sum(s * (c[2] + g * c[1]) for s, g, c in zip(scales, gaps, columns))
    logit = sum(c[3] for c in columns)
    return scales, (top, total, moment, logit)


def with_stats(table, merged):
    lane = lax.broadcasted_iota(jnp.int32, table.shape, 1)
    for k in range(4):
        table = jnp.where(lane == k, merged[k], table)
    return table


def core_body(count, place, keep, got, mine, theirs, new_stats, new_keep, *sends_and_scratch):
    sends, (total,) = sends_and_scratch[:count], sends_and_scratch[count:]
    scales, merged = merge_stats([mine[...], theirs[...]])
    new_stats[...] = with_stats(mine[...], merged)
    nz, loss, _ = keep.shape
    per = loss // (count + 1)
    for z in range(nz):
        total[z] = keep[z] * scales[0] + got[z].astype(f32) * scales[1]
    new_keep[...] = total[:, pl.ds(pl.multiple_of(place[0] * per, per), per), :]
    for s in range(count):
        to = lax.rem(place[0] + s + 1, count + 1)
        sends[s][...] = total[:, pl.ds(pl.multiple_of(to * per, per), per), :].astype(bf16)


def plane_body(count, nz, place, keep, *refs):
    got, refs = refs[:count], refs[count:]
    tables, refs = refs[: count + 1], refs[count + 1 :]
    new_stats, new_keep = refs[:2]
    sends, (scale_ref, total) = refs[2 : 1 + nz], refs[1 + nz :]
    scales, merged = merge_stats([t[...] for t in tables])
    new_stats[...] = with_stats(tables[0][...], merged)
    per = keep.shape[1]
    at = pl.multiple_of(place[0] * per, per)
    for k in range(count + 1):
        scale_ref[k] = jnp.broadcast_to(scales[k], scale_ref.shape[1:])
    factors = [scale_ref[k, pl.ds(at, per), 0:1] for k in range(count + 1)]
    for z in range(nz):
        value = keep[z] * factors[0]
        for k in range(count):
            value = value + got[k][z].astype(f32) * factors[k + 1]
        total[z] = value
    new_keep[...] = total[place[1]]
    for s in range(nz - 1):
        sends[s][...] = total[lax.rem(place[1] + s + 1, nz)].astype(bf16)


def line_body(nz, width, place, keep, *refs):
    got, refs = refs[: nz - 1], refs[nz - 1 :]
    tables, refs = refs[:nz], refs[nz:]
    target_rows, unit, gain, resid, loss_out, scale_ref, final = refs
    scales, merged = merge_stats([t[...] for t in tables])
    top, total, moment, logit = merged
    log_total = top + jnp.log(total)
    loss_out[...] = jnp.broadcast_to(
        jnp.mean(log_total - logit, axis=0, keepdims=True), loss_out.shape
    )
    per, block_width = keep.shape
    at = pl.multiple_of(place[0] * per, per)
    for k in range(nz):
        scale_ref[k] = jnp.broadcast_to(scales[k] / total, scale_ref.shape[1:])
    value = keep[...] * scale_ref[0, pl.ds(at, per), 0:1]
    for k in range(nz - 1):
        value = value + got[k][...].astype(f32) * scale_ref[k + 1, pl.ds(at, per), 0:1]
    inner_all = grad_weight * (moment / total + (top - logit)) / width
    short_all = jnp.exp(logit - log_total) - 1.0
    lane = lax.broadcasted_iota(jnp.int32, final.shape, 1)
    final[...] = jnp.where(
        lane == 0, inner_all, jnp.where(lane == 1, short_all, tables[0][...])
    )
    inner = final[pl.ds(at, per), 0:1]
    short = final[pl.ds(at, per), 1:2]
    inv = final[pl.ds(at, per), 4:5]
    grad = grad_weight * (value + short * target_rows[...].astype(f32))
    gain_at = pl.multiple_of(place[3] * block_width, block_width)
    scaled = grad * gain[:, pl.ds(gain_at, block_width)]
    resid[...] = (inv * (scaled - unit[...] * inner)).astype(bf16)


def project_body(nv, nc, place, *refs):
    pieces, refs = refs[:nv], refs[nv:]
    weight, resid, keep = refs[:3]
    sends, (whole, partial) = refs[3 : 2 + nc], refs[2 + nc :]
    per = pieces[0].shape[0]
    for s in range(nv):
        src = lax.rem(place[0] - s + nv, nv)
        whole[pl.ds(pl.multiple_of(src * per, per), per), :] = pieces[s][...]
    resid[...] = whole[...]
    partial[...] = dot(whole[...], weight[...], NT)
    rows, cols = keep.shape
    for s in range(nc):
        to = lax.rem(place[3] + s, nc)
        row_at = pl.multiple_of(lax.div(to, CORES) * rows, rows)
        col_at = pl.multiple_of(lax.rem(to, CORES) * cols, cols)
        value = partial[pl.ds(row_at, rows), pl.ds(col_at, cols)]
        if s == 0:
            keep[...] = value
        else:
            sends[s - 1][...] = value.astype(bf16)


def sum_body(keep, *refs):
    value = keep[...]
    for ref in refs[:-1]:
        value = value + ref[...].astype(f32)
    refs[-1][...] = value.astype(bf16)


def forward_body(
    loss_per, heads, group, heads_at_once, place, key_pos, query_pos, packed, p_own, p_rows, out, scratch
):
    nc = packed.shape[0]
    tokens = p_own.shape[2]
    loss = loss_per * nc
    key_width = heads * HEAD_SIZE
    score_scale = HEAD_SIZE ** (-0.5)
    ctx_at = place[3]
    own_at = pl.multiple_of(ctx_at * tokens, tokens)
    row_at = pl.multiple_of(ctx_at * loss_per, loss_per)
    for j in range(heads):
        key = jnp.concatenate(
            [packed[c, 0:tokens, j * HEAD_SIZE : (j + 1) * HEAD_SIZE] for c in range(nc)], axis=0
        )
        at = key_width + j * HEAD_SIZE
        value = jnp.concatenate(
            [packed[c, 0:tokens, at : at + HEAD_SIZE] for c in range(nc)], axis=0
        )
        for g0 in range(0, group, heads_at_once):
            stacked = []
            for g in range(g0, g0 + heads_at_once):
                stacked.append(query_of(packed, j * group + g, tokens, loss_per, key_width))
            query = jnp.concatenate(stacked, axis=0).astype(bf16)
            where_at = jnp.concatenate([query_pos[...]] * heads_at_once, axis=0)
            visible = key_pos[...] <= where_at
            scores = jnp.where(visible, dot(query, key, NT) * score_scale, masked_fill)
            top = jnp.max(scores, axis=1, keepdims=True)
            raw = jnp.where(visible, jnp.exp(scores - top), 0.0)
            prob = raw / jnp.sum(raw, axis=1, keepdims=True)
            scratch[...] = prob
            coarse = prob.astype(bf16)
            fine = (prob - coarse.astype(f32)).astype(bf16)
            first = g0 * loss
            n = heads_at_once * loss
            out[j, first : first + n, :] = dot(coarse, value, NN) + dot(fine, value, NN)
            p_own[j, first : first + n, :] = scratch[:, pl.ds(own_at, tokens)]
            for k in range(heads_at_once):
                p_rows[j, (g0 + k) * loss_per : (g0 + k + 1) * loss_per, :] = scratch[
                    pl.ds(pl.multiple_of(k * loss + row_at, loss_per), loss_per), :
                ]


def query_of(packed, head, tokens, loss_per, key_width):
    lane = head * HEAD_SIZE
    b, at = lane // (2 * key_width), lane % (2 * key_width)
    parts = []
    for c in range(packed.shape[0]):
        block = packed[c, tokens:, at : at + HEAD_SIZE].astype(f32)
        parts.append(block[b * loss_per : (b + 1) * loss_per])
    return jnp.concatenate(parts, axis=0)


def backward_body(loss_per, heads, group, nc, place, *refs):
    pieces, refs = refs[:nc], refs[nc:]
    packed, p_own, p_rows, out, query_grad, key_grad, value_grad, grad = refs
    tokens = p_own.shape[2]
    loss = loss_per * nc
    key_width = heads * HEAD_SIZE
    score_scale = HEAD_SIZE ** (-0.5)
    ctx_at = place[3]
    rows, cols = pieces[0].shape
    for s in range(nc):
        src = lax.rem(ctx_at - s + nc, nc)
        row_at = pl.multiple_of(lax.div(src, CORES) * rows, rows)
        col_at = pl.multiple_of(lax.rem(src, CORES) * cols, cols)
        grad[pl.ds(row_at, rows), pl.ds(col_at, cols)] = pieces[s][...].astype(f32)
    mine_at = pl.multiple_of(ctx_at * loss_per, loss_per)
    for j in range(heads):
        lanes = [slice((j * group + g) * HEAD_SIZE, (j * group + g + 1) * HEAD_SIZE) for g in range(group)]
        d_out = jnp.concatenate([grad[:, s] for s in lanes], axis=0)
        d_half = d_out.astype(bf16)
        delta = jnp.sum(d_out * out[j], axis=1, keepdims=True)
        query = jnp.concatenate(
            [query_of(packed, j * group + g, tokens, loss_per, key_width) for g in range(group)], axis=0
        ).astype(bf16)
        at = key_width + j * HEAD_SIZE
        own_value = packed[ctx_at, 0:tokens, at : at + HEAD_SIZE]
        prob = p_own[j]
        score_grad = (prob * (dot(d_half, own_value, NT) - delta)).astype(bf16)
        k_lanes = slice(j * HEAD_SIZE, (j + 1) * HEAD_SIZE)
        key_grad[:, k_lanes] = (dot(score_grad, query, TN) * score_scale).astype(bf16)
        value_grad[:, k_lanes] = dot(prob.astype(bf16), d_half, TN).astype(bf16)
        key = jnp.concatenate([packed[c, 0:tokens, k_lanes] for c in range(nc)], axis=0)
        value = jnp.concatenate([packed[c, 0:tokens, at : at + HEAD_SIZE] for c in range(nc)], axis=0)
        d_mine = jnp.concatenate([grad[pl.ds(mine_at, loss_per), s] for s in lanes], axis=0)
        out_mine = jnp.concatenate(
            [
                out[j, pl.ds(pl.multiple_of(g * loss + mine_at, loss_per), loss_per), :]
                for g in range(group)
            ],
            axis=0,
        )
        delta = jnp.sum(d_mine * out_mine, axis=1, keepdims=True)
        d_prob = dot(d_mine.astype(bf16), value, NT)
        score_grad = (p_rows[j] * (d_prob - delta)).astype(bf16)
        result = dot(score_grad, key, NN) * score_scale
        for g in range(group):
            query_grad[:, lanes[g]] = result[g * loss_per : (g + 1) * loss_per].astype(bf16)


def per_device(
    hidden,
    norm_gain,
    head_weight,
    targets,
    loss_rows,
    stretch_of_slot,
    queries,
    key_states,
    attention_values,
    output_weight,
):
    nc = lax.axis_size("ctx")
    nv = lax.axis_size("vocab")
    nz = nc // CORES
    ctx_at = lax.axis_index("ctx")
    vocab_at = lax.axis_index("vocab")
    tokens = hidden.shape[0]
    stretch_len = tokens // 2
    loss = loss_rows.shape[0]
    loss_per = loss // nc
    width = norm_gain.shape[0]
    voc_rows = head_weight.shape[0]
    part_width = hidden.shape[1]
    query_width = queries.shape[1]
    key_width = key_states.shape[1]
    heads = key_width // HEAD_SIZE
    group = query_width // key_width
    block_width = width // nc
    per_vocab = loss // nv
    all_tokens = tokens * nc

    first_id = (vocab_at * nc + ctx_at) * voc_rows
    place = jnp.stack([vocab_at, ctx_at // CORES, ctx_at % CORES, ctx_at, first_id]).astype(jnp.int32)

    slots = stretch_of_slot.shape[0]
    owner = lax.broadcasted_iota(jnp.int32, (loss, 1), 0) // loss_per
    slot = 2 * owner + loss_rows[:, None] // stretch_len
    slot_iota = lax.broadcasted_iota(jnp.int32, (1, slots), 1)
    stretch = jnp.sum(jnp.where(slot == slot_iota, stretch_of_slot[None, :], 0), axis=1, keepdims=True)
    query_pos = stretch * stretch_len + loss_rows[:, None] % stretch_len
    key_pos = (
        stretch_of_slot[:, None] * stretch_len
        + lax.broadcasted_iota(jnp.int32, (1, stretch_len), 1)
    ).reshape(1, all_tokens)
    local = targets - first_id
    is_local = (local >= 0) & (local < voc_rows)
    target_rows = head_weight.at[jnp.clip(local, 0, voc_rows - 1)].get(mode="promise_in_bounds")
    target_rows = jnp.where(is_local[:, None], target_rows, jnp.zeros((), bf16))

    extra = (query_width // (2 * key_width)) * loss_per
    picked, packed = call(
        functools.partial(pick_body, loss_per),
        (
            shape((2 * loss_per, part_width // 2), bf16),
            shape((tokens + extra, 2 * key_width), bf16),
        ),
        [smem(), smem()] + [vmem()] * 4,
    )(place, loss_rows, hidden, queries, key_states, attention_values)
    by_z = jnp.stack([picked] + [shifted(picked, "ctx", s, CORES) for s in range(1, nz)])
    by_plane = jnp.stack([by_z] + [shifted(by_z, "vocab", s) for s in range(1, nv)])
    other = swapped(by_plane)

    target_blocks = (
        target_rows.reshape(nv, per_vocab, nc, block_width)
        .transpose(2, 0, 1, 3)
        .reshape(nc * nv * per_vocab, block_width)
    )
    other, packed, target_blocks = lax.optimization_barrier((other, packed, target_blocks))
    packed_all = lax.all_gather(packed, "ctx")
    target_mine = lax.psum_scatter(
        target_blocks, ("ctx", "vocab"), scatter_dimension=0, tiled=True
    )

    first = voc_rows % CHUNK
    if voc_rows < SLOTS * CHUNK or first % 16 or not first:
        first = voc_rows if voc_rows < SLOTS * CHUNK else CHUNK
    chunks = (voc_rows - first) // CHUNK
    gain = norm_gain.reshape(1, width)
    keep, send, stats, unit = pl.pallas_call(
        functools.partial(flash_body, first),
        out_shape=(
            shape((nz, loss, block_width), f32),
            shape((nz, loss, block_width), bf16),
            shape((loss, LANES), f32),
            shape((per_vocab, block_width), f32),
        ),
        in_specs=[smem()] + [vmem()] * 4 + [pl.BlockSpec(memory_space=pl.ANY)],
        out_specs=[vmem()] * 4,
        scratch_shapes=[
            pltpu.VMEM((loss, width), bf16),
            pltpu.VMEM((loss, width), bf16),
            pltpu.VMEM((nc, loss, block_width), f32),
            pltpu.VMEM((loss, CHUNK), bf16),
            pltpu.VMEM((loss, LANES), f32),
            pltpu.VMEM((first, width), bf16),
            pltpu.VMEM((SLOTS if chunks else 1, CHUNK if chunks else 16, width), bf16),
            pltpu.SemaphoreType.DMA,
            pltpu.SemaphoreType.DMA((SLOTS,)),
        ],
        compiler_params=pltpu.CompilerParams(vmem_limit_bytes=50 * 2**20),
        cost_estimate=pl.CostEstimate(
            flops=4 * loss * width * voc_rows,
            bytes_accessed=2 * width * voc_rows,
            transcendentals=loss * voc_rows,
        ),
    )(place, by_plane, other, gain, targets.reshape(loss, 1), head_weight)

    at_once = max(1, min(group, (4 * 2**20) // (loss * all_tokens * 4)))
    p_own, p_rows, out = call(
        functools.partial(forward_body, loss_per, heads, group, at_once),
        (
            shape((heads, group * loss, tokens), f32),
            shape((heads, group * loss_per, all_tokens), f32),
            shape((heads, group * loss, HEAD_SIZE), f32),
        ),
        [smem()] + [vmem()] * 3,
        [pltpu.VMEM((at_once * loss, all_tokens), f32)],
        flops=6 * heads * group * loss * all_tokens * HEAD_SIZE,
        moved=2 * packed_all.size,
        exps=heads * group * loss * all_tokens,
    )(place, key_pos, query_pos, packed_all)

    got, got_stats = swapped(send), swapped(stats)
    stats, keep, *sends = call(
        functools.partial(core_body, nv - 1),
        (
            shape((loss, LANES), f32),
            shape((nz, per_vocab, block_width), f32),
        )
        + (shape((nz, per_vocab, block_width), bf16),) * (nv - 1),
        [smem()] + [vmem()] * 4,
        [pltpu.VMEM((nz, loss, block_width), f32)],
    )(place, keep, got, stats, got_stats)
    got = [shifted(sends[s - 1], "vocab", s) for s in range(1, nv)]
    tables = [stats] + [shifted(stats, "vocab", s) for s in range(1, nv)]
    stats, keep, *sends = call(
        functools.partial(plane_body, nv - 1, nz),
        (shape((loss, LANES), f32), shape((per_vocab, block_width), f32))
        + (shape((per_vocab, block_width), bf16),) * (nz - 1),
        [smem()] + [vmem()] * (1 + (nv - 1) + nv),
        [
            pltpu.VMEM((nv, loss, LANES), f32),
            pltpu.VMEM((nz, per_vocab, block_width), f32),
        ],
    )(place, keep, *got, *tables)
    got = [shifted(sends[s - 1], "ctx", s, CORES) for s in range(1, nz)]
    tables = [stats] + [shifted(stats, "ctx", s, CORES) for s in range(1, nz)]
    resid, mean_loss = call(
        functools.partial(line_body, nz, width),
        (shape((per_vocab, block_width), bf16), shape((8, LANES), f32)),
        [smem()] + [vmem()] * (1 + (nz - 1) + nz + 3),
        [pltpu.VMEM((nz, loss, LANES), f32), pltpu.VMEM((loss, LANES), f32)],
    )(place, keep, *got, *tables, target_mine, unit, gain)

    pieces = [resid] + [shifted(resid, "vocab", s) for s in range(1, nv)]
    rows, cols = loss // nz, query_width // CORES
    resid_rows, keep, *sends = call(
        functools.partial(project_body, nv, nc),
        (shape((loss, block_width), bf16), shape((rows, cols), f32))
        + (shape((rows, cols), bf16),) * (nc - 1),
        [smem()] + [vmem()] * (nv + 1),
        [pltpu.VMEM((loss, block_width), bf16), pltpu.VMEM((loss, query_width), f32)],
    )(place, *pieces, output_weight)
    got = [shifted(sends[s - 1], "ctx", s) for s in range(1, nc)]
    piece = call(sum_body, shape((rows, cols), bf16), [vmem()] * nc)(keep, *got)
    pieces = [piece] + [shifted(piece, "ctx", s) for s in range(1, nc)]
    query_grad, key_grad, value_grad = call(
        functools.partial(backward_body, loss_per, heads, group, nc),
        (
            shape((loss_per, query_width), bf16),
            shape((tokens, key_width), bf16),
            shape((tokens, key_width), bf16),
        ),
        [smem()] + [vmem()] * (nc + 4),
        [pltpu.VMEM((loss, query_width), f32)],
    )(place, *pieces, packed_all, p_own, p_rows, out)
    return (mean_loss[0, 0], query_grad, key_grad, value_grad, resid_rows.T)


def solution(mesh):
    placed = (
        P("ctx", "vocab"),
        P(),
        P(("vocab", "ctx"), None),
        P(),
        P(),
        P(),
        P("ctx", "vocab"),
        P("ctx", "vocab"),
        P("ctx", "vocab"),
        P("vocab", "ctx"),
    )
    return jax.shard_map(
        per_device,
        mesh=mesh,
        in_specs=placed,
        out_specs=(P(), P("ctx", "vocab"), P("ctx", "vocab"), P("ctx", "vocab"), P("ctx", None)),
        check_vma=False,
    )
```

```python
import functools

import jax
import jax.numpy as jnp
from jax import lax
from jax.experimental import pallas as pl
from jax.experimental.pallas import tpu as pltpu
from jax.sharding import PartitionSpec as P

HEAD_SIZE = 128
CORES = 2
CHUNK = 512
SLOTS = 3
LANES = 128

norm_eps = 1e-06
grad_weight = 16.0
masked_fill = -1e30

f32 = jnp.float32
bf16 = jnp.bfloat16

NT = (((1,), (1,)), ((), ()))
NN = (((1,), (0,)), ((), ()))
TN = (((0,), (0,)), ((), ()))


def dot(a, b, dims):
    return lax.dot_general(a, b, dims, preferred_element_type=f32)


def smem():
    return pl.BlockSpec(memory_space=pltpu.SMEM)


def vmem():
    return pl.BlockSpec(memory_space=pltpu.VMEM)


def shape(dims, dtype):
    return jax.ShapeDtypeStruct(dims, dtype)


def call(body, outs, ins, scratch=(), limit=48, flops=0, moved=0, exps=0):
    return pl.pallas_call(
        body,
        out_shape=outs,
        in_specs=ins,
        out_specs=jax.tree.map(lambda _: vmem(), outs),
        scratch_shapes=list(scratch),
        compiler_params=pltpu.CompilerParams(vmem_limit_bytes=limit * 2**20),
        cost_estimate=pl.CostEstimate(flops=flops, bytes_accessed=moved, transcendentals=exps),
    )


def shifted(value, axis, step, inner=1):
    size = lax.axis_size(axis)
    outer = size // inner
    pairs = [(i, ((i // inner + step) % outer) * inner + i % inner) for i in range(size)]
    return lax.ppermute(value, axis, pairs)


def swapped(value):
    size = lax.axis_size("ctx")
    return lax.ppermute(value, "ctx", [(i, i ^ 1) for i in range(size)])


def row_choice(loss_per, tokens, place, rows):
    base = place[3] * loss_per
    row_iota = lax.broadcasted_iota(jnp.int32, (loss_per, tokens), 0)
    col_iota = lax.broadcasted_iota(jnp.int32, (loss_per, tokens), 1)
    sel = jnp.zeros((loss_per, tokens), f32)
    for j in range(loss_per):
        sel = jnp.where((row_iota == j) & (col_iota == rows[base + j]), 1.0, sel)
    return sel.astype(bf16)


def pick_body(loss_per, place, rows, hidden, picked):
    tokens, width = hidden.shape
    mine = dot(row_choice(loss_per, tokens, place, rows), hidden[...], NN)
    half = width // 2
    picked[...] = jnp.concatenate([mine[:, :half], mine[:, half:]], axis=0).astype(bf16)


def pack_body(loss_per, place, rows, queries, keys, values, packed):
    tokens, key_width = keys.shape
    mine = dot(row_choice(loss_per, tokens, place, rows), queries[...], NN)
    packed[0:tokens, 0:key_width] = keys[...]
    packed[0:tokens, key_width : 2 * key_width] = values[...]
    parts = queries.shape[1] // (2 * key_width)
    stacked = [mine[:, b * 2 * key_width : (b + 1) * 2 * key_width] for b in range(parts)]
    packed[tokens : tokens + parts * loss_per, :] = jnp.concatenate(stacked, axis=0).astype(bf16)


def target_body(place, targets, weight, out, buf, rows, sems):
    loss, width = rows.shape
    blocks, _, block_width = out.shape
    total_rows = weight.shape[0]

    def local(i):
        at = targets[i] - place[4]
        return at, (at >= 0) & (at < total_rows)

    def copy(i, at):
        start = pl.multiple_of(lax.div(at, 16) * 16, 16)
        return pltpu.make_async_copy(weight.at[pl.ds(start, 16), :], buf.at[i], sems.at[i])

    @pl.loop(0, loss)
    def _(i):
        at, here = local(i)

        @pl.when(here)
        def _():
            copy(i, at).start()

    rows[...] = jnp.zeros_like(rows)

    @pl.loop(0, loss)
    def _(i):
        at, here = local(i)

        @pl.when(here)
        def _():
            copy(i, at).wait()
            line = lax.broadcasted_iota(jnp.int32, (16, width), 0)
            block = buf[i].astype(f32)
            row = jnp.sum(jnp.where(line == lax.rem(at, 16), block, 0.0), axis=0, keepdims=True)
            rows[pl.ds(i, 1), :] = row

    for b in range(blocks):
        out[b] = rows[:, b * block_width : (b + 1) * block_width].astype(bf16)


def flash_body(
    first,
    place,
    own,
    other,
    gain,
    targets,
    weight,
    keep,
    send,
    stats,
    unit,
    normed,
    raw,
    acc,
    probs,
    state,
    head_buf,
    buf,
    head_sem,
    sems,
):
    vocab_at, z_at, core_at, ctx_at, first_id = (place[k] for k in range(5))
    nv, nz = own.shape[0], own.shape[1]
    loss, width = normed.shape
    half = own.shape[3]
    total_rows = weight.shape[0]
    chunks = (total_rows - first) // CHUNK
    blocks = acc.shape[0]
    block_width = width // blocks

    def head_copy():
        return pltpu.make_async_copy(weight.at[pl.ds(0, first), :], head_buf, head_sem)

    def body_copy(c):
        slot = lax.rem(c, SLOTS)
        start = pl.multiple_of(first + c * CHUNK, 16)
        return pltpu.make_async_copy(
            weight.at[pl.ds(start, CHUNK), :], buf.at[slot], sems.at[slot]
        )

    head_copy().start()
    for c in range(min(SLOTS, chunks)):
        body_copy(c).start()

    is_even = core_at == 0
    for zr in range(nz):
        z_src = lax.rem(z_at - zr + nz, nz)
        square_own = jnp.zeros((8, 1), f32)
        square_other = jnp.zeros((8, 1), f32)
        for vr in range(nv):
            a = own[vr, zr].astype(f32)
            b = other[vr, zr].astype(f32)
            square_a = jnp.sum(a * a, axis=1, keepdims=True)
            square_b = jnp.sum(b * b, axis=1, keepdims=True)
            square_own += square_a[:8] + square_a[8:]
            square_other += square_b[:8] + square_b[8:]
        square = jnp.concatenate(
            [
                jnp.where(is_even, square_own, square_other),
                jnp.where(is_even, square_other, square_own),
            ],
            axis=0,
        )
        inv = lax.rsqrt(square / width + norm_eps)
        row_at = pl.multiple_of(z_src * 16, 16)
        state[pl.ds(row_at, 16), :] = jnp.broadcast_to(inv, (16, LANES))
        for vr in range(nv):
            v_src = vr
            a = own[vr, zr].astype(f32)
            b = other[vr, zr].astype(f32)
            low = jnp.where(is_even, a, b)
            high = jnp.where(is_even, b, a)
            for k in range(2):
                x = jnp.concatenate([low[8 * k : 8 * k + 8], high[8 * k : 8 * k + 8]], axis=0)
                lane_at = pl.multiple_of((v_src * 2 + k) * half, half)
                raw[pl.ds(row_at, 16), pl.ds(lane_at, half)] = x.astype(bf16)
                normed[pl.ds(row_at, 16), pl.ds(lane_at, half)] = (
                    x * inv * gain[:, pl.ds(lane_at, half)]
                ).astype(bf16)

    per_vocab = loss // nv
    mine_at = pl.multiple_of(vocab_at * per_vocab, per_vocab)
    feature_at = pl.multiple_of(ctx_at * block_width, block_width)
    unit[...] = (
        raw[pl.ds(mine_at, per_vocab), pl.ds(feature_at, block_width)].astype(f32)
        * state[pl.ds(mine_at, per_vocab), 0:1]
    )

    target_col = targets[...]

    def softmax(scores, base, before):
        cols = scores.shape[1]
        ids = base + lax.broadcasted_iota(jnp.int32, (loss, cols), 1)
        hit = ids == target_col
        top = jnp.max(scores, axis=1, keepdims=True)
        if before is not None:
            top = jnp.maximum(top, before[0])
        shifted_scores = scores - top
        weights = jnp.exp(shifted_scores)
        total = jnp.sum(weights, axis=1, keepdims=True)
        moment = jnp.sum(weights * shifted_scores, axis=1, keepdims=True)
        logit = jnp.sum(jnp.where(hit, scores, 0.0), axis=1, keepdims=True)
        scale = None
        if before is not None:
            gap = before[0] - top
            scale = jnp.exp(gap)
            total = total + before[1] * scale
            moment = moment + scale * (before[2] + gap * before[1])
            logit = logit + before[3]
        masked = jnp.where(hit, 0.0, weights).astype(bf16)
        return masked, scale, (top, total, moment, logit)

    def scores_of(block):
        return dot(block, normed[...], NT).T

    def add_product(p, scale, read):
        for b in range(blocks):
            part = dot(p, read(b * block_width, block_width), NN)
            if scale is None:
                acc[b] = part
            else:
                acc[b] = acc[b] * scale + part

    head_copy().wait()
    p, _, run = softmax(scores_of(head_buf[...]), first_id, None)
    add_product(p, None, lambda at, n: head_buf[:, at : at + n])
    if chunks:
        body_copy(0).wait()
        p, scale, run = softmax(scores_of(buf[0]), first_id + first, run)
        probs[...] = p

        def step(c, carry):
            scale, run = carry
            body_copy(c).wait()
            here = lax.rem(c, SLOTS)
            there = lax.rem(c - 1, SLOTS)
            scores = scores_of(buf[here])
            add_product(probs[...], scale, lambda at, n: buf[there, :, at : at + n])

            @pl.when(c + SLOTS - 1 < chunks)
            def _():
                body_copy(c + SLOTS - 1).start()

            p, scale, run = softmax(scores, first_id + first + c * CHUNK, run)
            probs[...] = p
            return scale, run

        scale, run = lax.fori_loop(1, chunks, step, (scale, run))
        last = (chunks - 1) % SLOTS
        add_product(probs[...], scale, lambda at, n: buf[last, :, at : at + n])

    for z in range(nz):
        keep[z] = acc[CORES * z + core_at]
        send[:, z * block_width : (z + 1) * block_width] = acc[CORES * z + 1 - core_at].astype(bf16)
    send[:, nz * block_width :] = split_columns(run)
    stats[...] = with_stats(state[...], run)


def split_columns(columns):
    rows = columns[0].shape[0]
    lane = lax.broadcasted_iota(jnp.int32, (rows, LANES), 1)
    table = jnp.zeros((rows, LANES), f32)
    for k, column in enumerate(columns):
        rest = column
        for j in range(3):
            term = rest.astype(bf16).astype(f32)
            table = jnp.where(lane == 3 * k + j, term, table)
            rest = rest - term
    return table.astype(bf16)


def joined_columns(block, count):
    block = block.astype(f32)
    return [
        block[:, 3 * k : 3 * k + 1] + block[:, 3 * k + 1 : 3 * k + 2] + block[:, 3 * k + 2 : 3 * k + 3]
        for k in range(count)
    ]


def stats_of(table):
    return [table[:, k : k + 1] for k in range(4)]


def merge_stats(columns):
    top = functools.reduce(jnp.maximum, [c[0] for c in columns])
    gaps = [c[0] - top for c in columns]
    scales = [jnp.exp(g) for g in gaps]
    total = sum(s * c[1] for s, c in zip(scales, columns))
    moment = sum(s * (c[2] + g * c[1]) for s, g, c in zip(scales, gaps, columns))
    logit = sum(c[3] for c in columns)
    return scales, (top, total, moment, logit)


def with_stats(table, merged):
    lane = lax.broadcasted_iota(jnp.int32, table.shape, 1)
    for k in range(4):
        table = jnp.where(lane == k, merged[k], table)
    return table


def core_body(count, place, keep, got, mine, target_rows, new_stats, new_keep, *rest):
    sends, (total, table, message) = rest[:count], rest[count:]
    nz, loss, block = keep.shape
    columns = [stats_of(mine[...]), joined_columns(got[:, nz * block :], 4)]
    scales, merged = merge_stats(columns)
    table[...] = with_stats(mine[...], merged)
    message[...] = split_columns(merged)
    per = loss // (count + 1)
    for z in range(nz):
        other = got[:, z * block : (z + 1) * block].astype(f32)
        total[z] = keep[z] * scales[0] + other * scales[1]
    at = pl.multiple_of(place[0] * per, per)
    new_stats[...] = table[pl.ds(at, per), :]
    new_keep[...] = total[:, pl.ds(at, per), :]
    for s in range(count):
        to = lax.rem(place[0] + s + 1, count + 1)
        rows = pl.ds(pl.multiple_of(to * per, per), per)
        for z in range(nz):
            sends[s][:, z * block : (z + 1) * block] = total[z, rows, :].astype(bf16)
        sends[s][:, nz * block : (nz + 1) * block] = target_rows[rows, :]
        sends[s][:, (nz + 1) * block :] = message[rows, :]


def plane_body(count, place, keep, mine, target_rows, *rest):
    got, rest = rest[:count], rest[count:]
    new_stats, new_keep, new_target = rest[:3]
    sends, (total,) = rest[3:-1], rest[-1:]
    nz, per, block = keep.shape
    columns = [stats_of(mine[...])] + [joined_columns(g[:, (nz + 1) * block :], 4) for g in got]
    scales, merged = merge_stats(columns)
    new_stats[...] = with_stats(mine[...], merged)
    message = split_columns(merged)
    for z in range(nz):
        value = keep[z] * scales[0]
        for k in range(count):
            value = value + got[k][:, z * block : (z + 1) * block].astype(f32) * scales[k + 1]
        total[z] = value
    new_keep[...] = total[place[1]]
    rows = target_rows[pl.ds(pl.multiple_of(place[0] * per, per), per), :].astype(f32)
    for k in range(count):
        rows = rows + got[k][:, nz * block : (nz + 1) * block].astype(f32)
    new_target[...] = rows.astype(bf16)
    for s in range(nz - 1):
        sends[s][:, :block] = total[lax.rem(place[1] + s + 1, nz)].astype(bf16)
        sends[s][:, block:] = message


def line_body(count, width, place, keep, mine, target_rows, unit, gain, *rest):
    got, (message,) = rest[:count], rest[count:]
    per, block = keep.shape
    columns = [stats_of(mine[...])] + [joined_columns(g[:, block:], 4) for g in got]
    scales, (top, total, moment, logit) = merge_stats(columns)
    log_total = top + jnp.log(total)
    value = keep[...] * (scales[0] / total)
    for k in range(count):
        value = value + got[k][:, :block].astype(f32) * (scales[k + 1] / total)
    inner = grad_weight * (moment / total + (top - logit)) / width
    short = jnp.exp(logit - log_total) - 1.0
    inv = mine[:, 4:5]
    grad = grad_weight * (value + short * target_rows[...].astype(f32))
    gain_at = pl.multiple_of(place[3] * block, block)
    scaled = grad * gain[:, pl.ds(gain_at, block)]
    message[:, :block] = (inv * (scaled - unit[...] * inner)).astype(bf16)
    message[:, block:] = split_columns([log_total - logit])


def project_body(place, gathered, weight, resid, loss_out, keep, send, whole, partial):
    nv, per, _ = gathered.shape
    block = whole.shape[1]
    loss_sum = jnp.zeros((1, 1), f32)
    for v in range(nv):
        whole[v * per : (v + 1) * per, :] = gathered[v, :, :block]
        (column,) = joined_columns(gathered[v, :, block:], 1)
        loss_sum = loss_sum + jnp.sum(column, axis=0, keepdims=True)
    loss_out[...] = jnp.broadcast_to(loss_sum / (nv * per), loss_out.shape)
    resid[...] = whole[...]
    partial[...] = dot(whole[...], weight[...], NT)
    cols = keep.shape[1]
    keep[...] = partial[:, pl.ds(pl.multiple_of(place[2] * cols, cols), cols)]
    send[...] = partial[:, pl.ds(pl.multiple_of((1 - place[2]) * cols, cols), cols)].astype(bf16)


def half_body(keep, got, out):
    value = (keep[...] + got[...].astype(f32)).astype(bf16)
    per = out.shape[1]
    for z in range(out.shape[0]):
        out[z] = value[z * per : (z + 1) * per]


def sum_body(parts, out):
    value = parts[0].astype(f32)
    for z in range(1, parts.shape[0]):
        value = value + parts[z].astype(f32)
    out[...] = value.astype(bf16)


def forward_body(
    loss_per, heads, group, heads_at_once, place, key_pos, query_pos, packed, p_own, p_rows, out, scratch
):
    nc = packed.shape[0]
    tokens = p_own.shape[2]
    loss = loss_per * nc
    key_width = heads * HEAD_SIZE
    score_scale = HEAD_SIZE ** (-0.5)
    ctx_at = place[3]
    own_at = pl.multiple_of(ctx_at * tokens, tokens)
    row_at = pl.multiple_of(ctx_at * loss_per, loss_per)
    for j in range(heads):
        key = jnp.concatenate(
            [packed[c, 0:tokens, j * HEAD_SIZE : (j + 1) * HEAD_SIZE] for c in range(nc)], axis=0
        )
        at = key_width + j * HEAD_SIZE
        value = jnp.concatenate(
            [packed[c, 0:tokens, at : at + HEAD_SIZE] for c in range(nc)], axis=0
        )
        for g0 in range(0, group, heads_at_once):
            stacked = []
            for g in range(g0, g0 + heads_at_once):
                stacked.append(query_of(packed, j * group + g, tokens, loss_per, key_width))
            query = jnp.concatenate(stacked, axis=0).astype(bf16)
            where_at = jnp.concatenate([query_pos[...]] * heads_at_once, axis=0)
            visible = key_pos[...] <= where_at
            scores = jnp.where(visible, dot(query, key, NT) * score_scale, masked_fill)
            top = jnp.max(scores, axis=1, keepdims=True)
            raw = jnp.where(visible, jnp.exp(scores - top), 0.0)
            prob = raw / jnp.sum(raw, axis=1, keepdims=True)
            scratch[...] = prob
            coarse = prob.astype(bf16)
            fine = (prob - coarse.astype(f32)).astype(bf16)
            first = g0 * loss
            n = heads_at_once * loss
            out[j, first : first + n, :] = dot(coarse, value, NN) + dot(fine, value, NN)
            p_own[j, first : first + n, :] = scratch[:, pl.ds(own_at, tokens)]
            for k in range(heads_at_once):
                p_rows[j, (g0 + k) * loss_per : (g0 + k + 1) * loss_per, :] = scratch[
                    pl.ds(pl.multiple_of(k * loss + row_at, loss_per), loss_per), :
                ]


def query_of(packed, head, tokens, loss_per, key_width):
    lane = head * HEAD_SIZE
    b, at = lane // (2 * key_width), lane % (2 * key_width)
    parts = []
    for c in range(packed.shape[0]):
        block = packed[c, tokens:, at : at + HEAD_SIZE].astype(f32)
        parts.append(block[b * loss_per : (b + 1) * loss_per])
    return jnp.concatenate(parts, axis=0)


def backward_body(
    loss_per, heads, group, place, half, other, packed, p_own, p_rows, out, query_grad, key_grad, value_grad, grad
):
    nc = packed.shape[0]
    tokens = p_own.shape[2]
    loss = loss_per * nc
    key_width = heads * HEAD_SIZE
    score_scale = HEAD_SIZE ** (-0.5)
    ctx_at = place[3]
    nz, rows, cols = half.shape
    col_at = pl.multiple_of(place[2] * cols, cols)
    other_at = pl.multiple_of((1 - place[2]) * cols, cols)
    for s in range(nz):
        row_at = pl.multiple_of(lax.rem(place[1] - s + nz, nz) * rows, rows)
        grad[pl.ds(row_at, rows), pl.ds(col_at, cols)] = half[s].astype(f32)
        grad[pl.ds(row_at, rows), pl.ds(other_at, cols)] = other[s].astype(f32)
    mine_at = pl.multiple_of(ctx_at * loss_per, loss_per)
    for j in range(heads):
        lanes = [slice((j * group + g) * HEAD_SIZE, (j * group + g + 1) * HEAD_SIZE) for g in range(group)]
        d_out = jnp.concatenate([grad[:, s] for s in lanes], axis=0)
        d_half = d_out.astype(bf16)
        delta = jnp.sum(d_out * out[j], axis=1, keepdims=True)
        query = jnp.concatenate(
            [query_of(packed, j * group + g, tokens, loss_per, key_width) for g in range(group)], axis=0
        ).astype(bf16)
        at = key_width + j * HEAD_SIZE
        own_value = packed[ctx_at, 0:tokens, at : at + HEAD_SIZE]
        prob = p_own[j]
        score_grad = (prob * (dot(d_half, own_value, NT) - delta)).astype(bf16)
        k_lanes = slice(j * HEAD_SIZE, (j + 1) * HEAD_SIZE)
        key_grad[:, k_lanes] = (dot(score_grad, query, TN) * score_scale).astype(bf16)
        value_grad[:, k_lanes] = dot(prob.astype(bf16), d_half, TN).astype(bf16)
        key = jnp.concatenate([packed[c, 0:tokens, k_lanes] for c in range(nc)], axis=0)
        value = jnp.concatenate([packed[c, 0:tokens, at : at + HEAD_SIZE] for c in range(nc)], axis=0)
        d_mine = jnp.concatenate([grad[pl.ds(mine_at, loss_per), s] for s in lanes], axis=0)
        out_mine = jnp.concatenate(
            [
                out[j, pl.ds(pl.multiple_of(g * loss + mine_at, loss_per), loss_per), :]
                for g in range(group)
            ],
            axis=0,
        )
        delta = jnp.sum(d_mine * out_mine, axis=1, keepdims=True)
        d_prob = dot(d_mine.astype(bf16), value, NT)
        score_grad = (p_rows[j] * (d_prob - delta)).astype(bf16)
        result = dot(score_grad, key, NN) * score_scale
        for g in range(group):
            query_grad[:, lanes[g]] = result[g * loss_per : (g + 1) * loss_per].astype(bf16)


def per_device(
    hidden,
    norm_gain,
    head_weight,
    targets,
    loss_rows,
    stretch_of_slot,
    queries,
    key_states,
    attention_values,
    output_weight,
):
    nc = lax.axis_size("ctx")
    nv = lax.axis_size("vocab")
    nz = nc // CORES
    ctx_at = lax.axis_index("ctx")
    vocab_at = lax.axis_index("vocab")
    tokens = hidden.shape[0]
    stretch_len = tokens // 2
    loss = loss_rows.shape[0]
    loss_per = loss // nc
    width = norm_gain.shape[0]
    voc_rows = head_weight.shape[0]
    part_width = hidden.shape[1]
    query_width = queries.shape[1]
    key_width = key_states.shape[1]
    heads = key_width // HEAD_SIZE
    group = query_width // key_width
    block_width = width // nc
    per_vocab = loss // nv
    all_tokens = tokens * nc

    first_id = (vocab_at * nc + ctx_at) * voc_rows
    place = jnp.stack([vocab_at, ctx_at // CORES, ctx_at % CORES, ctx_at, first_id]).astype(jnp.int32)

    slots = stretch_of_slot.shape[0]
    owner = lax.broadcasted_iota(jnp.int32, (loss, 1), 0) // loss_per
    slot = 2 * owner + loss_rows[:, None] // stretch_len
    slot_iota = lax.broadcasted_iota(jnp.int32, (1, slots), 1)
    stretch = jnp.sum(jnp.where(slot == slot_iota, stretch_of_slot[None, :], 0), axis=1, keepdims=True)
    query_pos = stretch * stretch_len + loss_rows[:, None] % stretch_len
    key_pos = (
        stretch_of_slot[:, None] * stretch_len
        + lax.broadcasted_iota(jnp.int32, (1, stretch_len), 1)
    ).reshape(1, all_tokens)
    if voc_rows % 16:
        local = targets - first_id
        is_local = (local >= 0) & (local < voc_rows)
        target_rows = head_weight.at[jnp.clip(local, 0, voc_rows - 1)].get(mode="promise_in_bounds")
        target_rows = jnp.where(is_local[:, None], target_rows, jnp.zeros((), bf16))
        target_rows = target_rows.reshape(loss, nc, block_width).transpose(1, 0, 2)
    else:
        target_rows = pl.pallas_call(
            target_body,
            out_shape=shape((nc, loss, block_width), bf16),
            in_specs=[smem(), smem(), pl.BlockSpec(memory_space=pl.ANY)],
            out_specs=vmem(),
            scratch_shapes=[
                pltpu.VMEM((loss, 16, width), bf16),
                pltpu.VMEM((loss, width), f32),
                pltpu.SemaphoreType.DMA((loss,)),
            ],
            compiler_params=pltpu.CompilerParams(vmem_limit_bytes=40 * 2**20),
        )(place, targets, head_weight)
    target_rows = lax.psum_scatter(
        target_rows.reshape(nc * loss, block_width), "ctx", scatter_dimension=0, tiled=True
    )

    picked = call(
        functools.partial(pick_body, loss_per),
        shape((2 * loss_per, part_width // 2), bf16),
        [smem(), smem(), vmem()],
    )(place, loss_rows, hidden)
    picked, queries = lax.optimization_barrier((picked, queries))
    extra = (query_width // (2 * key_width)) * loss_per
    packed = call(
        functools.partial(pack_body, loss_per),
        shape((tokens + extra, 2 * key_width), bf16),
        [smem(), smem()] + [vmem()] * 3,
    )(place, loss_rows, queries, key_states, attention_values)
    by_z = jnp.stack([picked] + [shifted(picked, "ctx", s, CORES) for s in range(1, nz)])
    by_plane = lax.all_gather(by_z, "vocab")
    other = swapped(by_plane)
    other, packed = lax.optimization_barrier((other, packed))
    packed_all = lax.all_gather(packed, "ctx")

    first = voc_rows % CHUNK
    if voc_rows < SLOTS * CHUNK or first % 16 or not first:
        first = voc_rows if voc_rows < SLOTS * CHUNK else CHUNK
    chunks = (voc_rows - first) // CHUNK
    gain = norm_gain.reshape(1, width)
    keep, send, stats, unit = pl.pallas_call(
        functools.partial(flash_body, first),
        out_shape=(
            shape((nz, loss, block_width), f32),
            shape((loss, nz * block_width + LANES), bf16),
            shape((loss, LANES), f32),
            shape((per_vocab, block_width), f32),
        ),
        in_specs=[smem()] + [vmem()] * 4 + [pl.BlockSpec(memory_space=pl.ANY)],
        out_specs=[vmem()] * 4,
        scratch_shapes=[
            pltpu.VMEM((loss, width), bf16),
            pltpu.VMEM((loss, width), bf16),
            pltpu.VMEM((nc, loss, block_width), f32),
            pltpu.VMEM((loss, CHUNK), bf16),
            pltpu.VMEM((loss, LANES), f32),
            pltpu.VMEM((first, width), bf16),
            pltpu.VMEM((SLOTS if chunks else 1, CHUNK if chunks else 16, width), bf16),
            pltpu.SemaphoreType.DMA,
            pltpu.SemaphoreType.DMA((SLOTS,)),
        ],
        compiler_params=pltpu.CompilerParams(vmem_limit_bytes=50 * 2**20),
        cost_estimate=pl.CostEstimate(
            flops=4 * loss * width * voc_rows,
            bytes_accessed=2 * width * voc_rows,
            transcendentals=loss * voc_rows,
        ),
    )(place, by_plane, other, gain, targets.reshape(loss, 1), head_weight)

    at_once = max(1, min(group, (4 * 2**20) // (loss * all_tokens * 4)))
    p_own, p_rows, out = call(
        functools.partial(forward_body, loss_per, heads, group, at_once),
        (
            shape((heads, group * loss, tokens), f32),
            shape((heads, group * loss_per, all_tokens), f32),
            shape((heads, group * loss, HEAD_SIZE), f32),
        ),
        [smem()] + [vmem()] * 3,
        [pltpu.VMEM((at_once * loss, all_tokens), f32)],
        flops=6 * heads * group * loss * all_tokens * HEAD_SIZE,
        moved=2 * packed_all.size,
        exps=heads * group * loss * all_tokens,
    )(place, key_pos, query_pos, packed_all)

    got = swapped(send)
    stats, keep, *sends = call(
        functools.partial(core_body, nv - 1),
        (
            shape((per_vocab, LANES), f32),
            shape((nz, per_vocab, block_width), f32),
        )
        + (shape((per_vocab, (nz + 1) * block_width + LANES), bf16),) * (nv - 1),
        [smem()] + [vmem()] * 4,
        [
            pltpu.VMEM((nz, loss, block_width), f32),
            pltpu.VMEM((loss, LANES), f32),
            pltpu.VMEM((loss, LANES), bf16),
        ],
    )(place, keep, got, stats, target_rows)
    got = [shifted(sends[s - 1], "vocab", s) for s in range(1, nv)]

    stats, packed_all = lax.optimization_barrier((stats, packed_all))
    at_once = max(1, min(group, (4 * 2**20) // (loss * all_tokens * 4)))
    p_own, p_rows, out = call(
        functools.partial(forward_body, loss_per, heads, group, at_once),
        (
            shape((heads, group * loss, tokens), f32),
            shape((heads, group * loss_per, all_tokens), f32),
            shape((heads, group * loss, HEAD_SIZE), f32),
        ),
        [smem()] + [vmem()] * 3,
        [pltpu.VMEM((at_once * loss, all_tokens), f32)],
        flops=6 * heads * group * loss * all_tokens * HEAD_SIZE,
        moved=2 * packed_all.size,
        exps=heads * group * loss * all_tokens,
    )(place, key_pos, query_pos, packed_all)
    stats, p_own, p_rows, out = lax.optimization_barrier((stats, p_own, p_rows, out))

    stats, keep, target_rows, *sends = call(
        functools.partial(plane_body, nv - 1),
        (
            shape((per_vocab, LANES), f32),
            shape((per_vocab, block_width), f32),
            shape((per_vocab, block_width), bf16),
        )
        + (shape((per_vocab, block_width + LANES), bf16),) * (nz - 1),
        [smem()] + [vmem()] * (3 + nv - 1),
        [pltpu.VMEM((nz, per_vocab, block_width), f32)],
    )(place, keep, stats, target_rows, *got)
    got = [shifted(sends[s - 1], "ctx", s, CORES) for s in range(1, nz)]
    message = call(
        functools.partial(line_body, nz - 1, width),
        shape((per_vocab, block_width + LANES), bf16),
        [smem()] + [vmem()] * (5 + nz - 1),
    )(place, keep, stats, target_rows, unit, gain, *got)

    gathered = lax.all_gather(message, "vocab")
    cols = query_width // CORES
    rows = loss // nz
    resid_rows, mean_loss, keep, send = call(
        project_body,
        (
            shape((loss, block_width), bf16),
            shape((8, LANES), f32),
            shape((loss, cols), f32),
            shape((loss, cols), bf16),
        ),
        [smem()] + [vmem()] * 2,
        [pltpu.VMEM((loss, block_width), bf16), pltpu.VMEM((loss, query_width), f32)],
    )(place, gathered, output_weight)
    parts = call(half_body, shape((nz, rows, cols), bf16), [vmem()] * 2)(keep, swapped(send))
    lines = [[CORES * z + c for z in range(nz)] for c in range(CORES)]
    parts = lax.all_to_all(parts, "ctx", 0, 0, axis_index_groups=lines)
    piece = call(sum_body, shape((rows, cols), bf16), [vmem()])(parts)
    half = jnp.stack([piece] + [shifted(piece, "ctx", s, CORES) for s in range(1, nz)])
    other = swapped(half)
    query_grad, key_grad, value_grad = call(
        functools.partial(backward_body, loss_per, heads, group),
        (
            shape((loss_per, query_width), bf16),
            shape((tokens, key_width), bf16),
            shape((tokens, key_width), bf16),
        ),
        [smem()] + [vmem()] * 6,
        [pltpu.VMEM((loss, query_width), f32)],
    )(place, half, other, packed_all, p_own, p_rows, out)
    return (mean_loss[0, 0], query_grad, key_grad, value_grad, resid_rows.T)


def solution(mesh):
    placed = (
        P("ctx", "vocab"),
        P(),
        P(("vocab", "ctx"), None),
        P(),
        P(),
        P(),
        P("ctx", "vocab"),
        P("ctx", "vocab"),
        P("ctx", "vocab"),
        P("vocab", "ctx"),
    )
    return jax.shard_map(
        per_device,
        mesh=mesh,
        in_specs=placed,
        out_specs=(P(), P("ctx", "vocab"), P("ctx", "vocab"), P("ctx", "vocab"), P("ctx", None)),
        check_vma=False,
    )
```

```python
import functools

import jax
import jax.numpy as jnp
from jax import lax
from jax.experimental import pallas as pl
from jax.experimental.pallas import tpu as pltpu
from jax.sharding import PartitionSpec as P

HEAD_SIZE = 128
CORES = 2
CHUNK = 512
SLOTS = 3
LANES = 128

norm_eps = 1e-06
grad_weight = 16.0
masked_fill = -1e30

f32 = jnp.float32
bf16 = jnp.bfloat16

NT = (((1,), (1,)), ((), ()))
NN = (((1,), (0,)), ((), ()))
TN = (((0,), (0,)), ((), ()))


def dot(a, b, dims):
    return lax.dot_general(a, b, dims, preferred_element_type=f32)


def smem():
    return pl.BlockSpec(memory_space=pltpu.SMEM)


def vmem():
    return pl.BlockSpec(memory_space=pltpu.VMEM)


def shape(dims, dtype):
    return jax.ShapeDtypeStruct(dims, dtype)


def call(body, outs, ins, scratch=(), limit=48, flops=0, moved=0, exps=0):
    return pl.pallas_call(
        body,
        out_shape=outs,
        in_specs=ins,
        out_specs=jax.tree.map(lambda _: vmem(), outs),
        scratch_shapes=list(scratch),
        compiler_params=pltpu.CompilerParams(vmem_limit_bytes=limit * 2**20),
        cost_estimate=pl.CostEstimate(flops=flops, bytes_accessed=moved, transcendentals=exps),
    )


def shifted(value, axis, step, inner=1):
    size = lax.axis_size(axis)
    outer = size // inner
    pairs = [(i, ((i // inner + step) % outer) * inner + i % inner) for i in range(size)]
    return lax.ppermute(value, axis, pairs)


def swapped(value):
    size = lax.axis_size("ctx")
    return lax.ppermute(value, "ctx", [(i, i ^ 1) for i in range(size)])


def row_choice(loss_per, tokens, place, rows):
    base = place[3] * loss_per
    row_iota = lax.broadcasted_iota(jnp.int32, (loss_per, tokens), 0)
    col_iota = lax.broadcasted_iota(jnp.int32, (loss_per, tokens), 1)
    sel = jnp.zeros((loss_per, tokens), f32)
    for j in range(loss_per):
        sel = jnp.where((row_iota == j) & (col_iota == rows[base + j]), 1.0, sel)
    return sel.astype(bf16)


def pick_body(loss_per, place, rows, hidden, picked):
    tokens, width = hidden.shape
    mine = dot(row_choice(loss_per, tokens, place, rows), hidden[...], NN)
    half = width // 2
    picked[...] = jnp.concatenate([mine[:, :half], mine[:, half:]], axis=0).astype(bf16)


def pack_body(loss_per, place, rows, queries, keys, values, packed):
    tokens, key_width = keys.shape
    mine = dot(row_choice(loss_per, tokens, place, rows), queries[...], NN)
    packed[0:tokens, 0:key_width] = keys[...]
    packed[0:tokens, key_width : 2 * key_width] = values[...]
    parts = queries.shape[1] // (2 * key_width)
    stacked = [mine[:, b * 2 * key_width : (b + 1) * 2 * key_width] for b in range(parts)]
    packed[tokens : tokens + parts * loss_per, :] = jnp.concatenate(stacked, axis=0).astype(bf16)


def target_body(place, targets, weight, out, buf, spots, sems):
    blocks, loss, block_width = out.shape
    width = blocks * block_width
    total_rows = weight.shape[0]
    offset = targets[...] - place[4]
    local = (offset >= 0) & (offset < total_rows)
    offset = offset.astype(f32)
    index = lax.broadcasted_iota(jnp.int32, (1, loss), 1).astype(f32)
    none = float(loss)
    count = jnp.sum(jnp.where(local, 1.0, 0.0)).astype(jnp.int32)

    def copy(k, at):
        start = pl.multiple_of(lax.div(at, 16) * 16, 16)
        return pltpu.make_async_copy(weight.at[pl.ds(start, 16), :], buf.at[k], sems.at[k])

    def begin(k, left):
        spot = jnp.min(left)
        at = jnp.sum(jnp.where(index == spot, offset, 0.0)).astype(jnp.int32)
        spots[0, k] = spot.astype(jnp.int32)
        spots[1, k] = at
        copy(k, at).start()
        return jnp.where(index == spot, none, left)

    lax.fori_loop(0, count, begin, jnp.where(local, index, none))
    out[...] = jnp.zeros_like(out)
    line = lax.broadcasted_iota(jnp.int32, (16, block_width), 0)

    @pl.loop(0, count)
    def _(k):
        spot, at = spots[0, k], spots[1, k]
        copy(k, at).wait()
        group = pl.ds(pl.multiple_of(lax.div(spot, 16) * 16, 16), 16)
        for b in range(blocks):
            block = buf[k, :, b * block_width : (b + 1) * block_width].astype(f32)
            row = jnp.sum(jnp.where(line == lax.rem(at, 16), block, 0.0), axis=0, keepdims=True)
            before = out[b, group, :].astype(f32)
            out[b, group, :] = jnp.where(line == lax.rem(spot, 16), row, before).astype(bf16)


def flash_body(
    first,
    place,
    own,
    other,
    gain,
    targets,
    weight,
    keep,
    send,
    stats,
    unit,
    normed,
    raw,
    acc,
    probs,
    state,
    head_buf,
    buf,
    head_sem,
    sems,
):
    vocab_at, z_at, core_at, ctx_at, first_id = (place[k] for k in range(5))
    nv, nz = own.shape[0], own.shape[1]
    loss, width = normed.shape
    half = own.shape[3]
    total_rows = weight.shape[0]
    chunks = (total_rows - first) // CHUNK
    blocks = acc.shape[0]
    block_width = width // blocks

    def head_copy():
        return pltpu.make_async_copy(weight.at[pl.ds(0, first), :], head_buf, head_sem)

    def body_copy(c):
        slot = lax.rem(c, SLOTS)
        start = pl.multiple_of(first + c * CHUNK, 16)
        return pltpu.make_async_copy(
            weight.at[pl.ds(start, CHUNK), :], buf.at[slot], sems.at[slot]
        )

    head_copy().start()
    for c in range(min(SLOTS, chunks)):
        body_copy(c).start()

    is_even = core_at == 0
    for zr in range(nz):
        z_src = lax.rem(z_at - zr + nz, nz)
        square_own = jnp.zeros((8, 1), f32)
        square_other = jnp.zeros((8, 1), f32)
        for vr in range(nv):
            a = own[vr, zr].astype(f32)
            b = other[vr, zr].astype(f32)
            square_a = jnp.sum(a * a, axis=1, keepdims=True)
            square_b = jnp.sum(b * b, axis=1, keepdims=True)
            square_own += square_a[:8] + square_a[8:]
            square_other += square_b[:8] + square_b[8:]
        square = jnp.concatenate(
            [
                jnp.where(is_even, square_own, square_other),
                jnp.where(is_even, square_other, square_own),
            ],
            axis=0,
        )
        inv = lax.rsqrt(square / width + norm_eps)
        row_at = pl.multiple_of(z_src * 16, 16)
        state[pl.ds(row_at, 16), :] = jnp.broadcast_to(inv, (16, LANES))
        for vr in range(nv):
            v_src = lax.rem(vocab_at - vr + nv, nv)
            a = own[vr, zr].astype(f32)
            b = other[vr, zr].astype(f32)
            low = jnp.where(is_even, a, b)
            high = jnp.where(is_even, b, a)
            for k in range(2):
                x = jnp.concatenate([low[8 * k : 8 * k + 8], high[8 * k : 8 * k + 8]], axis=0)
                lane_at = pl.multiple_of((v_src * 2 + k) * half, half)
                raw[pl.ds(row_at, 16), pl.ds(lane_at, half)] = x.astype(bf16)
                normed[pl.ds(row_at, 16), pl.ds(lane_at, half)] = (
                    x * inv * gain[:, pl.ds(lane_at, half)]
                ).astype(bf16)

    per_vocab = loss // nv
    mine_at = pl.multiple_of(vocab_at * per_vocab, per_vocab)
    feature_at = pl.multiple_of(ctx_at * block_width, block_width)
    unit[...] = (
        raw[pl.ds(mine_at, per_vocab), pl.ds(feature_at, block_width)].astype(f32)
        * state[pl.ds(mine_at, per_vocab), 0:1]
    )

    target_col = targets[...]

    def softmax(scores, base, before):
        cols = scores.shape[1]
        ids = base + lax.broadcasted_iota(jnp.int32, (loss, cols), 1)
        hit = ids == target_col
        top = jnp.max(scores, axis=1, keepdims=True)
        if before is not None:
            top = jnp.maximum(top, before[0])
        shifted_scores = scores - top
        weights = jnp.exp(shifted_scores)
        total = jnp.sum(weights, axis=1, keepdims=True)
        moment = jnp.sum(weights * shifted_scores, axis=1, keepdims=True)
        logit = jnp.sum(jnp.where(hit, scores, 0.0), axis=1, keepdims=True)
        scale = None
        if before is not None:
            gap = before[0] - top
            scale = jnp.exp(gap)
            total = total + before[1] * scale
            moment = moment + scale * (before[2] + gap * before[1])
            logit = logit + before[3]
        masked = jnp.where(hit, 0.0, weights).astype(bf16)
        return masked, scale, (top, total, moment, logit)

    def scores_of(block):
        return dot(block, normed[...], NT).T

    def add_product(p, scale, read):
        for b in range(blocks):
            part = dot(p, read(b * block_width, block_width), NN)
            if scale is None:
                acc[b] = part
            else:
                acc[b] = acc[b] * scale + part

    head_copy().wait()
    p, _, run = softmax(scores_of(head_buf[...]), first_id, None)
    add_product(p, None, lambda at, n: head_buf[:, at : at + n])
    if chunks:
        body_copy(0).wait()
        p, scale, run = softmax(scores_of(buf[0]), first_id + first, run)
        probs[...] = p

        def step(c, carry):
            scale, run = carry
            body_copy(c).wait()
            here = lax.rem(c, SLOTS)
            there = lax.rem(c - 1, SLOTS)
            scores = scores_of(buf[here])
            add_product(probs[...], scale, lambda at, n: buf[there, :, at : at + n])

            p, scale, run = softmax(scores, first_id + first + c * CHUNK, run)
            probs[...] = p

            @pl.when(c + SLOTS - 1 < chunks)
            def _():
                body_copy(c + SLOTS - 1).start()

            return scale, run

        scale, run = lax.fori_loop(1, chunks, step, (scale, run))
        last = (chunks - 1) % SLOTS
        add_product(probs[...], scale, lambda at, n: buf[last, :, at : at + n])

    for z in range(nz):
        keep[z] = acc[CORES * z + core_at]
        send[:, z * block_width : (z + 1) * block_width] = acc[CORES * z + 1 - core_at].astype(bf16)
    send[:, nz * block_width :] = split_columns(run)
    stats[...] = with_stats(state[...], run)


def split_columns(columns):
    rows = columns[0].shape[0]
    lane = lax.broadcasted_iota(jnp.int32, (rows, LANES), 1)
    table = jnp.zeros((rows, LANES), f32)
    for k, column in enumerate(columns):
        rest = column
        for j in range(3):
            term = rest.astype(bf16).astype(f32)
            table = jnp.where(lane == 3 * k + j, term, table)
            rest = rest - term
    return table.astype(bf16)


def joined_columns(block, count):
    block = block.astype(f32)
    return [
        block[:, 3 * k : 3 * k + 1] + block[:, 3 * k + 1 : 3 * k + 2] + block[:, 3 * k + 2 : 3 * k + 3]
        for k in range(count)
    ]


def stats_of(table):
    return [table[:, k : k + 1] for k in range(4)]


def merge_stats(columns):
    top = functools.reduce(jnp.maximum, [c[0] for c in columns])
    gaps = [c[0] - top for c in columns]
    scales = [jnp.exp(g) for g in gaps]
    total = sum(s * c[1] for s, c in zip(scales, columns))
    moment = sum(s * (c[2] + g * c[1]) for s, g, c in zip(scales, gaps, columns))
    logit = sum(c[3] for c in columns)
    return scales, (top, total, moment, logit)


def with_stats(table, merged):
    lane = lax.broadcasted_iota(jnp.int32, table.shape, 1)
    for k in range(4):
        table = jnp.where(lane == k, merged[k], table)
    return table


def core_body(count, place, keep, got, mine, target_rows, new_stats, new_keep, new_rows, *rest):
    sends, (total, table, message, rows_here, sem) = rest[:count], rest[count:]
    nz, loss, block = keep.shape
    rows_copy = pltpu.make_async_copy(target_rows, rows_here, sem)
    rows_copy.start()
    columns = [stats_of(mine[...]), joined_columns(got[:, nz * block :], 4)]
    scales, merged = merge_stats(columns)
    table[...] = with_stats(mine[...], merged)
    message[...] = split_columns(merged)
    per = loss // (count + 1)
    for z in range(nz):
        other = got[:, z * block : (z + 1) * block].astype(f32)
        total[z] = keep[z] * scales[0] + other * scales[1]
    at = pl.multiple_of(place[0] * per, per)
    new_stats[...] = table[pl.ds(at, per), :]
    new_keep[...] = total[:, pl.ds(at, per), :]
    for s in range(count):
        to = lax.rem(place[0] + s + 1, count + 1)
        rows = pl.ds(pl.multiple_of(to * per, per), per)
        for z in range(nz):
            sends[s][:, z * block : (z + 1) * block] = total[z, rows, :].astype(bf16)
        sends[s][:, (nz + 1) * block :] = message[rows, :]
    rows_copy.wait()
    for s in range(count):
        to = lax.rem(place[0] + s + 1, count + 1)
        rows = pl.ds(pl.multiple_of(to * per, per), per)
        sends[s][:, nz * block : (nz + 1) * block] = rows_here[rows, :]
    new_rows[...] = rows_here[pl.ds(at, per), :]


def plane_body(count, place, keep, mine, target_rows, *rest):
    got, rest = rest[:count], rest[count:]
    new_stats, new_keep, new_target = rest[:3]
    sends, (total,) = rest[3:-1], rest[-1:]
    nz, per, block = keep.shape
    columns = [stats_of(mine[...])] + [joined_columns(g[:, (nz + 1) * block :], 4) for g in got]
    scales, merged = merge_stats(columns)
    new_stats[...] = with_stats(mine[...], merged)
    message = split_columns(merged)
    for z in range(nz):
        value = keep[z] * scales[0]
        for k in range(count):
            value = value + got[k][:, z * block : (z + 1) * block].astype(f32) * scales[k + 1]
        total[z] = value
    new_keep[...] = total[place[1]]
    rows = target_rows[...].astype(f32)
    for k in range(count):
        rows = rows + got[k][:, nz * block : (nz + 1) * block].astype(f32)
    new_target[...] = rows.astype(bf16)
    for s in range(nz - 1):
        sends[s][:, :block] = total[lax.rem(place[1] + s + 1, nz)].astype(bf16)
        sends[s][:, block:] = message


def line_body(count, width, place, keep, mine, target_rows, unit, gain, *rest):
    got, (message,) = rest[:count], rest[count:]
    per, block = keep.shape
    columns = [stats_of(mine[...])] + [joined_columns(g[:, block:], 4) for g in got]
    scales, (top, total, moment, logit) = merge_stats(columns)
    log_total = top + jnp.log(total)
    value = keep[...] * (scales[0] / total)
    for k in range(count):
        value = value + got[k][:, :block].astype(f32) * (scales[k + 1] / total)
    inner = grad_weight * (moment / total + (top - logit)) / width
    short = jnp.exp(logit - log_total) - 1.0
    inv = mine[:, 4:5]
    grad = grad_weight * (value + short * target_rows[...].astype(f32))
    gain_at = pl.multiple_of(place[3] * block, block)
    scaled = grad * gain[:, pl.ds(gain_at, block)]
    message[:, :block] = (inv * (scaled - unit[...] * inner)).astype(bf16)
    message[:, block:] = split_columns([log_total - logit])


def project_body(nv, place, *refs):
    gathered, (weight, resid, loss_out, keep, send, whole, partial) = refs[:nv], refs[nv:]
    per = gathered[0].shape[0]
    block = whole.shape[1]
    loss_sum = jnp.zeros((1, 1), f32)
    for v in range(nv):
        src = lax.rem(place[0] - v + nv, nv)
        whole[pl.ds(pl.multiple_of(src * per, per), per), :] = gathered[v][:, :block]
        (column,) = joined_columns(gathered[v][:, block:], 1)
        loss_sum = loss_sum + jnp.sum(column, axis=0, keepdims=True)
    loss_out[...] = jnp.broadcast_to(loss_sum / (nv * per), loss_out.shape)
    resid[...] = whole[...]
    partial[...] = dot(whole[...], weight[...], NT)
    cols = keep.shape[1]
    keep[...] = partial[:, pl.ds(pl.multiple_of(place[2] * cols, cols), cols)]
    send[...] = partial[:, pl.ds(pl.multiple_of((1 - place[2]) * cols, cols), cols)].astype(bf16)


def half_body(place, keep, got, new_keep, *rest):
    sends, (total,) = rest[:-1], rest[-1:]
    per = new_keep.shape[0]
    nz = len(sends) + 1
    total[...] = keep[...] + got[...].astype(f32)
    new_keep[...] = total[pl.ds(pl.multiple_of(place[1] * per, per), per), :]
    for s in range(nz - 1):
        to = lax.rem(place[1] + s + 1, nz)
        sends[s][...] = total[pl.ds(pl.multiple_of(to * per, per), per), :].astype(bf16)


def sum_body(keep, *refs):
    value = keep[...]
    for ref in refs[:-1]:
        value = value + ref[...].astype(f32)
    refs[-1][...] = value.astype(bf16)


def forward_body(
    loss_per, heads, group, heads_at_once, place, key_pos, query_pos, packed, p_own, p_rows, out, scratch
):
    nc = packed.shape[0]
    tokens = p_own.shape[2]
    loss = loss_per * nc
    key_width = heads * HEAD_SIZE
    score_scale = HEAD_SIZE ** (-0.5)
    ctx_at = place[3]
    own_at = pl.multiple_of(ctx_at * tokens, tokens)
    row_at = pl.multiple_of(ctx_at * loss_per, loss_per)
    for j in range(heads):
        key = jnp.concatenate(
            [packed[c, 0:tokens, j * HEAD_SIZE : (j + 1) * HEAD_SIZE] for c in range(nc)], axis=0
        )
        at = key_width + j * HEAD_SIZE
        value = jnp.concatenate(
            [packed[c, 0:tokens, at : at + HEAD_SIZE] for c in range(nc)], axis=0
        )
        for g0 in range(0, group, heads_at_once):
            stacked = []
            for g in range(g0, g0 + heads_at_once):
                stacked.append(query_of(packed, j * group + g, tokens, loss_per, key_width))
            query = jnp.concatenate(stacked, axis=0).astype(bf16)
            where_at = jnp.concatenate([query_pos[...]] * heads_at_once, axis=0)
            visible = key_pos[...] <= where_at
            scores = jnp.where(visible, dot(query, key, NT) * score_scale, masked_fill)
            top = jnp.max(scores, axis=1, keepdims=True)
            raw = jnp.where(visible, jnp.exp(scores - top), 0.0)
            prob = raw / jnp.sum(raw, axis=1, keepdims=True)
            scratch[...] = prob
            coarse = prob.astype(bf16)
            fine = (prob - coarse.astype(f32)).astype(bf16)
            first = g0 * loss
            n = heads_at_once * loss
            out[j, first : first + n, :] = dot(coarse, value, NN) + dot(fine, value, NN)
            p_own[j, first : first + n, :] = scratch[:, pl.ds(own_at, tokens)]
            for k in range(heads_at_once):
                p_rows[j, (g0 + k) * loss_per : (g0 + k + 1) * loss_per, :] = scratch[
                    pl.ds(pl.multiple_of(k * loss + row_at, loss_per), loss_per), :
                ]


def query_of(packed, head, tokens, loss_per, key_width):
    lane = head * HEAD_SIZE
    b, at = lane // (2 * key_width), lane % (2 * key_width)
    parts = []
    for c in range(packed.shape[0]):
        block = packed[c, tokens:, at : at + HEAD_SIZE].astype(f32)
        parts.append(block[b * loss_per : (b + 1) * loss_per])
    return jnp.concatenate(parts, axis=0)


def backward_body(
    loss_per, heads, group, place, half, other, packed, p_own, p_rows, out, query_grad, key_grad, value_grad, grad
):
    nc = packed.shape[0]
    tokens = p_own.shape[2]
    loss = loss_per * nc
    key_width = heads * HEAD_SIZE
    score_scale = HEAD_SIZE ** (-0.5)
    ctx_at = place[3]
    nz, rows, cols = half.shape
    col_at = pl.multiple_of(place[2] * cols, cols)
    other_at = pl.multiple_of((1 - place[2]) * cols, cols)
    for s in range(nz):
        row_at = pl.multiple_of(lax.rem(place[1] - s + nz, nz) * rows, rows)
        grad[pl.ds(row_at, rows), pl.ds(col_at, cols)] = half[s].astype(f32)
        grad[pl.ds(row_at, rows), pl.ds(other_at, cols)] = other[s].astype(f32)
    mine_at = pl.multiple_of(ctx_at * loss_per, loss_per)
    for j in range(heads):
        lanes = [slice((j * group + g) * HEAD_SIZE, (j * group + g + 1) * HEAD_SIZE) for g in range(group)]
        d_out = jnp.concatenate([grad[:, s] for s in lanes], axis=0)
        d_half = d_out.astype(bf16)
        delta = jnp.sum(d_out * out[j], axis=1, keepdims=True)
        query = jnp.concatenate(
            [query_of(packed, j * group + g, tokens, loss_per, key_width) for g in range(group)], axis=0
        ).astype(bf16)
        at = key_width + j * HEAD_SIZE
        own_value = packed[ctx_at, 0:tokens, at : at + HEAD_SIZE]
        prob = p_own[j]
        score_grad = (prob * (dot(d_half, own_value, NT) - delta)).astype(bf16)
        k_lanes = slice(j * HEAD_SIZE, (j + 1) * HEAD_SIZE)
        key_grad[:, k_lanes] = (dot(score_grad, query, TN) * score_scale).astype(bf16)
        value_grad[:, k_lanes] = dot(prob.astype(bf16), d_half, TN).astype(bf16)
        key = jnp.concatenate([packed[c, 0:tokens, k_lanes] for c in range(nc)], axis=0)
        value = jnp.concatenate([packed[c, 0:tokens, at : at + HEAD_SIZE] for c in range(nc)], axis=0)
        d_mine = jnp.concatenate([grad[pl.ds(mine_at, loss_per), s] for s in lanes], axis=0)
        out_mine = jnp.concatenate(
            [
                out[j, pl.ds(pl.multiple_of(g * loss + mine_at, loss_per), loss_per), :]
                for g in range(group)
            ],
            axis=0,
        )
        delta = jnp.sum(d_mine * out_mine, axis=1, keepdims=True)
        d_prob = dot(d_mine.astype(bf16), value, NT)
        score_grad = (p_rows[j] * (d_prob - delta)).astype(bf16)
        result = dot(score_grad, key, NN) * score_scale
        for g in range(group):
            query_grad[:, lanes[g]] = result[g * loss_per : (g + 1) * loss_per].astype(bf16)


def per_device(
    hidden,
    norm_gain,
    head_weight,
    targets,
    loss_rows,
    stretch_of_slot,
    queries,
    key_states,
    attention_values,
    output_weight,
):
    nc = lax.axis_size("ctx")
    nv = lax.axis_size("vocab")
    nz = nc // CORES
    ctx_at = lax.axis_index("ctx")
    vocab_at = lax.axis_index("vocab")
    tokens = hidden.shape[0]
    stretch_len = tokens // 2
    loss = loss_rows.shape[0]
    loss_per = loss // nc
    width = norm_gain.shape[0]
    voc_rows = head_weight.shape[0]
    part_width = hidden.shape[1]
    query_width = queries.shape[1]
    key_width = key_states.shape[1]
    heads = key_width // HEAD_SIZE
    group = query_width // key_width
    block_width = width // nc
    per_vocab = loss // nv
    all_tokens = tokens * nc

    first_id = (vocab_at * nc + ctx_at) * voc_rows
    place = jnp.stack([vocab_at, ctx_at // CORES, ctx_at % CORES, ctx_at, first_id]).astype(jnp.int32)

    slots = stretch_of_slot.shape[0]
    owner = lax.broadcasted_iota(jnp.int32, (loss, 1), 0) // loss_per
    slot = 2 * owner + loss_rows[:, None] // stretch_len
    slot_iota = lax.broadcasted_iota(jnp.int32, (1, slots), 1)
    stretch = jnp.sum(jnp.where(slot == slot_iota, stretch_of_slot[None, :], 0), axis=1, keepdims=True)
    query_pos = stretch * stretch_len + loss_rows[:, None] % stretch_len
    key_pos = (
        stretch_of_slot[:, None] * stretch_len
        + lax.broadcasted_iota(jnp.int32, (1, stretch_len), 1)
    ).reshape(1, all_tokens)
    picked = call(
        functools.partial(pick_body, loss_per),
        shape((2 * loss_per, part_width // 2), bf16),
        [smem(), smem(), vmem()],
    )(place, loss_rows, hidden)
    picked, queries = lax.optimization_barrier((picked, queries))
    extra = (query_width // (2 * key_width)) * loss_per
    packed = call(
        functools.partial(pack_body, loss_per),
        shape((tokens + extra, 2 * key_width), bf16),
        [smem(), smem()] + [vmem()] * 3,
    )(place, loss_rows, queries, key_states, attention_values)
    by_z = jnp.stack([picked] + [shifted(picked, "ctx", s, CORES) for s in range(1, nz)])
    planes = [by_z] + [shifted(by_z, "vocab", s) for s in range(1, nv)]
    by_z, targets_late = lax.optimization_barrier((by_z, targets))
    if voc_rows % 16:
        local = targets_late - first_id
        is_local = (local >= 0) & (local < voc_rows)
        target_rows = head_weight.at[jnp.clip(local, 0, voc_rows - 1)].get(mode="promise_in_bounds")
        target_rows = jnp.where(is_local[:, None], target_rows, jnp.zeros((), bf16))
        target_rows = target_rows.reshape(loss, nc, block_width).transpose(1, 0, 2)
    else:
        target_rows = pl.pallas_call(
            target_body,
            out_shape=shape((nc, loss, block_width), bf16),
            in_specs=[smem(), vmem(), pl.BlockSpec(memory_space=pl.ANY)],
            out_specs=vmem(),
            scratch_shapes=[
                pltpu.VMEM((loss, 16, width), bf16),
                pltpu.SMEM((2, loss), jnp.int32),
                pltpu.SemaphoreType.DMA((loss,)),
            ],
            compiler_params=pltpu.CompilerParams(vmem_limit_bytes=40 * 2**20),
            cost_estimate=pl.CostEstimate(
                flops=0, bytes_accessed=2 * 16 * loss * width, transcendentals=0
            ),
        )(place, targets_late.reshape(1, loss), head_weight)
    target_rows = lax.psum_scatter(
        target_rows.reshape(nc * loss, block_width), "ctx", scatter_dimension=0, tiled=True
    )
    by_plane = jnp.stack(planes)
    other = swapped(by_plane)
    other, packed = lax.optimization_barrier((other, packed))
    packed_all = lax.all_gather(packed, "ctx")

    first = voc_rows % CHUNK
    if voc_rows < SLOTS * CHUNK or first % 16 or not first:
        first = voc_rows if voc_rows < SLOTS * CHUNK else CHUNK
    chunks = (voc_rows - first) // CHUNK
    gain = norm_gain.reshape(1, width)
    keep, send, stats, unit = pl.pallas_call(
        functools.partial(flash_body, first),
        out_shape=(
            shape((nz, loss, block_width), f32),
            shape((loss, nz * block_width + LANES), bf16),
            shape((loss, LANES), f32),
            shape((per_vocab, block_width), f32),
        ),
        in_specs=[smem()] + [vmem()] * 4 + [pl.BlockSpec(memory_space=pl.ANY)],
        out_specs=[vmem()] * 4,
        scratch_shapes=[
            pltpu.VMEM((loss, width), bf16),
            pltpu.VMEM((loss, width), bf16),
            pltpu.VMEM((nc, loss, block_width), f32),
            pltpu.VMEM((loss, CHUNK), bf16),
            pltpu.VMEM((loss, LANES), f32),
            pltpu.VMEM((first, width), bf16),
            pltpu.VMEM((SLOTS if chunks else 1, CHUNK if chunks else 16, width), bf16),
            pltpu.SemaphoreType.DMA,
            pltpu.SemaphoreType.DMA((SLOTS,)),
        ],
        compiler_params=pltpu.CompilerParams(vmem_limit_bytes=50 * 2**20),
        cost_estimate=pl.CostEstimate(
            flops=4 * max(loss, 256) * width * voc_rows,
            bytes_accessed=4 * width * voc_rows,
            transcendentals=loss * voc_rows,
        ),
    )(place, by_plane, other, gain, targets.reshape(loss, 1), head_weight)

    at_once = max(1, min(group, (4 * 2**20) // (loss * all_tokens * 4)))
    p_own, p_rows, out = call(
        functools.partial(forward_body, loss_per, heads, group, at_once),
        (
            shape((heads, group * loss, tokens), f32),
            shape((heads, group * loss_per, all_tokens), f32),
            shape((heads, group * loss, HEAD_SIZE), f32),
        ),
        [smem()] + [vmem()] * 3,
        [pltpu.VMEM((at_once * loss, all_tokens), f32)],
        flops=6 * heads * group * loss * all_tokens * HEAD_SIZE,
        moved=2 * packed_all.size,
        exps=heads * group * loss * all_tokens,
    )(place, key_pos, query_pos, packed_all)

    got = swapped(send)
    stats, keep, target_rows, *sends = call(
        functools.partial(core_body, nv - 1),
        (
            shape((per_vocab, LANES), f32),
            shape((nz, per_vocab, block_width), f32),
            shape((per_vocab, block_width), bf16),
        )
        + (shape((per_vocab, (nz + 1) * block_width + LANES), bf16),) * (nv - 1),
        [smem()] + [vmem()] * 3 + [pl.BlockSpec(memory_space=pl.ANY)],
        [
            pltpu.VMEM((nz, loss, block_width), f32),
            pltpu.VMEM((loss, LANES), f32),
            pltpu.VMEM((loss, LANES), bf16),
            pltpu.VMEM((loss, block_width), bf16),
            pltpu.SemaphoreType.DMA,
        ],
    )(place, keep, got, stats, target_rows)
    got = [shifted(sends[s - 1], "vocab", s) for s in range(1, nv)]

    stats, query_pos = lax.optimization_barrier((stats, query_pos))
    at_once = max(1, min(group, (4 * 2**20) // (loss * all_tokens * 4)))
    p_own, p_rows, out = call(
        functools.partial(forward_body, loss_per, heads, group, at_once),
        (
            shape((heads, group * loss, tokens), f32),
            shape((heads, group * loss_per, all_tokens), f32),
            shape((heads, group * loss, HEAD_SIZE), f32),
        ),
        [smem()] + [vmem()] * 3,
        [pltpu.VMEM((at_once * loss, all_tokens), f32)],
        flops=6 * heads * group * loss * all_tokens * HEAD_SIZE,
        moved=2 * packed_all.size,
        exps=heads * group * loss * all_tokens,
    )(place, key_pos, query_pos, packed_all)
    stats, p_own, p_rows, out = lax.optimization_barrier((stats, p_own, p_rows, out))

    stats, keep, target_rows, *sends = call(
        functools.partial(plane_body, nv - 1),
        (
            shape((per_vocab, LANES), f32),
            shape((per_vocab, block_width), f32),
            shape((per_vocab, block_width), bf16),
        )
        + (shape((per_vocab, block_width + LANES), bf16),) * (nz - 1),
        [smem()] + [vmem()] * (3 + nv - 1),
        [pltpu.VMEM((nz, per_vocab, block_width), f32)],
    )(place, keep, stats, target_rows, *got)
    got = [shifted(sends[s - 1], "ctx", s, CORES) for s in range(1, nz)]
    message = call(
        functools.partial(line_body, nz - 1, width),
        shape((per_vocab, block_width + LANES), bf16),
        [smem()] + [vmem()] * (5 + nz - 1),
    )(place, keep, stats, target_rows, unit, gain, *got)

    gathered = [message] + [shifted(message, "vocab", s) for s in range(1, nv)]
    cols = query_width // CORES
    rows = loss // nz
    resid_rows, mean_loss, keep, send = call(
        functools.partial(project_body, nv),
        (
            shape((loss, block_width), bf16),
            shape((8, LANES), f32),
            shape((loss, cols), f32),
            shape((loss, cols), bf16),
        ),
        [smem()] + [vmem()] * (nv + 1),
        [pltpu.VMEM((loss, block_width), bf16), pltpu.VMEM((loss, query_width), f32)],
    )(place, *gathered, output_weight)
    keep, *sends = call(
        half_body,
        (shape((rows, cols), f32),) + (shape((rows, cols), bf16),) * (nz - 1),
        [smem()] + [vmem()] * 2,
        [pltpu.VMEM((loss, cols), f32)],
    )(place, keep, swapped(send))
    got = [shifted(sends[s - 1], "ctx", s, CORES) for s in range(1, nz)]
    piece = call(sum_body, shape((rows, cols), bf16), [vmem()] * nz)(keep, *got)
    half = jnp.stack([piece] + [shifted(piece, "ctx", s, CORES) for s in range(1, nz)])
    other = swapped(half)
    query_grad, key_grad, value_grad = call(
        functools.partial(backward_body, loss_per, heads, group),
        (
            shape((loss_per, query_width), bf16),
            shape((tokens, key_width), bf16),
            shape((tokens, key_width), bf16),
        ),
        [smem()] + [vmem()] * 6,
        [pltpu.VMEM((loss, query_width), f32)],
    )(place, half, other, packed_all, p_own, p_rows, out)
    return (mean_loss[0, 0], query_grad, key_grad, value_grad, resid_rows.T)


def solution(mesh):
    placed = (
        P("ctx", "vocab"),
        P(),
        P(("vocab", "ctx"), None),
        P(),
        P(),
        P(),
        P("ctx", "vocab"),
        P("ctx", "vocab"),
        P("ctx", "vocab"),
        P("vocab", "ctx"),
    )
    return jax.shard_map(
        per_device,
        mesh=mesh,
        in_specs=placed,
        out_specs=(P(), P("ctx", "vocab"), P("ctx", "vocab"), P("ctx", "vocab"), P("ctx", None)),
        check_vma=False,
    )
```

```python
import functools

import jax
import jax.numpy as jnp
from jax import lax
from jax.experimental import pallas as pl
from jax.experimental.pallas import tpu as pltpu
from jax.sharding import PartitionSpec as P

HEAD_SIZE = 128
CORES = 2
CHUNK = 512
SLOTS = 3
LANES = 128

norm_eps = 1e-06
grad_weight = 16.0
masked_fill = -1e30

f32 = jnp.float32
bf16 = jnp.bfloat16

NT = (((1,), (1,)), ((), ()))
NN = (((1,), (0,)), ((), ()))
TN = (((0,), (0,)), ((), ()))


def dot(a, b, dims):
    return lax.dot_general(a, b, dims, preferred_element_type=f32)


def smem():
    return pl.BlockSpec(memory_space=pltpu.SMEM)


def hbm():
    return pl.BlockSpec(memory_space=pltpu.HBM)


def vmem():
    return pl.BlockSpec(memory_space=pltpu.VMEM)


def shape(dims, dtype):
    return jax.ShapeDtypeStruct(dims, dtype)


def call(body, outs, ins, scratch=(), limit=16, flops=0, moved=0, exps=0):
    return pl.pallas_call(
        body,
        out_shape=outs,
        in_specs=ins,
        out_specs=jax.tree.map(lambda _: vmem(), outs),
        scratch_shapes=list(scratch),
        compiler_params=pltpu.CompilerParams(vmem_limit_bytes=limit * 2**20),
        cost_estimate=pl.CostEstimate(flops=flops, bytes_accessed=moved, transcendentals=exps),
    )


def shifted(value, axis, step, inner=1):
    size = lax.axis_size(axis)
    outer = size // inner
    pairs = [(i, ((i // inner + step) % outer) * inner + i % inner) for i in range(size)]
    return lax.ppermute(value, axis, pairs)


def crossed(value, bit):
    size = lax.axis_size("ctx")
    return lax.ppermute(value, "ctx", [(i, i ^ (bit * CORES)) for i in range(size)])


def swapped(value):
    size = lax.axis_size("ctx")
    return lax.ppermute(value, "ctx", [(i, i ^ 1) for i in range(size)])


def row_choice(loss_per, tokens, place, rows):
    base = place[3] * loss_per
    row_iota = lax.broadcasted_iota(jnp.int32, (loss_per, tokens), 0)
    col_iota = lax.broadcasted_iota(jnp.int32, (loss_per, tokens), 1)
    sel = jnp.zeros((loss_per, tokens), f32)
    for j in range(loss_per):
        sel = jnp.where((row_iota == j) & (col_iota == rows[base + j]), 1.0, sel)
    return sel.astype(bf16)


def pick_body(loss_per, place, rows, hidden, picked, here, sem):
    tokens, width = hidden.shape
    copy = pltpu.make_async_copy(hidden, here, sem)
    copy.start()
    choice = row_choice(loss_per, tokens, place, rows)
    copy.wait()
    mine = dot(choice, here[...], NN)
    half = width // 2
    picked[...] = jnp.concatenate([mine[:, :half], mine[:, half:]], axis=0).astype(bf16)


def pack_body(loss_per, place, rows, queries, keys, values, packed):
    tokens, key_width = keys.shape
    mine = dot(row_choice(loss_per, tokens, place, rows), queries[...], NN)
    packed[0:tokens, 0:key_width] = keys[...]
    packed[0:tokens, key_width : 2 * key_width] = values[...]
    parts = queries.shape[1] // (2 * key_width)
    stacked = [mine[:, b * 2 * key_width : (b + 1) * 2 * key_width] for b in range(parts)]
    packed[tokens : tokens + parts * loss_per, :] = jnp.concatenate(stacked, axis=0).astype(bf16)


def target_body(place, targets, weight, out, buf, spots, sems):
    blocks, loss, block_width = out.shape
    width = blocks * block_width
    total_rows = weight.shape[0]
    offset = targets[...] - place[4]
    local = (offset >= 0) & (offset < total_rows)
    offset = offset.astype(f32)
    index = lax.broadcasted_iota(jnp.int32, (1, loss), 1).astype(f32)
    none = float(loss)
    count = jnp.sum(jnp.where(local, 1.0, 0.0)).astype(jnp.int32)

    def copy(k, at):
        start = pl.multiple_of(lax.div(at, 16) * 16, 16)
        return pltpu.make_async_copy(weight.at[pl.ds(start, 16), :], buf.at[k], sems.at[k])

    def begin(k, left):
        spot = jnp.min(left)
        at = jnp.sum(jnp.where(index == spot, offset, 0.0)).astype(jnp.int32)
        spots[0, k] = spot.astype(jnp.int32)
        spots[1, k] = at
        copy(k, at).start()
        return jnp.where(index == spot, none, left)

    lax.fori_loop(0, count, begin, jnp.where(local, index, none))
    out[...] = jnp.zeros_like(out)
    line = lax.broadcasted_iota(jnp.int32, (16, block_width), 0)

    @pl.loop(0, count)
    def _(k):
        spot, at = spots[0, k], spots[1, k]
        copy(k, at).wait()
        group = pl.ds(pl.multiple_of(lax.div(spot, 16) * 16, 16), 16)
        for b in range(blocks):
            block = buf[k, :, b * block_width : (b + 1) * block_width].astype(f32)
            row = jnp.sum(jnp.where(line == lax.rem(at, 16), block, 0.0), axis=0, keepdims=True)
            before = out[b, group, :].astype(f32)
            out[b, group, :] = jnp.where(line == lax.rem(spot, 16), row, before).astype(bf16)


def flash_body(
    first,
    place,
    own,
    other,
    gain,
    targets,
    weight,
    keep,
    send,
    stats,
    unit,
    normed,
    raw,
    acc,
    probs,
    state,
    head_buf,
    buf,
    head_sem,
    sems,
):
    vocab_at, z_at, core_at, ctx_at, first_id = (place[k] for k in range(5))
    nv, nz = own.shape[0], own.shape[1]
    loss, width = normed.shape
    half = own.shape[3]
    total_rows = weight.shape[0]
    chunks = (total_rows - first) // CHUNK
    blocks = acc.shape[0]
    block_width = width // blocks

    def head_copy():
        return pltpu.make_async_copy(weight.at[pl.ds(0, first), :], head_buf, head_sem)

    def body_copy(c):
        slot = lax.rem(c, SLOTS)
        start = pl.multiple_of(first + c * CHUNK, 16)
        return pltpu.make_async_copy(
            weight.at[pl.ds(start, CHUNK), :], buf.at[slot], sems.at[slot]
        )

    head_copy().start()
    for c in range(min(SLOTS, chunks)):
        body_copy(c).start()

    is_even = core_at == 0
    for zr in range(nz):
        z_src = lax.bitwise_xor(z_at, zr)
        square_own = jnp.zeros((8, 1), f32)
        square_other = jnp.zeros((8, 1), f32)
        for vr in range(nv):
            a = own[vr, zr].astype(f32)
            b = other[vr, zr].astype(f32)
            square_a = jnp.sum(a * a, axis=1, keepdims=True)
            square_b = jnp.sum(b * b, axis=1, keepdims=True)
            square_own += square_a[:8] + square_a[8:]
            square_other += square_b[:8] + square_b[8:]
        square = jnp.concatenate(
            [
                jnp.where(is_even, square_own, square_other),
                jnp.where(is_even, square_other, square_own),
            ],
            axis=0,
        )
        inv = lax.rsqrt(square / width + norm_eps)
        row_at = pl.multiple_of(z_src * 16, 16)
        state[pl.ds(row_at, 16), :] = jnp.broadcast_to(inv, (16, LANES))
        for vr in range(nv):
            v_src = lax.rem(vocab_at - vr + nv, nv)
            a = own[vr, zr].astype(f32)
            b = other[vr, zr].astype(f32)
            low = jnp.where(is_even, a, b)
            high = jnp.where(is_even, b, a)
            for k in range(2):
                x = jnp.concatenate([low[8 * k : 8 * k + 8], high[8 * k : 8 * k + 8]], axis=0)
                lane_at = pl.multiple_of((v_src * 2 + k) * half, half)
                raw[pl.ds(row_at, 16), pl.ds(lane_at, half)] = x.astype(bf16)
                normed[pl.ds(row_at, 16), pl.ds(lane_at, half)] = (
                    x * inv * gain[:, pl.ds(lane_at, half)]
                ).astype(bf16)

    per_vocab = loss // nv
    mine_at = pl.multiple_of(vocab_at * per_vocab, per_vocab)
    feature_at = pl.multiple_of(ctx_at * block_width, block_width)
    unit[...] = (
        raw[pl.ds(mine_at, per_vocab), pl.ds(feature_at, block_width)].astype(f32)
        * state[pl.ds(mine_at, per_vocab), 0:1]
    )

    target_col = targets[...]

    def softmax(scores, base, before):
        cols = scores.shape[1]
        ids = base + lax.broadcasted_iota(jnp.int32, (loss, cols), 1)
        hit = ids == target_col
        top = jnp.max(scores, axis=1, keepdims=True)
        if before is not None:
            top = jnp.maximum(top, before[0])
        shifted_scores = scores - top
        weights = jnp.exp(shifted_scores)
        total = jnp.sum(weights, axis=1, keepdims=True)
        moment = jnp.sum(weights * shifted_scores, axis=1, keepdims=True)
        logit = jnp.sum(jnp.where(hit, scores, 0.0), axis=1, keepdims=True)
        scale = None
        if before is not None:
            gap = before[0] - top
            scale = jnp.exp(gap)
            total = total + before[1] * scale
            moment = moment + scale * (before[2] + gap * before[1])
            logit = logit + before[3]
        masked = jnp.where(hit, 0.0, weights).astype(bf16)
        return masked, scale, (top, total, moment, logit)

    def scores_of(block):
        return dot(block, normed[...], NT).T

    def add_product(p, scale, read):
        for b in range(blocks):
            part = dot(p, read(b * block_width, block_width), NN)
            if scale is None:
                acc[b] = part
            else:
                acc[b] = acc[b] * scale + part

    head_copy().wait()
    p, _, run = softmax(scores_of(head_buf[...]), first_id, None)
    add_product(p, None, lambda at, n: head_buf[:, at : at + n])
    if chunks:
        body_copy(0).wait()
        p, scale, run = softmax(scores_of(buf[0]), first_id + first, run)
        probs[...] = p

        def step(c, carry):
            scale, run = carry
            body_copy(c).wait()
            here = lax.rem(c, SLOTS)
            there = lax.rem(c - 1, SLOTS)
            scores = scores_of(buf[here])
            add_product(probs[...], scale, lambda at, n: buf[there, :, at : at + n])

            p, scale, run = softmax(scores, first_id + first + c * CHUNK, run)
            probs[...] = p

            @pl.when(c + SLOTS - 1 < chunks)
            def _():
                body_copy(c + SLOTS - 1).start()

            return scale, run

        scale, run = lax.fori_loop(1, chunks, step, (scale, run))
        last = (chunks - 1) % SLOTS
        add_product(probs[...], scale, lambda at, n: buf[last, :, at : at + n])

    for z in range(nz):
        keep[z] = acc[CORES * z + core_at]
        send[:, z * block_width : (z + 1) * block_width] = acc[CORES * z + 1 - core_at].astype(bf16)
    send[:, nz * block_width :] = split_columns(run)
    stats[...] = with_stats(state[...], run)


def split_columns(columns):
    rows = columns[0].shape[0]
    lane = lax.broadcasted_iota(jnp.int32, (rows, LANES), 1)
    table = jnp.zeros((rows, LANES), f32)
    for k, column in enumerate(columns):
        rest = column
        for j in range(3):
            term = rest.astype(bf16).astype(f32)
            table = jnp.where(lane == 3 * k + j, term, table)
            rest = rest - term
    return table.astype(bf16)


def joined_columns(block, count):
    block = block.astype(f32)
    return [
        block[:, 3 * k : 3 * k + 1] + block[:, 3 * k + 1 : 3 * k + 2] + block[:, 3 * k + 2 : 3 * k + 3]
        for k in range(count)
    ]


def stats_of(table):
    return [table[:, k : k + 1] for k in range(4)]


def merge_stats(columns):
    top = functools.reduce(jnp.maximum, [c[0] for c in columns])
    gaps = [c[0] - top for c in columns]
    scales = [jnp.exp(g) for g in gaps]
    total = sum(s * c[1] for s, c in zip(scales, columns))
    moment = sum(s * (c[2] + g * c[1]) for s, g, c in zip(scales, gaps, columns))
    logit = sum(c[3] for c in columns)
    return scales, (top, total, moment, logit)


def with_stats(table, merged):
    lane = lax.broadcasted_iota(jnp.int32, table.shape, 1)
    for k in range(4):
        table = jnp.where(lane == k, merged[k], table)
    return table


def core_body(count, place, keep, got, mine, target_rows, new_stats, new_keep, new_rows, *rest):
    sends, (total, table, message, rows_here, sem) = rest[:count], rest[count:]
    nz, loss, block = keep.shape
    rows_copy = pltpu.make_async_copy(target_rows, rows_here, sem)
    rows_copy.start()
    columns = [stats_of(mine[...]), joined_columns(got[:, nz * block :], 4)]
    scales, merged = merge_stats(columns)
    table[...] = with_stats(mine[...], merged)
    message[...] = split_columns(merged)
    per = loss // (count + 1)
    for z in range(nz):
        other = got[:, z * block : (z + 1) * block].astype(f32)
        total[z] = keep[z] * scales[0] + other * scales[1]
    at = pl.multiple_of(place[0] * per, per)
    new_stats[...] = table[pl.ds(at, per), :]
    new_keep[...] = total[:, pl.ds(at, per), :]
    for s in range(count):
        to = lax.rem(place[0] + s + 1, count + 1)
        rows = pl.ds(pl.multiple_of(to * per, per), per)
        for z in range(nz):
            sends[s][:, z * block : (z + 1) * block] = total[z, rows, :].astype(bf16)
        sends[s][:, (nz + 1) * block :] = message[rows, :]
    rows_copy.wait()
    for s in range(count):
        to = lax.rem(place[0] + s + 1, count + 1)
        rows = pl.ds(pl.multiple_of(to * per, per), per)
        sends[s][:, nz * block : (nz + 1) * block] = rows_here[rows, :]
    new_rows[...] = rows_here[pl.ds(at, per), :]


def plane_body(count, place, keep, mine, target_rows, *rest):
    got, rest = rest[:count], rest[count:]
    new_stats, new_keep, new_target = rest[:3]
    sends, (total,) = rest[3:-1], rest[-1:]
    nz, per, block = keep.shape
    columns = [stats_of(mine[...])] + [joined_columns(g[:, (nz + 1) * block :], 4) for g in got]
    scales, merged = merge_stats(columns)
    new_stats[...] = with_stats(mine[...], merged)
    message = split_columns(merged)
    for z in range(nz):
        value = keep[z] * scales[0]
        for k in range(count):
            value = value + got[k][:, z * block : (z + 1) * block].astype(f32) * scales[k + 1]
        total[z] = value
    new_keep[...] = total[place[1]]
    rows = target_rows[...].astype(f32)
    for k in range(count):
        rows = rows + got[k][:, nz * block : (nz + 1) * block].astype(f32)
    new_target[...] = rows.astype(bf16)
    for s in range(nz - 1):
        sends[s][:, :block] = total[lax.rem(place[1] + s + 1, nz)].astype(bf16)
        sends[s][:, block:] = message


def line_body(count, width, place, keep, mine, target_rows, unit, gain, *rest):
    got, (message,) = rest[:count], rest[count:]
    per, block = keep.shape
    columns = [stats_of(mine[...])] + [joined_columns(g[:, block:], 4) for g in got]
    scales, (top, total, moment, logit) = merge_stats(columns)
    log_total = top + jnp.log(total)
    value = keep[...] * (scales[0] / total)
    for k in range(count):
        value = value + got[k][:, :block].astype(f32) * (scales[k + 1] / total)
    inner = grad_weight * (moment / total + (top - logit)) / width
    short = jnp.exp(logit - log_total) - 1.0
    inv = mine[:, 4:5]
    grad = grad_weight * (value + short * target_rows[...].astype(f32))
    gain_at = pl.multiple_of(place[3] * block, block)
    scaled = grad * gain[:, pl.ds(gain_at, block)]
    message[:, :block] = (inv * (scaled - unit[...] * inner)).astype(bf16)
    message[:, block:] = split_columns([log_total - logit])


def project_body(nv, place, *refs):
    gathered, refs = refs[:nv], refs[nv:]
    weight, resid, loss_out, keep, send, whole, partial, here, sems = refs
    parts, part, _ = here.shape
    copies = [
        pltpu.make_async_copy(weight.at[pl.ds(k * part, part), :], here.at[k], sems.at[k])
        for k in range(parts)
    ]
    for copy in copies:
        copy.start()
    per = gathered[0].shape[0]
    block = whole.shape[1]
    loss_sum = jnp.zeros((1, 1), f32)
    for v in range(nv):
        src = lax.rem(place[0] - v + nv, nv)
        whole[pl.ds(pl.multiple_of(src * per, per), per), :] = gathered[v][:, :block]
        (column,) = joined_columns(gathered[v][:, block:], 1)
        loss_sum = loss_sum + jnp.sum(column, axis=0, keepdims=True)
    loss_out[...] = loss_sum / (nv * per)
    resid[...] = whole[...]
    for k in range(parts):
        copies[k].wait()
        partial[:, k * part : (k + 1) * part] = dot(whole[...], here[k], NT)
    cols = keep.shape[1]
    keep[...] = partial[:, pl.ds(pl.multiple_of(place[2] * cols, cols), cols)]
    send[...] = partial[:, pl.ds(pl.multiple_of((1 - place[2]) * cols, cols), cols)].astype(bf16)


def sum_body(keep, *refs):
    value = keep[...].astype(f32)
    for ref in refs[:-1]:
        value = value + ref[...].astype(f32)
    refs[-1][...] = value.astype(bf16)


def forward_body(
    loss_per, heads, group, heads_at_once, j, place, key_pos, query_pos, packed, p_own, p_rows, out, scratch
):
    nc = packed.shape[0]
    tokens = p_own.shape[1]
    loss = loss_per * nc
    key_width = heads * HEAD_SIZE
    score_scale = HEAD_SIZE ** (-0.5)
    ctx_at = place[3]
    own_at = pl.multiple_of(ctx_at * tokens, tokens)
    row_at = pl.multiple_of(ctx_at * loss_per, loss_per)
    key = jnp.concatenate(
        [packed[c, 0:tokens, j * HEAD_SIZE : (j + 1) * HEAD_SIZE] for c in range(nc)], axis=0
    )
    at = key_width + j * HEAD_SIZE
    value = jnp.concatenate(
        [packed[c, 0:tokens, at : at + HEAD_SIZE] for c in range(nc)], axis=0
    )
    for g0 in range(0, group, heads_at_once):
        stacked = []
        for g in range(g0, g0 + heads_at_once):
            stacked.append(query_of(packed, j * group + g, tokens, loss_per, key_width))
        query = jnp.concatenate(stacked, axis=0).astype(bf16)
        where_at = jnp.concatenate([query_pos[...]] * heads_at_once, axis=0)
        visible = key_pos[...] <= where_at
        scores = jnp.where(visible, dot(query, key, NT) * score_scale, masked_fill)
        top = jnp.max(scores, axis=1, keepdims=True)
        raw = jnp.where(visible, jnp.exp(scores - top), 0.0)
        prob = raw / jnp.sum(raw, axis=1, keepdims=True)
        scratch[...] = prob
        coarse = prob.astype(bf16)
        fine = (prob - coarse.astype(f32)).astype(bf16)
        first = g0 * loss
        n = heads_at_once * loss
        out[first : first + n, :] = dot(coarse, value, NN) + dot(fine, value, NN)
        p_own[first : first + n, :] = scratch[:, pl.ds(own_at, tokens)]
        for k in range(heads_at_once):
            p_rows[(g0 + k) * loss_per : (g0 + k + 1) * loss_per, :] = scratch[
                pl.ds(pl.multiple_of(k * loss + row_at, loss_per), loss_per), :
            ]


def query_of(packed, head, tokens, loss_per, key_width):
    lane = head * HEAD_SIZE
    b, at = lane // (2 * key_width), lane % (2 * key_width)
    parts = []
    for c in range(packed.shape[0]):
        block = packed[c, tokens:, at : at + HEAD_SIZE].astype(f32)
        parts.append(block[b * loss_per : (b + 1) * loss_per])
    return jnp.concatenate(parts, axis=0)


def backward_body(loss_per, heads, group, place, half, other, packed, *refs):
    attention = [refs[3 * j : 3 * j + 3] for j in range(heads)]
    query_grad, key_grad, value_grad, grad = refs[3 * heads :]
    nc = packed.shape[0]
    tokens = key_grad.shape[0]
    loss = loss_per * nc
    key_width = heads * HEAD_SIZE
    score_scale = HEAD_SIZE ** (-0.5)
    ctx_at = place[3]
    cols = half.shape[1]
    grad[:, pl.ds(pl.multiple_of(place[2] * cols, cols), cols)] = half[...].astype(f32)
    grad[:, pl.ds(pl.multiple_of((1 - place[2]) * cols, cols), cols)] = other[...].astype(f32)
    mine_at = pl.multiple_of(ctx_at * loss_per, loss_per)
    for j in range(heads):
        p_own, p_rows, out = attention[j]
        lanes = [slice((j * group + g) * HEAD_SIZE, (j * group + g + 1) * HEAD_SIZE) for g in range(group)]
        d_out = jnp.concatenate([grad[:, s] for s in lanes], axis=0)
        d_half = d_out.astype(bf16)
        delta = jnp.sum(d_out * out[...], axis=1, keepdims=True)
        query = jnp.concatenate(
            [query_of(packed, j * group + g, tokens, loss_per, key_width) for g in range(group)], axis=0
        ).astype(bf16)
        at = key_width + j * HEAD_SIZE
        own_value = packed[ctx_at, 0:tokens, at : at + HEAD_SIZE]
        prob = p_own[...]
        score_grad = (prob * (dot(d_half, own_value, NT) - delta)).astype(bf16)
        k_lanes = slice(j * HEAD_SIZE, (j + 1) * HEAD_SIZE)
        key_grad[:, k_lanes] = (dot(score_grad, query, TN) * score_scale).astype(bf16)
        value_grad[:, k_lanes] = dot(prob.astype(bf16), d_half, TN).astype(bf16)
        key = jnp.concatenate([packed[c, 0:tokens, k_lanes] for c in range(nc)], axis=0)
        value = jnp.concatenate([packed[c, 0:tokens, at : at + HEAD_SIZE] for c in range(nc)], axis=0)
        d_mine = jnp.concatenate([grad[pl.ds(mine_at, loss_per), s] for s in lanes], axis=0)
        out_mine = jnp.concatenate(
            [
                out[pl.ds(pl.multiple_of(g * loss + mine_at, loss_per), loss_per), :]
                for g in range(group)
            ],
            axis=0,
        )
        delta = jnp.sum(d_mine * out_mine, axis=1, keepdims=True)
        d_prob = dot(d_mine.astype(bf16), value, NT)
        score_grad = (p_rows[...] * (d_prob - delta)).astype(bf16)
        result = dot(score_grad, key, NN) * score_scale
        for g in range(group):
            query_grad[:, lanes[g]] = result[g * loss_per : (g + 1) * loss_per].astype(bf16)


def per_device(
    hidden,
    norm_gain,
    head_weight,
    targets,
    loss_rows,
    stretch_of_slot,
    queries,
    key_states,
    attention_values,
    output_weight,
):
    nc = lax.axis_size("ctx")
    nv = lax.axis_size("vocab")
    nz = nc // CORES
    ctx_at = lax.axis_index("ctx")
    vocab_at = lax.axis_index("vocab")
    tokens = hidden.shape[0]
    stretch_len = tokens // 2
    loss = loss_rows.shape[0]
    loss_per = loss // nc
    width = norm_gain.shape[0]
    voc_rows = head_weight.shape[0]
    part_width = hidden.shape[1]
    query_width = queries.shape[1]
    key_width = key_states.shape[1]
    heads = key_width // HEAD_SIZE
    group = query_width // key_width
    block_width = width // nc
    per_vocab = loss // nv
    all_tokens = tokens * nc

    first_id = (vocab_at * nc + ctx_at) * voc_rows
    place = jnp.stack([vocab_at, ctx_at // CORES, ctx_at % CORES, ctx_at, first_id]).astype(jnp.int32)

    slots = stretch_of_slot.shape[0]
    owner = lax.broadcasted_iota(jnp.int32, (loss, 1), 0) // loss_per
    slot = 2 * owner + loss_rows[:, None] // stretch_len
    slot_iota = lax.broadcasted_iota(jnp.int32, (1, slots), 1)
    stretch = jnp.sum(jnp.where(slot == slot_iota, stretch_of_slot[None, :], 0), axis=1, keepdims=True)
    query_pos = stretch * stretch_len + loss_rows[:, None] % stretch_len
    key_pos = (
        stretch_of_slot[:, None] * stretch_len
        + lax.broadcasted_iota(jnp.int32, (1, stretch_len), 1)
    ).reshape(1, all_tokens)
    picked = call(
        functools.partial(pick_body, loss_per),
        shape((2 * loss_per, part_width // 2), bf16),
        [smem(), smem(), hbm()],
        [pltpu.VMEM((tokens, part_width), bf16), pltpu.SemaphoreType.DMA],
    )(place, loss_rows, hidden)
    picked, queries, targets_late = lax.optimization_barrier((picked, queries, targets))
    extra = (query_width // (2 * key_width)) * loss_per
    packed = call(
        functools.partial(pack_body, loss_per),
        shape((tokens + extra, 2 * key_width), bf16),
        [smem(), smem()] + [vmem()] * 3,
        moved=2 * queries.size,
    )(place, loss_rows, queries, key_states, attention_values)
    by_z = picked[None]
    bit = 1
    while bit < nz:
        by_z = jnp.concatenate([by_z, crossed(by_z, bit)], axis=0)
        bit *= 2
    planes = [by_z] + [shifted(by_z, "vocab", s) for s in range(1, nv)]
    if voc_rows % 16:
        local = targets_late - first_id
        is_local = (local >= 0) & (local < voc_rows)
        target_rows = head_weight.at[jnp.clip(local, 0, voc_rows - 1)].get(mode="promise_in_bounds")
        target_rows = jnp.where(is_local[:, None], target_rows, jnp.zeros((), bf16))
        target_rows = target_rows.reshape(loss, nc, block_width).transpose(1, 0, 2)
    else:
        target_rows = pl.pallas_call(
            target_body,
            out_shape=shape((nc, loss, block_width), bf16),
            in_specs=[smem(), vmem(), pl.BlockSpec(memory_space=pl.ANY)],
            out_specs=vmem(),
            scratch_shapes=[
                pltpu.VMEM((loss, 16, width), bf16),
                pltpu.SMEM((2, loss), jnp.int32),
                pltpu.SemaphoreType.DMA((loss,)),
            ],
            compiler_params=pltpu.CompilerParams(vmem_limit_bytes=40 * 2**20),
            cost_estimate=pl.CostEstimate(
                flops=0, bytes_accessed=2 * 16 * loss * width, transcendentals=0
            ),
        )(place, targets_late.reshape(1, loss), head_weight)
    by_plane = jnp.stack(planes)
    other = swapped(by_plane)
    other, packed, target_rows = lax.optimization_barrier((other, packed, target_rows))
    target_rows = lax.psum_scatter(
        target_rows.reshape(nc * loss, block_width), "ctx", scatter_dimension=0, tiled=True
    )
    packed_all = lax.all_gather(packed, "ctx")

    first = voc_rows % CHUNK
    if voc_rows < SLOTS * CHUNK or first % 16 or not first:
        first = voc_rows if voc_rows < SLOTS * CHUNK else CHUNK
    chunks = (voc_rows - first) // CHUNK
    gain = norm_gain.reshape(1, width)
    keep, send, stats, unit = pl.pallas_call(
        functools.partial(flash_body, first),
        out_shape=(
            shape((nz, loss, block_width), f32),
            shape((loss, nz * block_width + LANES), bf16),
            shape((loss, LANES), f32),
            shape((per_vocab, block_width), f32),
        ),
        in_specs=[smem()] + [vmem()] * 4 + [pl.BlockSpec(memory_space=pl.ANY)],
        out_specs=[vmem()] * 4,
        scratch_shapes=[
            pltpu.VMEM((loss, width), bf16),
            pltpu.VMEM((loss, width), bf16),
            pltpu.VMEM((nc, loss, block_width), f32),
            pltpu.VMEM((loss, CHUNK), bf16),
            pltpu.VMEM((loss, LANES), f32),
            pltpu.VMEM((first, width), bf16),
            pltpu.VMEM((SLOTS if chunks else 1, CHUNK if chunks else 16, width), bf16),
            pltpu.SemaphoreType.DMA,
            pltpu.SemaphoreType.DMA((SLOTS,)),
        ],
        compiler_params=pltpu.CompilerParams(vmem_limit_bytes=50 * 2**20),
        cost_estimate=pl.CostEstimate(
            flops=4 * max(loss, 256) * width * voc_rows,
            bytes_accessed=4 * width * voc_rows,
            transcendentals=loss * voc_rows,
        ),
    )(place, by_plane, other, gain, targets.reshape(loss, 1), head_weight)

    got = swapped(send)
    stats, keep, target_rows, *sends = call(
        functools.partial(core_body, nv - 1),
        (
            shape((per_vocab, LANES), f32),
            shape((nz, per_vocab, block_width), f32),
            shape((per_vocab, block_width), bf16),
        )
        + (shape((per_vocab, (nz + 1) * block_width + LANES), bf16),) * (nv - 1),
        [smem()] + [vmem()] * 3 + [hbm()],
        [
            pltpu.VMEM((nz, loss, block_width), f32),
            pltpu.VMEM((loss, LANES), f32),
            pltpu.VMEM((loss, LANES), bf16),
            pltpu.VMEM((loss, block_width), bf16),
            pltpu.SemaphoreType.DMA,
        ],
    )(place, keep, got, stats, target_rows)
    got = [shifted(sends[s - 1], "vocab", s) for s in range(1, nv)]

    at_once = max(1, min(group, (4 * 2**20) // (loss * all_tokens * 4)))

    def forward(j, query_pos):
        return call(
            functools.partial(forward_body, loss_per, heads, group, at_once, j),
            (
                shape((group * loss, tokens), f32),
                shape((group * loss_per, all_tokens), f32),
                shape((group * loss, HEAD_SIZE), f32),
            ),
            [smem()] + [vmem()] * 3,
            [pltpu.VMEM((at_once * loss, all_tokens), f32)],
            limit=40,
            flops=24 * group * loss * all_tokens * HEAD_SIZE,
            moved=2 * packed_all.size,
            exps=group * loss * all_tokens,
        )(place, key_pos, query_pos, packed_all)

    stats, keep, target_rows, *sends = call(
        functools.partial(plane_body, nv - 1),
        (
            shape((per_vocab, LANES), f32),
            shape((per_vocab, block_width), f32),
            shape((per_vocab, block_width), bf16),
        )
        + (shape((per_vocab, block_width + LANES), bf16),) * (nz - 1),
        [smem()] + [vmem()] * (3 + nv - 1),
        [pltpu.VMEM((nz, per_vocab, block_width), f32)],
    )(place, keep, stats, target_rows, *got)
    got = [shifted(sends[s - 1], "ctx", s, CORES) for s in range(1, nz)]
    stats, query_pos = lax.optimization_barrier((stats, query_pos))
    attention = [forward(j, query_pos) for j in range(heads // 2)]
    stats, attention = lax.optimization_barrier((stats, attention))
    message = call(
        functools.partial(line_body, nz - 1, width),
        shape((per_vocab, block_width + LANES), bf16),
        [smem()] + [vmem()] * (5 + nz - 1),
    )(place, keep, stats, target_rows, unit, gain, *got)

    gathered = [message] + [shifted(message, "vocab", s) for s in range(1, nv)]
    cols = query_width // CORES
    resid_rows, mean_loss, keep, send = call(
        functools.partial(project_body, nv),
        (
            shape((loss, block_width), bf16),
            shape((1, 1), f32),
            shape((loss, cols), f32),
            shape((loss, cols), bf16),
        ),
        [smem()] + [vmem()] * nv + [hbm()],
        [
            pltpu.VMEM((loss, block_width), bf16),
            pltpu.VMEM((loss, query_width), f32),
            pltpu.VMEM((4, query_width // 4, block_width), bf16),
            pltpu.SemaphoreType.DMA((4,)),
        ],
    )(place, *gathered, output_weight)
    half = call(sum_body, shape((loss, cols), bf16), [vmem()] * 2)(keep, swapped(send))
    bit = 1
    while bit < nz:
        got = crossed(half, bit)
        if 2 * bit == nz:
            half, query_pos = lax.optimization_barrier((half, query_pos))
            attention += [forward(j, query_pos) for j in range(heads // 2, heads)]
            half, attention = lax.optimization_barrier((half, attention))
        half = call(sum_body, shape((loss, cols), bf16), [vmem()] * 2)(half, got)
        bit *= 2
    other = swapped(half)
    query_grad, key_grad, value_grad = call(
        functools.partial(backward_body, loss_per, heads, group),
        (
            shape((loss_per, query_width), bf16),
            shape((tokens, key_width), bf16),
            shape((tokens, key_width), bf16),
        ),
        [smem()] + [vmem()] * (3 + 3 * heads),
        [pltpu.VMEM((loss, query_width), f32)],
    )(place, half, other, packed_all, *jax.tree.leaves(attention))
    return (mean_loss.reshape(()), query_grad, key_grad, value_grad, resid_rows.T)


def solution(mesh):
    placed = (
        P("ctx", "vocab"),
        P(),
        P(("vocab", "ctx"), None),
        P(),
        P(),
        P(),
        P("ctx", "vocab"),
        P("ctx", "vocab"),
        P("ctx", "vocab"),
        P("vocab", "ctx"),
    )
    return jax.shard_map(
        per_device,
        mesh=mesh,
        in_specs=placed,
        out_specs=(P(), P("ctx", "vocab"), P("ctx", "vocab"), P("ctx", "vocab"), P("ctx", None)),
        check_vma=False,
    )
```

```python
import functools

import jax
import jax.numpy as jnp
from jax import lax
from jax.experimental import pallas as pl
from jax.experimental.pallas import tpu as pltpu
from jax.sharding import PartitionSpec as P

HEAD_SIZE = 128
CORES = 2
CHUNK = 512
SLOTS = 4
LANES = 128

norm_eps = 1e-06
grad_weight = 16.0
masked_fill = -1e30

f32 = jnp.float32
bf16 = jnp.bfloat16

NT = (((1,), (1,)), ((), ()))
NN = (((1,), (0,)), ((), ()))
TN = (((0,), (0,)), ((), ()))


def dot(a, b, dims):
    return lax.dot_general(a, b, dims, preferred_element_type=f32)


def smem():
    return pl.BlockSpec(memory_space=pltpu.SMEM)


def hbm():
    return pl.BlockSpec(memory_space=pltpu.HBM)


def vmem():
    return pl.BlockSpec(memory_space=pltpu.VMEM)


def shape(dims, dtype):
    return jax.ShapeDtypeStruct(dims, dtype)


def call(body, outs, ins, scratch=(), limit=16, flops=0, moved=0, exps=0):
    return pl.pallas_call(
        body,
        out_shape=outs,
        in_specs=ins,
        out_specs=jax.tree.map(lambda _: vmem(), outs),
        scratch_shapes=list(scratch),
        compiler_params=pltpu.CompilerParams(vmem_limit_bytes=limit * 2**20),
        cost_estimate=pl.CostEstimate(flops=flops, bytes_accessed=moved, transcendentals=exps),
    )


def shifted(value, axis, step, inner=1):
    size = lax.axis_size(axis)
    outer = size // inner
    pairs = [(i, ((i // inner + step) % outer) * inner + i % inner) for i in range(size)]
    return lax.ppermute(value, axis, pairs)


def crossed(value, bit):
    size = lax.axis_size("ctx")
    return lax.ppermute(value, "ctx", [(i, i ^ (bit * CORES)) for i in range(size)])


def swapped(value):
    size = lax.axis_size("ctx")
    return lax.ppermute(value, "ctx", [(i, i ^ 1) for i in range(size)])


def row_choice(loss_per, tokens, place, rows):
    base = place[3] * loss_per
    row_iota = lax.broadcasted_iota(jnp.int32, (loss_per, tokens), 0)
    col_iota = lax.broadcasted_iota(jnp.int32, (loss_per, tokens), 1)
    sel = jnp.zeros((loss_per, tokens), f32)
    for j in range(loss_per):
        sel = jnp.where((row_iota == j) & (col_iota == rows[base + j]), 1.0, sel)
    return sel.astype(bf16)


def pick_body(loss_per, place, rows, hidden, picked, here, sem):
    tokens, width = hidden.shape
    copy = pltpu.make_async_copy(hidden, here, sem)
    copy.start()
    choice = row_choice(loss_per, tokens, place, rows)
    copy.wait()
    mine = dot(choice, here[...], NN)
    half = width // 2
    picked[...] = jnp.concatenate([mine[:, :half], mine[:, half:]], axis=0).astype(bf16)


def pack_body(loss_per, place, rows, queries, keys, values, packed):
    tokens, key_width = keys.shape
    mine = dot(row_choice(loss_per, tokens, place, rows), queries[...], NN)
    packed[0:tokens, 0:key_width] = keys[...]
    packed[0:tokens, key_width : 2 * key_width] = values[...]
    parts = queries.shape[1] // (2 * key_width)
    stacked = [mine[:, b * 2 * key_width : (b + 1) * 2 * key_width] for b in range(parts)]
    packed[tokens : tokens + parts * loss_per, :] = jnp.concatenate(stacked, axis=0).astype(bf16)


def target_body(place, targets, weight, out, buf, spots, sems):
    blocks, loss, block_width = out.shape
    width = blocks * block_width
    total_rows = weight.shape[0]
    offset = targets[...] - place[4]
    local = (offset >= 0) & (offset < total_rows)
    offset = offset.astype(f32)
    index = lax.broadcasted_iota(jnp.int32, (1, loss), 1).astype(f32)
    none = float(loss)
    count = jnp.sum(jnp.where(local, 1.0, 0.0)).astype(jnp.int32)

    def copy(k, at):
        start = pl.multiple_of(lax.div(at, 16) * 16, 16)
        return pltpu.make_async_copy(weight.at[pl.ds(start, 16), :], buf.at[k], sems.at[k])

    def begin(k, left):
        spot = jnp.min(left)
        at = jnp.sum(jnp.where(index == spot, offset, 0.0)).astype(jnp.int32)
        spots[0, k] = spot.astype(jnp.int32)
        spots[1, k] = at
        copy(k, at).start()
        return jnp.where(index == spot, none, left)

    lax.fori_loop(0, count, begin, jnp.where(local, index, none))
    out[...] = jnp.zeros_like(out)
    line = lax.broadcasted_iota(jnp.int32, (16, block_width), 0)

    @pl.loop(0, count)
    def _(k):
        spot, at = spots[0, k], spots[1, k]
        copy(k, at).wait()
        group = pl.ds(pl.multiple_of(lax.div(spot, 16) * 16, 16), 16)
        for b in range(blocks):
            block = buf[k, :, b * block_width : (b + 1) * block_width].astype(f32)
            row = jnp.sum(jnp.where(line == lax.rem(at, 16), block, 0.0), axis=0, keepdims=True)
            before = out[b, group, :].astype(f32)
            out[b, group, :] = jnp.where(line == lax.rem(spot, 16), row, before).astype(bf16)


def flash_body(
    first,
    place,
    own,
    other,
    gain,
    targets,
    weight,
    keep,
    send,
    stats,
    unit,
    normed,
    raw,
    acc,
    probs,
    fresh,
    state,
    head_buf,
    buf,
    head_sem,
    sems,
):
    vocab_at, z_at, core_at, ctx_at, first_id = (place[k] for k in range(5))
    nv, nz = own.shape[0], own.shape[1]
    loss, width = normed.shape
    half = own.shape[3]
    total_rows = weight.shape[0]
    chunks = (total_rows - first) // CHUNK
    blocks = acc.shape[0]
    block_width = width // blocks

    def head_copy():
        return pltpu.make_async_copy(weight.at[pl.ds(0, first), :], head_buf, head_sem)

    def body_copy(c):
        slot = lax.rem(c, SLOTS)
        start = pl.multiple_of(first + c * CHUNK, 16)
        return pltpu.make_async_copy(
            weight.at[pl.ds(start, CHUNK), :], buf.at[slot], sems.at[slot]
        )

    head_copy().start()
    for c in range(min(SLOTS, chunks)):
        body_copy(c).start()

    is_even = core_at == 0
    for zr in range(nz):
        z_src = lax.rem(z_at - zr + nz, nz)
        square_own = jnp.zeros((8, 1), f32)
        square_other = jnp.zeros((8, 1), f32)
        for vr in range(nv):
            a = own[vr, zr].astype(f32)
            b = other[vr, zr].astype(f32)
            square_a = jnp.sum(a * a, axis=1, keepdims=True)
            square_b = jnp.sum(b * b, axis=1, keepdims=True)
            square_own += square_a[:8] + square_a[8:]
            square_other += square_b[:8] + square_b[8:]
        square = jnp.concatenate(
            [
                jnp.where(is_even, square_own, square_other),
                jnp.where(is_even, square_other, square_own),
            ],
            axis=0,
        )
        inv = lax.rsqrt(square / width + norm_eps)
        row_at = pl.multiple_of(z_src * 16, 16)
        state[pl.ds(row_at, 16), :] = jnp.broadcast_to(inv, (16, LANES))
        for vr in range(nv):
            v_src = lax.rem(vocab_at - vr + nv, nv)
            a = own[vr, zr].astype(f32)
            b = other[vr, zr].astype(f32)
            low = jnp.where(is_even, a, b)
            high = jnp.where(is_even, b, a)
            for k in range(2):
                x = jnp.concatenate([low[8 * k : 8 * k + 8], high[8 * k : 8 * k + 8]], axis=0)
                lane_at = pl.multiple_of((v_src * 2 + k) * half, half)
                raw[pl.ds(row_at, 16), pl.ds(lane_at, half)] = x.astype(bf16)
                normed[pl.ds(row_at, 16), pl.ds(lane_at, half)] = (
                    x * inv * gain[:, pl.ds(lane_at, half)]
                ).astype(bf16)

    per_vocab = loss // nv
    mine_at = pl.multiple_of(vocab_at * per_vocab, per_vocab)
    feature_at = pl.multiple_of(ctx_at * block_width, block_width)
    unit[...] = (
        raw[pl.ds(mine_at, per_vocab), pl.ds(feature_at, block_width)].astype(f32)
        * state[pl.ds(mine_at, per_vocab), 0:1]
    )

    target_col = targets[...]

    def softmax(scores, base, before):
        cols = scores.shape[1]
        ids = base + lax.broadcasted_iota(jnp.int32, (loss, cols), 1)
        hit = ids == target_col
        top = jnp.max(scores, axis=1, keepdims=True)
        if before is not None:
            top = jnp.maximum(top, before[0])
        shifted_scores = scores - top
        weights = jnp.exp(shifted_scores)
        total = jnp.sum(weights, axis=1, keepdims=True)
        moment = jnp.sum(weights * shifted_scores, axis=1, keepdims=True)
        logit = jnp.sum(jnp.where(hit, scores, 0.0), axis=1, keepdims=True)
        scale = None
        if before is not None:
            gap = before[0] - top
            scale = jnp.exp(gap)
            total = total + before[1] * scale
            moment = moment + scale * (before[2] + gap * before[1])
            logit = logit + before[3]
        masked = jnp.where(hit, 0.0, weights).astype(bf16)
        return masked, scale, (top, total, moment, logit)

    def scores_of(block):
        return dot(block, normed[...], NT).T

    def add_product(p, scale, read):
        for b in range(blocks):
            part = dot(p, read(b * block_width, block_width), NN)
            if scale is None:
                acc[b] = part
            else:
                acc[b] = acc[b] * scale + part

    def part(ref, slot):
        return lambda at, n: ref[slot, :, at : at + n]

    head_copy().wait()
    p, _, run = softmax(scores_of(head_buf[...]), first_id, None)
    if not chunks:
        add_product(p, None, lambda at, n: head_buf[:, at : at + n])
    else:
        def start_of(c):
            return first_id + first + c * CHUNK

        body_copy(0).wait()
        fresh[...] = scores_of(buf[0])
        add_product(p, None, lambda at, n: head_buf[:, at : at + n])
        body_copy(1).wait()
        scores = scores_of(buf[1])
        p, scale, run = softmax(fresh[...], start_of(0), run)
        probs[...] = p
        fresh[...] = scores

        def step(c, carry):
            scale, run = carry
            body_copy(c).wait()
            scores = scores_of(buf[lax.rem(c, SLOTS)])
            p, next_scale, run = softmax(fresh[...], start_of(c - 1), run)
            add_product(probs[...], scale, part(buf, lax.rem(c - 2, SLOTS)))
            probs[...] = p
            fresh[...] = scores

            @pl.when(c + 2 < chunks)
            def _():
                body_copy(c + 2).start()

            return next_scale, run

        scale, run = lax.fori_loop(2, chunks, step, (scale, run))
        p, next_scale, run = softmax(fresh[...], start_of(chunks - 1), run)
        add_product(probs[...], scale, part(buf, (chunks - 2) % SLOTS))
        add_product(p, next_scale, part(buf, (chunks - 1) % SLOTS))

    for z in range(nz):
        keep[z] = acc[CORES * z + core_at]
        send[:, z * block_width : (z + 1) * block_width] = acc[CORES * z + 1 - core_at].astype(bf16)
    send[:, nz * block_width :] = split_columns(run)
    stats[...] = with_stats(state[...], run)


def split_columns(columns):
    rows = columns[0].shape[0]
    lane = lax.broadcasted_iota(jnp.int32, (rows, LANES), 1)
    table = jnp.zeros((rows, LANES), f32)
    for k, column in enumerate(columns):
        rest = column
        for j in range(3):
            term = rest.astype(bf16).astype(f32)
            table = jnp.where(lane == 3 * k + j, term, table)
            rest = rest - term
    return table.astype(bf16)


def joined_columns(block, count):
    block = block.astype(f32)
    return [
        block[:, 3 * k : 3 * k + 1] + block[:, 3 * k + 1 : 3 * k + 2] + block[:, 3 * k + 2 : 3 * k + 3]
        for k in range(count)
    ]


def stats_of(table):
    return [table[:, k : k + 1] for k in range(4)]


def merge_stats(columns):
    top = functools.reduce(jnp.maximum, [c[0] for c in columns])
    gaps = [c[0] - top for c in columns]
    scales = [jnp.exp(g) for g in gaps]
    total = sum(s * c[1] for s, c in zip(scales, columns))
    moment = sum(s * (c[2] + g * c[1]) for s, g, c in zip(scales, gaps, columns))
    logit = sum(c[3] for c in columns)
    return scales, (top, total, moment, logit)


def with_stats(table, merged):
    lane = lax.broadcasted_iota(jnp.int32, table.shape, 1)
    for k in range(4):
        table = jnp.where(lane == k, merged[k], table)
    return table


def core_body(count, place, keep, got, mine, target_rows, new_stats, new_keep, new_rows, *rest):
    sends, (total, table, message, rows_here, sem) = rest[:count], rest[count:]
    nz, loss, block = keep.shape
    rows_copy = pltpu.make_async_copy(target_rows, rows_here, sem)
    rows_copy.start()
    columns = [stats_of(mine[...]), joined_columns(got[:, nz * block :], 4)]
    scales, merged = merge_stats(columns)
    table[...] = with_stats(mine[...], merged)
    message[...] = split_columns(merged)
    per = loss // (count + 1)
    for z in range(nz):
        other = got[:, z * block : (z + 1) * block].astype(f32)
        total[z] = keep[z] * scales[0] + other * scales[1]
    at = pl.multiple_of(place[0] * per, per)
    new_stats[...] = table[pl.ds(at, per), :]
    new_keep[...] = total[:, pl.ds(at, per), :]
    for s in range(count):
        to = lax.rem(place[0] + s + 1, count + 1)
        rows = pl.ds(pl.multiple_of(to * per, per), per)
        for z in range(nz):
            sends[s][:, z * block : (z + 1) * block] = total[z, rows, :].astype(bf16)
        sends[s][:, (nz + 1) * block :] = message[rows, :]
    rows_copy.wait()
    for s in range(count):
        to = lax.rem(place[0] + s + 1, count + 1)
        rows = pl.ds(pl.multiple_of(to * per, per), per)
        sends[s][:, nz * block : (nz + 1) * block] = rows_here[rows, :]
    new_rows[...] = rows_here[pl.ds(at, per), :]


def plane_body(count, place, keep, mine, target_rows, *rest):
    got, rest = rest[:count], rest[count:]
    new_stats, new_keep, new_target = rest[:3]
    sends, (total,) = rest[3:-1], rest[-1:]
    nz, per, block = keep.shape
    columns = [stats_of(mine[...])] + [joined_columns(g[:, (nz + 1) * block :], 4) for g in got]
    scales, merged = merge_stats(columns)
    new_stats[...] = with_stats(mine[...], merged)
    message = split_columns(merged)
    for z in range(nz):
        value = keep[z] * scales[0]
        for k in range(count):
            value = value + got[k][:, z * block : (z + 1) * block].astype(f32) * scales[k + 1]
        total[z] = value
    new_keep[...] = total[place[1]]
    rows = target_rows[...].astype(f32)
    for k in range(count):
        rows = rows + got[k][:, nz * block : (nz + 1) * block].astype(f32)
    new_target[...] = rows.astype(bf16)
    for s in range(nz - 1):
        sends[s][:, :block] = total[lax.rem(place[1] + s + 1, nz)].astype(bf16)
        sends[s][:, block:] = message


def line_body(count, width, place, keep, mine, target_rows, unit, gain, *rest):
    got, (message,) = rest[:count], rest[count:]
    per, block = keep.shape
    columns = [stats_of(mine[...])] + [joined_columns(g[:, block:], 4) for g in got]
    scales, (top, total, moment, logit) = merge_stats(columns)
    log_total = top + jnp.log(total)
    value = keep[...] * (scales[0] / total)
    for k in range(count):
        value = value + got[k][:, :block].astype(f32) * (scales[k + 1] / total)
    inner = grad_weight * (moment / total + (top - logit)) / width
    short = jnp.exp(logit - log_total) - 1.0
    inv = mine[:, 4:5]
    grad = grad_weight * (value + short * target_rows[...].astype(f32))
    gain_at = pl.multiple_of(place[3] * block, block)
    scaled = grad * gain[:, pl.ds(gain_at, block)]
    message[:, :block] = (inv * (scaled - unit[...] * inner)).astype(bf16)
    message[:, block:] = split_columns([log_total - logit])


def project_body(nv, place, *refs):
    gathered, refs = refs[:nv], refs[nv:]
    weight, resid, loss_out, keep, send, whole, partial, here, sems = refs
    parts, part, _ = here.shape
    copies = [
        pltpu.make_async_copy(weight.at[pl.ds(k * part, part), :], here.at[k], sems.at[k])
        for k in range(parts)
    ]
    for copy in copies:
        copy.start()
    per = gathered[0].shape[0]
    block = whole.shape[1]
    loss_sum = jnp.zeros((1, 1), f32)
    for v in range(nv):
        src = lax.rem(place[0] - v + nv, nv)
        whole[pl.ds(pl.multiple_of(src * per, per), per), :] = gathered[v][:, :block]
        (column,) = joined_columns(gathered[v][:, block:], 1)
        loss_sum = loss_sum + jnp.sum(column, axis=0, keepdims=True)
    loss_out[...] = loss_sum / (nv * per)
    resid[...] = whole[...]
    for k in range(parts):
        copies[k].wait()
        partial[:, k * part : (k + 1) * part] = dot(whole[...], here[k], NT)
    cols = keep.shape[1]
    keep[...] = partial[:, pl.ds(pl.multiple_of(place[2] * cols, cols), cols)]
    send[...] = partial[:, pl.ds(pl.multiple_of((1 - place[2]) * cols, cols), cols)].astype(bf16)


def sum_body(keep, *refs):
    value = keep[...].astype(f32)
    for ref in refs[:-1]:
        value = value + ref[...].astype(f32)
    refs[-1][...] = value.astype(bf16)


def forward_body(
    loss_per, heads, group, heads_at_once, j, place, key_pos, query_pos, packed, p_own, p_rows, out, scratch
):
    nc = packed.shape[0]
    tokens = p_own.shape[1]
    loss = loss_per * nc
    key_width = heads * HEAD_SIZE
    score_scale = HEAD_SIZE ** (-0.5)
    ctx_at = place[3]
    own_at = pl.multiple_of(ctx_at * tokens, tokens)
    row_at = pl.multiple_of(ctx_at * loss_per, loss_per)
    key = jnp.concatenate(
        [packed[c, 0:tokens, j * HEAD_SIZE : (j + 1) * HEAD_SIZE] for c in range(nc)], axis=0
    )
    at = key_width + j * HEAD_SIZE
    value = jnp.concatenate(
        [packed[c, 0:tokens, at : at + HEAD_SIZE] for c in range(nc)], axis=0
    )
    for g0 in range(0, group, heads_at_once):
        stacked = []
        for g in range(g0, g0 + heads_at_once):
            stacked.append(query_of(packed, j * group + g, tokens, loss_per, key_width))
        query = jnp.concatenate(stacked, axis=0).astype(bf16)
        where_at = jnp.concatenate([query_pos[...]] * heads_at_once, axis=0)
        visible = key_pos[...] <= where_at
        scores = jnp.where(visible, dot(query, key, NT) * score_scale, masked_fill)
        top = jnp.max(scores, axis=1, keepdims=True)
        raw = jnp.where(visible, jnp.exp(scores - top), 0.0)
        prob = raw / jnp.sum(raw, axis=1, keepdims=True)
        scratch[...] = prob
        coarse = prob.astype(bf16)
        fine = (prob - coarse.astype(f32)).astype(bf16)
        first = g0 * loss
        n = heads_at_once * loss
        out[first : first + n, :] = dot(coarse, value, NN) + dot(fine, value, NN)
        p_own[first : first + n, :] = scratch[:, pl.ds(own_at, tokens)]
        for k in range(heads_at_once):
            p_rows[(g0 + k) * loss_per : (g0 + k + 1) * loss_per, :] = scratch[
                pl.ds(pl.multiple_of(k * loss + row_at, loss_per), loss_per), :
            ]


def query_of(packed, head, tokens, loss_per, key_width):
    lane = head * HEAD_SIZE
    b, at = lane // (2 * key_width), lane % (2 * key_width)
    parts = []
    for c in range(packed.shape[0]):
        block = packed[c, tokens:, at : at + HEAD_SIZE].astype(f32)
        parts.append(block[b * loss_per : (b + 1) * loss_per])
    return jnp.concatenate(parts, axis=0)


def backward_body(loss_per, heads, group, place, half, other, packed, *refs):
    attention = [refs[3 * j : 3 * j + 3] for j in range(heads)]
    query_grad, key_grad, value_grad, grad = refs[3 * heads :]
    nc = packed.shape[0]
    tokens = key_grad.shape[0]
    loss = loss_per * nc
    key_width = heads * HEAD_SIZE
    score_scale = HEAD_SIZE ** (-0.5)
    ctx_at = place[3]
    cols = half.shape[1]
    grad[:, pl.ds(pl.multiple_of(place[2] * cols, cols), cols)] = half[...].astype(f32)
    grad[:, pl.ds(pl.multiple_of((1 - place[2]) * cols, cols), cols)] = other[...].astype(f32)
    mine_at = pl.multiple_of(ctx_at * loss_per, loss_per)
    for j in range(heads):
        p_own, p_rows, out = attention[j]
        lanes = [slice((j * group + g) * HEAD_SIZE, (j * group + g + 1) * HEAD_SIZE) for g in range(group)]
        d_out = jnp.concatenate([grad[:, s] for s in lanes], axis=0)
        d_half = d_out.astype(bf16)
        delta = jnp.sum(d_out * out[...], axis=1, keepdims=True)
        query = jnp.concatenate(
            [query_of(packed, j * group + g, tokens, loss_per, key_width) for g in range(group)], axis=0
        ).astype(bf16)
        at = key_width + j * HEAD_SIZE
        own_value = packed[ctx_at, 0:tokens, at : at + HEAD_SIZE]
        prob = p_own[...]
        score_grad = (prob * (dot(d_half, own_value, NT) - delta)).astype(bf16)
        k_lanes = slice(j * HEAD_SIZE, (j + 1) * HEAD_SIZE)
        key_grad[:, k_lanes] = (dot(score_grad, query, TN) * score_scale).astype(bf16)
        value_grad[:, k_lanes] = dot(prob.astype(bf16), d_half, TN).astype(bf16)
        key = jnp.concatenate([packed[c, 0:tokens, k_lanes] for c in range(nc)], axis=0)
        value = jnp.concatenate([packed[c, 0:tokens, at : at + HEAD_SIZE] for c in range(nc)], axis=0)
        d_mine = jnp.concatenate([grad[pl.ds(mine_at, loss_per), s] for s in lanes], axis=0)
        out_mine = jnp.concatenate(
            [
                out[pl.ds(pl.multiple_of(g * loss + mine_at, loss_per), loss_per), :]
                for g in range(group)
            ],
            axis=0,
        )
        delta = jnp.sum(d_mine * out_mine, axis=1, keepdims=True)
        d_prob = dot(d_mine.astype(bf16), value, NT)
        score_grad = (p_rows[...] * (d_prob - delta)).astype(bf16)
        result = dot(score_grad, key, NN) * score_scale
        for g in range(group):
            query_grad[:, lanes[g]] = result[g * loss_per : (g + 1) * loss_per].astype(bf16)


def per_device(
    hidden,
    norm_gain,
    head_weight,
    targets,
    loss_rows,
    stretch_of_slot,
    queries,
    key_states,
    attention_values,
    output_weight,
):
    nc = lax.axis_size("ctx")
    nv = lax.axis_size("vocab")
    nz = nc // CORES
    ctx_at = lax.axis_index("ctx")
    vocab_at = lax.axis_index("vocab")
    tokens = hidden.shape[0]
    stretch_len = tokens // 2
    loss = loss_rows.shape[0]
    loss_per = loss // nc
    width = norm_gain.shape[0]
    voc_rows = head_weight.shape[0]
    part_width = hidden.shape[1]
    query_width = queries.shape[1]
    key_width = key_states.shape[1]
    heads = key_width // HEAD_SIZE
    group = query_width // key_width
    block_width = width // nc
    per_vocab = loss // nv
    all_tokens = tokens * nc

    first_id = (vocab_at * nc + ctx_at) * voc_rows
    place = jnp.stack([vocab_at, ctx_at // CORES, ctx_at % CORES, ctx_at, first_id]).astype(jnp.int32)

    slots = stretch_of_slot.shape[0]
    owner = lax.broadcasted_iota(jnp.int32, (loss, 1), 0) // loss_per
    slot = 2 * owner + loss_rows[:, None] // stretch_len
    slot_iota = lax.broadcasted_iota(jnp.int32, (1, slots), 1)
    stretch = jnp.sum(jnp.where(slot == slot_iota, stretch_of_slot[None, :], 0), axis=1, keepdims=True)
    query_pos = stretch * stretch_len + loss_rows[:, None] % stretch_len
    key_pos = (
        stretch_of_slot[:, None] * stretch_len
        + lax.broadcasted_iota(jnp.int32, (1, stretch_len), 1)
    ).reshape(1, all_tokens)
    picked = call(
        functools.partial(pick_body, loss_per),
        shape((2 * loss_per, part_width // 2), bf16),
        [smem(), smem(), hbm()],
        [pltpu.VMEM((tokens, part_width), bf16), pltpu.SemaphoreType.DMA],
    )(place, loss_rows, hidden)
    picked, queries, targets_late = lax.optimization_barrier((picked, queries, targets))
    extra = (query_width // (2 * key_width)) * loss_per
    packed = call(
        functools.partial(pack_body, loss_per),
        shape((tokens + extra, 2 * key_width), bf16),
        [smem(), smem()] + [vmem()] * 3,
        moved=2 * queries.size,
    )(place, loss_rows, queries, key_states, attention_values)
    by_z = jnp.stack([picked] + [shifted(picked, "ctx", s, CORES) for s in range(1, nz)])
    planes = [by_z] + [shifted(by_z, "vocab", s) for s in range(1, nv)]
    if voc_rows % 16:
        local = targets_late - first_id
        is_local = (local >= 0) & (local < voc_rows)
        target_rows = head_weight.at[jnp.clip(local, 0, voc_rows - 1)].get(mode="promise_in_bounds")
        target_rows = jnp.where(is_local[:, None], target_rows, jnp.zeros((), bf16))
        target_rows = target_rows.reshape(loss, nc, block_width).transpose(1, 0, 2)
    else:
        target_rows = pl.pallas_call(
            target_body,
            out_shape=shape((nc, loss, block_width), bf16),
            in_specs=[smem(), vmem(), pl.BlockSpec(memory_space=pl.ANY)],
            out_specs=vmem(),
            scratch_shapes=[
                pltpu.VMEM((loss, 16, width), bf16),
                pltpu.SMEM((2, loss), jnp.int32),
                pltpu.SemaphoreType.DMA((loss,)),
            ],
            compiler_params=pltpu.CompilerParams(vmem_limit_bytes=40 * 2**20),
            cost_estimate=pl.CostEstimate(
                flops=0, bytes_accessed=2 * 16 * loss * width, transcendentals=0
            ),
        )(place, targets_late.reshape(1, loss), head_weight)
    planes, target_rows = lax.optimization_barrier((planes, target_rows))
    by_plane = jnp.stack(planes)
    other = swapped(by_plane)
    target_rows = lax.psum_scatter(
        target_rows.reshape(nc * loss, block_width), "ctx", scatter_dimension=0, tiled=True
    )
    other, packed = lax.optimization_barrier((other, packed))
    packed_all = lax.all_gather(packed, "ctx")

    first = voc_rows % CHUNK
    if voc_rows < SLOTS * CHUNK or first % 16 or not first:
        first = voc_rows if voc_rows < SLOTS * CHUNK else CHUNK
    chunks = (voc_rows - first) // CHUNK
    gain = norm_gain.reshape(1, width)
    keep, send, stats, unit = pl.pallas_call(
        functools.partial(flash_body, first),
        out_shape=(
            shape((nz, loss, block_width), f32),
            shape((loss, nz * block_width + LANES), bf16),
            shape((loss, LANES), f32),
            shape((per_vocab, block_width), f32),
        ),
        in_specs=[smem()] + [vmem()] * 4 + [pl.BlockSpec(memory_space=pl.ANY)],
        out_specs=[vmem()] * 4,
        scratch_shapes=[
            pltpu.VMEM((loss, width), bf16),
            pltpu.VMEM((loss, width), bf16),
            pltpu.VMEM((nc, loss, block_width), f32),
            pltpu.VMEM((loss, CHUNK), bf16),
            pltpu.VMEM((loss, CHUNK), f32),
            pltpu.VMEM((loss, LANES), f32),
            pltpu.VMEM((first, width), bf16),
            pltpu.VMEM((SLOTS if chunks else 1, CHUNK if chunks else 16, width), bf16),
            pltpu.SemaphoreType.DMA,
            pltpu.SemaphoreType.DMA((SLOTS,)),
        ],
        compiler_params=pltpu.CompilerParams(vmem_limit_bytes=47 * 2**20),
        cost_estimate=pl.CostEstimate(
            flops=4 * max(loss, 256) * width * voc_rows,
            bytes_accessed=4 * width * voc_rows,
            transcendentals=loss * voc_rows,
        ),
    )(place, by_plane, other, gain, targets.reshape(loss, 1), head_weight)

    send, target_rows = lax.optimization_barrier((send, target_rows))
    got = swapped(send)
    stats, keep, target_rows, *sends = call(
        functools.partial(core_body, nv - 1),
        (
            shape((per_vocab, LANES), f32),
            shape((nz, per_vocab, block_width), f32),
            shape((per_vocab, block_width), bf16),
        )
        + (shape((per_vocab, (nz + 1) * block_width + LANES), bf16),) * (nv - 1),
        [smem()] + [vmem()] * 3 + [hbm()],
        [
            pltpu.VMEM((nz, loss, block_width), f32),
            pltpu.VMEM((loss, LANES), f32),
            pltpu.VMEM((loss, LANES), bf16),
            pltpu.VMEM((loss, block_width), bf16),
            pltpu.SemaphoreType.DMA,
        ],
    )(place, keep, got, stats, target_rows)
    got = [shifted(sends[s - 1], "vocab", s) for s in range(1, nv)]

    at_once = max(1, min(group, (4 * 2**20) // (loss * all_tokens * 4)))

    def forward(j, query_pos):
        return call(
            functools.partial(forward_body, loss_per, heads, group, at_once, j),
            (
                shape((group * loss, tokens), f32),
                shape((group * loss_per, all_tokens), f32),
                shape((group * loss, HEAD_SIZE), f32),
            ),
            [smem()] + [vmem()] * 3,
            [pltpu.VMEM((at_once * loss, all_tokens), f32)],
            limit=40,
            flops=24 * group * loss * all_tokens * HEAD_SIZE,
            moved=2 * packed_all.size,
            exps=group * loss * all_tokens,
        )(place, key_pos, query_pos, packed_all)

    stats, packed_all = lax.optimization_barrier((stats, packed_all))
    stats, keep, target_rows, *sends = call(
        functools.partial(plane_body, nv - 1),
        (
            shape((per_vocab, LANES), f32),
            shape((per_vocab, block_width), f32),
            shape((per_vocab, block_width), bf16),
        )
        + (shape((per_vocab, block_width + LANES), bf16),) * (nz - 1),
        [smem()] + [vmem()] * (3 + nv - 1),
        [pltpu.VMEM((nz, per_vocab, block_width), f32)],
    )(place, keep, stats, target_rows, *got)
    got = [shifted(sends[s - 1], "ctx", s, CORES) for s in range(1, nz)]
    message = call(
        functools.partial(line_body, nz - 1, width),
        shape((per_vocab, block_width + LANES), bf16),
        [smem()] + [vmem()] * (5 + nz - 1),
    )(place, keep, stats, target_rows, unit, gain, *got)

    gathered = [message] + [shifted(message, "vocab", s) for s in range(1, nv)]
    cols = query_width // CORES
    resid_rows, mean_loss, keep, send = call(
        functools.partial(project_body, nv),
        (
            shape((loss, block_width), bf16),
            shape((1, 1), f32),
            shape((loss, cols), f32),
            shape((loss, cols), bf16),
        ),
        [smem()] + [vmem()] * nv + [hbm()],
        [
            pltpu.VMEM((loss, block_width), bf16),
            pltpu.VMEM((loss, query_width), f32),
            pltpu.VMEM((4, query_width // 4, block_width), bf16),
            pltpu.SemaphoreType.DMA((4,)),
        ],
    )(place, *gathered, output_weight)
    half = call(sum_body, shape((loss, cols), bf16), [vmem()] * 2)(keep, swapped(send))
    windows = nz.bit_length() - 1
    attention = [None] * heads
    for k in range(windows):
        got = crossed(half, 2**k)
        here = range(k, heads, windows)
        half, query_pos = lax.optimization_barrier((half, query_pos))
        made = [forward(j, query_pos) for j in here]
        half, made = lax.optimization_barrier((half, made))
        for j, result in zip(here, made):
            attention[j] = result
        half = call(sum_body, shape((loss, cols), bf16), [vmem()] * 2)(half, got)
    other = swapped(half)
    query_grad, key_grad, value_grad = call(
        functools.partial(backward_body, loss_per, heads, group),
        (
            shape((loss_per, query_width), bf16),
            shape((tokens, key_width), bf16),
            shape((tokens, key_width), bf16),
        ),
        [smem()] + [vmem()] * (3 + 3 * heads),
        [pltpu.VMEM((loss, query_width), f32)],
    )(place, half, other, packed_all, *jax.tree.leaves(attention))
    return (mean_loss.reshape(()), query_grad, key_grad, value_grad, resid_rows.T)


def solution(mesh):
    placed = (
        P("ctx", "vocab"),
        P(),
        P(("vocab", "ctx"), None),
        P(),
        P(),
        P(),
        P("ctx", "vocab"),
        P("ctx", "vocab"),
        P("ctx", "vocab"),
        P("vocab", "ctx"),
    )
    return jax.shard_map(
        per_device,
        mesh=mesh,
        in_specs=placed,
        out_specs=(P(), P("ctx", "vocab"), P("ctx", "vocab"), P("ctx", "vocab"), P("ctx", None)),
        check_vma=False,
    )
```

```python
import functools

import jax
import jax.numpy as jnp
from jax import lax
from jax.experimental import pallas as pl
from jax.experimental.pallas import tpu as pltpu
from jax.sharding import PartitionSpec as P

HEAD_SIZE = 128
CORES = 2
CHUNK = 512
SLOTS = 3
LANES = 128

norm_eps = 1e-06
grad_weight = 16.0
masked_fill = -1e30

f32 = jnp.float32
bf16 = jnp.bfloat16

NT = (((1,), (1,)), ((), ()))
NN = (((1,), (0,)), ((), ()))
TN = (((0,), (0,)), ((), ()))


def dot(a, b, dims):
    return lax.dot_general(a, b, dims, preferred_element_type=f32)


def smem():
    return pl.BlockSpec(memory_space=pltpu.SMEM)


def hbm():
    return pl.BlockSpec(memory_space=pltpu.HBM)


def vmem():
    return pl.BlockSpec(memory_space=pltpu.VMEM)


def shape(dims, dtype):
    return jax.ShapeDtypeStruct(dims, dtype)


def call(body, outs, ins, scratch=(), limit=16, flops=0, moved=0, exps=0):
    return pl.pallas_call(
        body,
        out_shape=outs,
        in_specs=ins,
        out_specs=jax.tree.map(lambda _: vmem(), outs),
        scratch_shapes=list(scratch),
        compiler_params=pltpu.CompilerParams(vmem_limit_bytes=limit * 2**20),
        cost_estimate=pl.CostEstimate(flops=flops, bytes_accessed=moved, transcendentals=exps),
    )


def shifted(value, axis, step, inner=1):
    size = lax.axis_size(axis)
    outer = size // inner
    pairs = [(i, ((i // inner + step) % outer) * inner + i % inner) for i in range(size)]
    return lax.ppermute(value, axis, pairs)


def crossed(value, bit):
    size = lax.axis_size("ctx")
    return lax.ppermute(value, "ctx", [(i, i ^ (bit * CORES)) for i in range(size)])


def swapped(value):
    size = lax.axis_size("ctx")
    return lax.ppermute(value, "ctx", [(i, i ^ 1) for i in range(size)])


def row_choice(loss_per, tokens, place, rows):
    base = place[3] * loss_per
    row_iota = lax.broadcasted_iota(jnp.int32, (loss_per, tokens), 0)
    col_iota = lax.broadcasted_iota(jnp.int32, (loss_per, tokens), 1)
    sel = jnp.zeros((loss_per, tokens), f32)
    for j in range(loss_per):
        sel = jnp.where((row_iota == j) & (col_iota == rows[base + j]), 1.0, sel)
    return sel.astype(bf16)


def pick_body(loss_per, place, rows, hidden, picked, here, sem):
    tokens, width = hidden.shape
    copy = pltpu.make_async_copy(hidden, here, sem)
    copy.start()
    choice = row_choice(loss_per, tokens, place, rows)
    copy.wait()
    mine = dot(choice, here[...], NN)
    half = width // 2
    picked[...] = jnp.concatenate([mine[:, :half], mine[:, half:]], axis=0).astype(bf16)


def pack_body(loss_per, place, rows, queries, keys, values, packed):
    tokens, key_width = keys.shape
    mine = dot(row_choice(loss_per, tokens, place, rows), queries[...], NN)
    packed[0:tokens, 0:key_width] = keys[...]
    packed[0:tokens, key_width : 2 * key_width] = values[...]
    parts = queries.shape[1] // (2 * key_width)
    stacked = [mine[:, b * 2 * key_width : (b + 1) * 2 * key_width] for b in range(parts)]
    packed[tokens : tokens + parts * loss_per, :] = jnp.concatenate(stacked, axis=0).astype(bf16)


def target_body(place, targets, weight, out, buf, spots, sems):
    blocks, loss, block_width = out.shape
    width = blocks * block_width
    total_rows = weight.shape[0]
    offset = targets[...] - place[4]
    local = (offset >= 0) & (offset < total_rows)
    offset = offset.astype(f32)
    index = lax.broadcasted_iota(jnp.int32, (1, loss), 1).astype(f32)
    none = float(loss)
    count = jnp.sum(jnp.where(local, 1.0, 0.0)).astype(jnp.int32)

    def copy(k, at):
        start = pl.multiple_of(lax.div(at, 16) * 16, 16)
        return pltpu.make_async_copy(weight.at[pl.ds(start, 16), :], buf.at[k], sems.at[k])

    def begin(k, left):
        spot = jnp.min(left)
        at = jnp.sum(jnp.where(index == spot, offset, 0.0)).astype(jnp.int32)
        spots[0, k] = spot.astype(jnp.int32)
        spots[1, k] = at
        copy(k, at).start()
        return jnp.where(index == spot, none, left)

    lax.fori_loop(0, count, begin, jnp.where(local, index, none))
    out[...] = jnp.zeros_like(out)
    line = lax.broadcasted_iota(jnp.int32, (16, block_width), 0)

    @pl.loop(0, count)
    def _(k):
        spot, at = spots[0, k], spots[1, k]
        copy(k, at).wait()
        group = pl.ds(pl.multiple_of(lax.div(spot, 16) * 16, 16), 16)
        for b in range(blocks):
            block = buf[k, :, b * block_width : (b + 1) * block_width].astype(f32)
            row = jnp.sum(jnp.where(line == lax.rem(at, 16), block, 0.0), axis=0, keepdims=True)
            before = out[b, group, :].astype(f32)
            out[b, group, :] = jnp.where(line == lax.rem(spot, 16), row, before).astype(bf16)


def flash_body(
    first,
    place,
    own,
    other,
    gain,
    targets,
    weight,
    keep,
    send,
    stats,
    unit,
    normed,
    raw,
    acc,
    probs,
    state,
    head_buf,
    buf,
    head_sem,
    sems,
):
    vocab_at, z_at, core_at, ctx_at, first_id = (place[k] for k in range(5))
    nv, nz = own.shape[0], own.shape[1]
    loss, width = normed.shape
    half = own.shape[3]
    total_rows = weight.shape[0]
    chunks = (total_rows - first) // CHUNK
    blocks = acc.shape[0]
    block_width = width // blocks

    def head_copy():
        return pltpu.make_async_copy(weight.at[pl.ds(0, first), :], head_buf, head_sem)

    def body_copy(c):
        slot = lax.rem(c, SLOTS)
        start = pl.multiple_of(first + c * CHUNK, 16)
        return pltpu.make_async_copy(
            weight.at[pl.ds(start, CHUNK), :], buf.at[slot], sems.at[slot]
        )

    head_copy().start()
    def half_copy(k):
        piece = CHUNK // 2
        return pltpu.make_async_copy(
            weight.at[pl.ds(first + k * piece, piece), :],
            buf.at[0, pl.ds(k * piece, piece), :],
            (sems.at[0], sems.at[SLOTS])[k],
        )

    if chunks:
        half_copy(0).start()
        half_copy(1).start()
        for c in range(1, min(SLOTS, chunks)):
            body_copy(c).start()

    is_even = core_at == 0
    for zr in range(nz):
        z_src = lax.rem(z_at - zr + nz, nz)
        square_own = jnp.zeros((8, 1), f32)
        square_other = jnp.zeros((8, 1), f32)
        for vr in range(nv):
            a = own[vr, zr].astype(f32)
            b = other[vr, zr].astype(f32)
            square_a = jnp.sum(a * a, axis=1, keepdims=True)
            square_b = jnp.sum(b * b, axis=1, keepdims=True)
            square_own += square_a[:8] + square_a[8:]
            square_other += square_b[:8] + square_b[8:]
        square = jnp.concatenate(
            [
                jnp.where(is_even, square_own, square_other),
                jnp.where(is_even, square_other, square_own),
            ],
            axis=0,
        )
        inv = lax.rsqrt(square / width + norm_eps)
        row_at = pl.multiple_of(z_src * 16, 16)
        state[pl.ds(row_at, 16), :] = jnp.broadcast_to(inv, (16, LANES))
        for vr in range(nv):
            v_src = lax.rem(vocab_at - vr + nv, nv)
            a = own[vr, zr].astype(f32)
            b = other[vr, zr].astype(f32)
            low = jnp.where(is_even, a, b)
            high = jnp.where(is_even, b, a)
            for k in range(2):
                x = jnp.concatenate([low[8 * k : 8 * k + 8], high[8 * k : 8 * k + 8]], axis=0)
                lane_at = pl.multiple_of((v_src * 2 + k) * half, half)
                raw[pl.ds(row_at, 16), pl.ds(lane_at, half)] = x.astype(bf16)
                normed[pl.ds(row_at, 16), pl.ds(lane_at, half)] = (
                    x * inv * gain[:, pl.ds(lane_at, half)]
                ).astype(bf16)

    per_vocab = loss // nv
    mine_at = pl.multiple_of(vocab_at * per_vocab, per_vocab)
    feature_at = pl.multiple_of(ctx_at * block_width, block_width)
    unit[...] = (
        raw[pl.ds(mine_at, per_vocab), pl.ds(feature_at, block_width)].astype(f32)
        * state[pl.ds(mine_at, per_vocab), 0:1]
    )

    target_col = targets[...]

    def softmax(scores, base, before):
        cols = scores.shape[1]
        ids = base + lax.broadcasted_iota(jnp.int32, (loss, cols), 1)
        hit = ids == target_col
        top = jnp.max(scores, axis=1, keepdims=True)
        if before is not None:
            top = jnp.maximum(top, before[0])
        shifted_scores = scores - top
        weights = jnp.exp(shifted_scores)
        total = jnp.sum(weights, axis=1, keepdims=True)
        moment = jnp.sum(weights * shifted_scores, axis=1, keepdims=True)
        logit = jnp.sum(jnp.where(hit, scores, 0.0), axis=1, keepdims=True)
        scale = None
        if before is not None:
            gap = before[0] - top
            scale = jnp.exp(gap)
            total = total + before[1] * scale
            moment = moment + scale * (before[2] + gap * before[1])
            logit = logit + before[3]
        masked = jnp.where(hit, 0.0, weights).astype(bf16)
        return masked, scale, (top, total, moment, logit)

    def scores_of(block):
        return dot(block, normed[...], NT).T

    def add_product(p, scale, read):
        for b in range(blocks):
            part = dot(p, read(b * block_width, block_width), NN)
            if scale is None:
                acc[b] = part
            else:
                acc[b] = acc[b] * scale + part

    def part(ref, slot):
        return lambda at, n: ref[slot, :, at : at + n]

    head_copy().wait()
    p, _, run = softmax(scores_of(head_buf[...]), first_id, None)
    if not chunks:
        add_product(p, None, lambda at, n: head_buf[:, at : at + n])
    else:
        def start_of(c):
            return first_id + first + c * CHUNK

        piece = CHUNK // 2
        low, high = buf.at[0, pl.ds(0, piece), :], buf.at[0, pl.ds(piece, piece), :]
        half_copy(0).wait()
        scores = scores_of(low[...])
        add_product(p, None, lambda at, n: head_buf[:, at : at + n])
        p, scale, run = softmax(scores, start_of(0), run)
        half_copy(1).wait()
        scores = scores_of(high[...])
        add_product(p, scale, lambda at, n: low[:, at : at + n])
        p, scale, run = softmax(scores, start_of(0) + piece, run)
        body_copy(1).wait()
        scores = scores_of(buf[1])
        add_product(p, scale, lambda at, n: high[:, at : at + n])
        p, scale, run = softmax(scores, start_of(1), run)
        probs[...] = p
        if chunks > SLOTS:
            body_copy(SLOTS).start()

        def step(c, carry):
            scale, run = carry
            body_copy(c).wait()
            scores = scores_of(buf[lax.rem(c, SLOTS)])
            add_product(probs[...], scale, part(buf, lax.rem(c - 1, SLOTS)))
            p, scale, run = softmax(scores, start_of(c), run)
            probs[...] = p

            @pl.when(c + 2 < chunks)
            def _():
                body_copy(c + 2).start()

            return scale, run

        scale, run = lax.fori_loop(2, chunks, step, (scale, run))
        add_product(probs[...], scale, part(buf, (chunks - 1) % SLOTS))

    for z in range(nz):
        keep[z] = acc[CORES * z + core_at]
        send[:, z * block_width : (z + 1) * block_width] = acc[CORES * z + 1 - core_at].astype(bf16)
    send[:, nz * block_width :] = split_columns(run)
    stats[...] = with_stats(state[...], run)


def split_columns(columns):
    rows = columns[0].shape[0]
    lane = lax.broadcasted_iota(jnp.int32, (rows, LANES), 1)
    table = jnp.zeros((rows, LANES), f32)
    for k, column in enumerate(columns):
        rest = column
        for j in range(3):
            term = rest.astype(bf16).astype(f32)
            table = jnp.where(lane == 3 * k + j, term, table)
            rest = rest - term
    return table.astype(bf16)


def joined_columns(block, count):
    block = block.astype(f32)
    return [
        block[:, 3 * k : 3 * k + 1] + block[:, 3 * k + 1 : 3 * k + 2] + block[:, 3 * k + 2 : 3 * k + 3]
        for k in range(count)
    ]


def stats_of(table):
    return [table[:, k : k + 1] for k in range(4)]


def merge_stats(columns):
    top = functools.reduce(jnp.maximum, [c[0] for c in columns])
    gaps = [c[0] - top for c in columns]
    scales = [jnp.exp(g) for g in gaps]
    total = sum(s * c[1] for s, c in zip(scales, columns))
    moment = sum(s * (c[2] + g * c[1]) for s, g, c in zip(scales, gaps, columns))
    logit = sum(c[3] for c in columns)
    return scales, (top, total, moment, logit)


def with_stats(table, merged):
    lane = lax.broadcasted_iota(jnp.int32, table.shape, 1)
    for k in range(4):
        table = jnp.where(lane == k, merged[k], table)
    return table


def core_body(count, place, keep, got, mine, target_rows, new_stats, new_keep, new_rows, *rest):
    sends, (total, table, message, rows_here, sem) = rest[:count], rest[count:]
    nz, loss, block = keep.shape
    rows_copy = pltpu.make_async_copy(target_rows, rows_here, sem)
    rows_copy.start()
    columns = [stats_of(mine[...]), joined_columns(got[:, nz * block :], 4)]
    scales, merged = merge_stats(columns)
    table[...] = with_stats(mine[...], merged)
    message[...] = split_columns(merged)
    per = loss // (count + 1)
    for z in range(nz):
        other = got[:, z * block : (z + 1) * block].astype(f32)
        total[z] = keep[z] * scales[0] + other * scales[1]
    at = pl.multiple_of(place[0] * per, per)
    new_stats[...] = table[pl.ds(at, per), :]
    new_keep[...] = total[:, pl.ds(at, per), :]
    for s in range(count):
        to = lax.rem(place[0] + s + 1, count + 1)
        rows = pl.ds(pl.multiple_of(to * per, per), per)
        for z in range(nz):
            sends[s][:, z * block : (z + 1) * block] = total[z, rows, :].astype(bf16)
        sends[s][:, (nz + 1) * block :] = message[rows, :]
    rows_copy.wait()
    for s in range(count):
        to = lax.rem(place[0] + s + 1, count + 1)
        rows = pl.ds(pl.multiple_of(to * per, per), per)
        sends[s][:, nz * block : (nz + 1) * block] = rows_here[rows, :]
    new_rows[...] = rows_here[pl.ds(at, per), :]


def plane_body(count, place, keep, mine, target_rows, *rest):
    got, rest = rest[:count], rest[count:]
    new_stats, new_keep, new_target = rest[:3]
    sends, (total,) = rest[3:-1], rest[-1:]
    nz, per, block = keep.shape
    columns = [stats_of(mine[...])] + [joined_columns(g[:, (nz + 1) * block :], 4) for g in got]
    scales, merged = merge_stats(columns)
    new_stats[...] = with_stats(mine[...], merged)
    message = split_columns(merged)
    for z in range(nz):
        value = keep[z] * scales[0]
        for k in range(count):
            value = value + got[k][:, z * block : (z + 1) * block].astype(f32) * scales[k + 1]
        total[z] = value
    new_keep[...] = total[place[1]]
    rows = target_rows[...].astype(f32)
    for k in range(count):
        rows = rows + got[k][:, nz * block : (nz + 1) * block].astype(f32)
    new_target[...] = rows.astype(bf16)
    for s in range(nz - 1):
        sends[s][:, :block] = total[lax.rem(place[1] + s + 1, nz)].astype(bf16)
        sends[s][:, block:] = message


def line_body(count, width, place, keep, mine, target_rows, unit, gain, *rest):
    got, (message,) = rest[:count], rest[count:]
    per, block = keep.shape
    columns = [stats_of(mine[...])] + [joined_columns(g[:, block:], 4) for g in got]
    scales, (top, total, moment, logit) = merge_stats(columns)
    log_total = top + jnp.log(total)
    value = keep[...] * (scales[0] / total)
    for k in range(count):
        value = value + got[k][:, :block].astype(f32) * (scales[k + 1] / total)
    inner = grad_weight * (moment / total + (top - logit)) / width
    short = jnp.exp(logit - log_total) - 1.0
    inv = mine[:, 4:5]
    grad = grad_weight * (value + short * target_rows[...].astype(f32))
    gain_at = pl.multiple_of(place[3] * block, block)
    scaled = grad * gain[:, pl.ds(gain_at, block)]
    message[:, :block] = (inv * (scaled - unit[...] * inner)).astype(bf16)
    message[:, block:] = split_columns([log_total - logit])


def project_body(nv, place, *refs):
    gathered, refs = refs[:nv], refs[nv:]
    weight, resid, loss_out, keep, send, whole, partial, here, sems = refs
    parts, part, _ = here.shape
    copies = [
        pltpu.make_async_copy(weight.at[pl.ds(k * part, part), :], here.at[k], sems.at[k])
        for k in range(parts)
    ]
    for copy in copies:
        copy.start()
    per = gathered[0].shape[0]
    block = whole.shape[1]
    loss_sum = jnp.zeros((1, 1), f32)
    for v in range(nv):
        src = lax.rem(place[0] - v + nv, nv)
        whole[pl.ds(pl.multiple_of(src * per, per), per), :] = gathered[v][:, :block]
        (column,) = joined_columns(gathered[v][:, block:], 1)
        loss_sum = loss_sum + jnp.sum(column, axis=0, keepdims=True)
    loss_out[...] = loss_sum / (nv * per)
    resid[...] = whole[...]
    for k in range(parts):
        copies[k].wait()
        partial[:, k * part : (k + 1) * part] = dot(whole[...], here[k], NT)
    cols = keep.shape[1]
    keep[...] = partial[:, pl.ds(pl.multiple_of(place[2] * cols, cols), cols)]
    send[...] = partial[:, pl.ds(pl.multiple_of((1 - place[2]) * cols, cols), cols)].astype(bf16)


def sum_body(keep, *refs):
    value = keep[...].astype(f32)
    for ref in refs[:-1]:
        value = value + ref[...].astype(f32)
    refs[-1][...] = value.astype(bf16)


def forward_body(
    loss_per, heads, group, heads_at_once, j, place, key_pos, query_pos, packed, p_own, p_rows, out, scratch
):
    nc = packed.shape[0]
    tokens = p_own.shape[1]
    loss = loss_per * nc
    key_width = heads * HEAD_SIZE
    score_scale = HEAD_SIZE ** (-0.5)
    ctx_at = place[3]
    own_at = pl.multiple_of(ctx_at * tokens, tokens)
    row_at = pl.multiple_of(ctx_at * loss_per, loss_per)
    key = jnp.concatenate(
        [packed[c, 0:tokens, j * HEAD_SIZE : (j + 1) * HEAD_SIZE] for c in range(nc)], axis=0
    )
    at = key_width + j * HEAD_SIZE
    value = jnp.concatenate(
        [packed[c, 0:tokens, at : at + HEAD_SIZE] for c in range(nc)], axis=0
    )
    for g0 in range(0, group, heads_at_once):
        stacked = []
        for g in range(g0, g0 + heads_at_once):
            stacked.append(query_of(packed, j * group + g, tokens, loss_per, key_width))
        query = jnp.concatenate(stacked, axis=0).astype(bf16)
        where_at = jnp.concatenate([query_pos[...]] * heads_at_once, axis=0)
        visible = key_pos[...] <= where_at
        scores = jnp.where(visible, dot(query, key, NT) * score_scale, masked_fill)
        top = jnp.max(scores, axis=1, keepdims=True)
        raw = jnp.where(visible, jnp.exp(scores - top), 0.0)
        prob = raw / jnp.sum(raw, axis=1, keepdims=True)
        scratch[...] = prob
        coarse = prob.astype(bf16)
        fine = (prob - coarse.astype(f32)).astype(bf16)
        first = g0 * loss
        n = heads_at_once * loss
        out[first : first + n, :] = dot(coarse, value, NN) + dot(fine, value, NN)
        p_own[first : first + n, :] = scratch[:, pl.ds(own_at, tokens)]
        for k in range(heads_at_once):
            p_rows[(g0 + k) * loss_per : (g0 + k + 1) * loss_per, :] = scratch[
                pl.ds(pl.multiple_of(k * loss + row_at, loss_per), loss_per), :
            ]


def query_of(packed, head, tokens, loss_per, key_width):
    lane = head * HEAD_SIZE
    b, at = lane // (2 * key_width), lane % (2 * key_width)
    parts = []
    for c in range(packed.shape[0]):
        block = packed[c, tokens:, at : at + HEAD_SIZE].astype(f32)
        parts.append(block[b * loss_per : (b + 1) * loss_per])
    return jnp.concatenate(parts, axis=0)


def backward_body(loss_per, heads, group, place, half, other, packed, *refs):
    attention = [refs[3 * j : 3 * j + 3] for j in range(heads)]
    query_grad, key_grad, value_grad, grad = refs[3 * heads :]
    nc = packed.shape[0]
    tokens = key_grad.shape[0]
    loss = loss_per * nc
    key_width = heads * HEAD_SIZE
    score_scale = HEAD_SIZE ** (-0.5)
    ctx_at = place[3]
    cols = half.shape[1]
    grad[:, pl.ds(pl.multiple_of(place[2] * cols, cols), cols)] = half[...].astype(f32)
    grad[:, pl.ds(pl.multiple_of((1 - place[2]) * cols, cols), cols)] = other[...].astype(f32)
    mine_at = pl.multiple_of(ctx_at * loss_per, loss_per)
    for j in range(heads):
        p_own, p_rows, out = attention[j]
        lanes = [slice((j * group + g) * HEAD_SIZE, (j * group + g + 1) * HEAD_SIZE) for g in range(group)]
        d_out = jnp.concatenate([grad[:, s] for s in lanes], axis=0)
        d_half = d_out.astype(bf16)
        delta = jnp.sum(d_out * out[...], axis=1, keepdims=True)
        query = jnp.concatenate(
            [query_of(packed, j * group + g, tokens, loss_per, key_width) for g in range(group)], axis=0
        ).astype(bf16)
        at = key_width + j * HEAD_SIZE
        own_value = packed[ctx_at, 0:tokens, at : at + HEAD_SIZE]
        prob = p_own[...]
        score_grad = (prob * (dot(d_half, own_value, NT) - delta)).astype(bf16)
        k_lanes = slice(j * HEAD_SIZE, (j + 1) * HEAD_SIZE)
        key_grad[:, k_lanes] = (dot(score_grad, query, TN) * score_scale).astype(bf16)
        value_grad[:, k_lanes] = dot(prob.astype(bf16), d_half, TN).astype(bf16)
        key = jnp.concatenate([packed[c, 0:tokens, k_lanes] for c in range(nc)], axis=0)
        value = jnp.concatenate([packed[c, 0:tokens, at : at + HEAD_SIZE] for c in range(nc)], axis=0)
        d_mine = jnp.concatenate([grad[pl.ds(mine_at, loss_per), s] for s in lanes], axis=0)
        out_mine = jnp.concatenate(
            [
                out[pl.ds(pl.multiple_of(g * loss + mine_at, loss_per), loss_per), :]
                for g in range(group)
            ],
            axis=0,
        )
        delta = jnp.sum(d_mine * out_mine, axis=1, keepdims=True)
        d_prob = dot(d_mine.astype(bf16), value, NT)
        score_grad = (p_rows[...] * (d_prob - delta)).astype(bf16)
        result = dot(score_grad, key, NN) * score_scale
        for g in range(group):
            query_grad[:, lanes[g]] = result[g * loss_per : (g + 1) * loss_per].astype(bf16)


def per_device(
    hidden,
    norm_gain,
    head_weight,
    targets,
    loss_rows,
    stretch_of_slot,
    queries,
    key_states,
    attention_values,
    output_weight,
):
    nc = lax.axis_size("ctx")
    nv = lax.axis_size("vocab")
    nz = nc // CORES
    ctx_at = lax.axis_index("ctx")
    vocab_at = lax.axis_index("vocab")
    tokens = hidden.shape[0]
    stretch_len = tokens // 2
    loss = loss_rows.shape[0]
    loss_per = loss // nc
    width = norm_gain.shape[0]
    voc_rows = head_weight.shape[0]
    part_width = hidden.shape[1]
    query_width = queries.shape[1]
    key_width = key_states.shape[1]
    heads = key_width // HEAD_SIZE
    group = query_width // key_width
    block_width = width // nc
    per_vocab = loss // nv
    all_tokens = tokens * nc

    first_id = (vocab_at * nc + ctx_at) * voc_rows
    place = jnp.stack([vocab_at, ctx_at // CORES, ctx_at % CORES, ctx_at, first_id]).astype(jnp.int32)

    slots = stretch_of_slot.shape[0]
    owner = lax.broadcasted_iota(jnp.int32, (loss, 1), 0) // loss_per
    slot = 2 * owner + loss_rows[:, None] // stretch_len
    slot_iota = lax.broadcasted_iota(jnp.int32, (1, slots), 1)
    stretch = jnp.sum(jnp.where(slot == slot_iota, stretch_of_slot[None, :], 0), axis=1, keepdims=True)
    query_pos = stretch * stretch_len + loss_rows[:, None] % stretch_len
    key_pos = (
        stretch_of_slot[:, None] * stretch_len
        + lax.broadcasted_iota(jnp.int32, (1, stretch_len), 1)
    ).reshape(1, all_tokens)
    picked = call(
        functools.partial(pick_body, loss_per),
        shape((2 * loss_per, part_width // 2), bf16),
        [smem(), smem(), hbm()],
        [pltpu.VMEM((tokens, part_width), bf16), pltpu.SemaphoreType.DMA],
        limit=56,
    )(place, loss_rows, hidden)
    picked, queries, targets_late = lax.optimization_barrier((picked, queries, targets))
    extra = (query_width // (2 * key_width)) * loss_per
    packed = call(
        functools.partial(pack_body, loss_per),
        shape((tokens + extra, 2 * key_width), bf16),
        [smem(), smem()] + [vmem()] * 3,
        moved=2 * queries.size,
    )(place, loss_rows, queries, key_states, attention_values)
    by_z = jnp.stack([picked] + [shifted(picked, "ctx", s, CORES) for s in range(1, nz)])
    planes = [by_z] + [shifted(by_z, "vocab", s) for s in range(1, nv)]
    if voc_rows % 16:
        local = targets_late - first_id
        is_local = (local >= 0) & (local < voc_rows)
        target_rows = head_weight.at[jnp.clip(local, 0, voc_rows - 1)].get(mode="promise_in_bounds")
        target_rows = jnp.where(is_local[:, None], target_rows, jnp.zeros((), bf16))
        target_rows = target_rows.reshape(loss, nc, block_width).transpose(1, 0, 2)
    else:
        target_rows = pl.pallas_call(
            target_body,
            out_shape=shape((nc, loss, block_width), bf16),
            in_specs=[smem(), vmem(), pl.BlockSpec(memory_space=pl.ANY)],
            out_specs=vmem(),
            scratch_shapes=[
                pltpu.VMEM((loss, 16, width), bf16),
                pltpu.SMEM((2, loss), jnp.int32),
                pltpu.SemaphoreType.DMA((loss,)),
            ],
            compiler_params=pltpu.CompilerParams(vmem_limit_bytes=40 * 2**20),
            cost_estimate=pl.CostEstimate(
                flops=0, bytes_accessed=2 * 16 * loss * width, transcendentals=0
            ),
        )(place, targets_late.reshape(1, loss), head_weight)
    planes, target_rows = lax.optimization_barrier((planes, target_rows))
    by_plane = jnp.stack(planes)
    other = swapped(by_plane)
    target_rows = lax.psum_scatter(
        target_rows.reshape(nc * loss, block_width), "ctx", scatter_dimension=0, tiled=True
    )
    other, packed = lax.optimization_barrier((other, packed))
    packed_all = lax.all_gather(packed, "ctx")

    first = voc_rows % CHUNK
    if voc_rows < SLOTS * CHUNK or first % 16 or not first:
        first = voc_rows if voc_rows < SLOTS * CHUNK else CHUNK
    chunks = (voc_rows - first) // CHUNK
    gain = norm_gain.reshape(1, width)
    keep, send, stats, unit = pl.pallas_call(
        functools.partial(flash_body, first),
        out_shape=(
            shape((nz, loss, block_width), f32),
            shape((loss, nz * block_width + LANES), bf16),
            shape((loss, LANES), f32),
            shape((per_vocab, block_width), f32),
        ),
        in_specs=[smem()] + [vmem()] * 4 + [pl.BlockSpec(memory_space=pl.ANY)],
        out_specs=[vmem()] * 4,
        scratch_shapes=[
            pltpu.VMEM((loss, width), bf16),
            pltpu.VMEM((loss, width), bf16),
            pltpu.VMEM((nc, loss, block_width), f32),
            pltpu.VMEM((loss, CHUNK), bf16),
            pltpu.VMEM((loss, LANES), f32),
            pltpu.VMEM((first, width), bf16),
            pltpu.VMEM((SLOTS if chunks else 1, CHUNK if chunks else 16, width), bf16),
            pltpu.SemaphoreType.DMA,
            pltpu.SemaphoreType.DMA((SLOTS + 1,)),
        ],
        compiler_params=pltpu.CompilerParams(vmem_limit_bytes=47 * 2**20),
        cost_estimate=pl.CostEstimate(
            flops=4 * max(loss, 256) * width * voc_rows,
            bytes_accessed=4 * width * voc_rows,
            transcendentals=loss * voc_rows,
        ),
    )(place, by_plane, other, gain, targets.reshape(loss, 1), head_weight)

    send, target_rows = lax.optimization_barrier((send, target_rows))
    got = swapped(send)
    stats, keep, target_rows, *sends = call(
        functools.partial(core_body, nv - 1),
        (
            shape((per_vocab, LANES), f32),
            shape((nz, per_vocab, block_width), f32),
            shape((per_vocab, block_width), bf16),
        )
        + (shape((per_vocab, (nz + 1) * block_width + LANES), bf16),) * (nv - 1),
        [smem()] + [vmem()] * 3 + [hbm()],
        [
            pltpu.VMEM((nz, loss, block_width), f32),
            pltpu.VMEM((loss, LANES), f32),
            pltpu.VMEM((loss, LANES), bf16),
            pltpu.VMEM((loss, block_width), bf16),
            pltpu.SemaphoreType.DMA,
        ],
    )(place, keep, got, stats, target_rows)
    got = [shifted(sends[s - 1], "vocab", s) for s in range(1, nv)]

    at_once = max(1, min(group, (4 * 2**20) // (loss * all_tokens * 4)))

    def forward(j, query_pos):
        return call(
            functools.partial(forward_body, loss_per, heads, group, at_once, j),
            (
                shape((group * loss, tokens), f32),
                shape((group * loss_per, all_tokens), f32),
                shape((group * loss, HEAD_SIZE), f32),
            ),
            [smem()] + [vmem()] * 3,
            [pltpu.VMEM((at_once * loss, all_tokens), f32)],
            limit=40,
            flops=24 * group * loss * all_tokens * HEAD_SIZE,
            moved=2 * packed_all.size,
            exps=group * loss * all_tokens,
        )(place, key_pos, query_pos, packed_all)

    stats, packed_all = lax.optimization_barrier((stats, packed_all))
    stats, keep, target_rows, *sends = call(
        functools.partial(plane_body, nv - 1),
        (
            shape((per_vocab, LANES), f32),
            shape((per_vocab, block_width), f32),
            shape((per_vocab, block_width), bf16),
        )
        + (shape((per_vocab, block_width + LANES), bf16),) * (nz - 1),
        [smem()] + [vmem()] * (3 + nv - 1),
        [pltpu.VMEM((nz, per_vocab, block_width), f32)],
    )(place, keep, stats, target_rows, *got)
    got = [shifted(sends[s - 1], "ctx", s, CORES) for s in range(1, nz)]
    message = call(
        functools.partial(line_body, nz - 1, width),
        shape((per_vocab, block_width + LANES), bf16),
        [smem()] + [vmem()] * (5 + nz - 1),
    )(place, keep, stats, target_rows, unit, gain, *got)

    gathered = [message] + [shifted(message, "vocab", s) for s in range(1, nv)]
    cols = query_width // CORES
    resid_rows, mean_loss, keep, send = call(
        functools.partial(project_body, nv),
        (
            shape((loss, block_width), bf16),
            shape((1, 1), f32),
            shape((loss, cols), f32),
            shape((loss, cols), bf16),
        ),
        [smem()] + [vmem()] * nv + [hbm()],
        [
            pltpu.VMEM((loss, block_width), bf16),
            pltpu.VMEM((loss, query_width), f32),
            pltpu.VMEM((4, query_width // 4, block_width), bf16),
            pltpu.SemaphoreType.DMA((4,)),
        ],
        limit=52,
    )(place, *gathered, output_weight)
    half = call(sum_body, shape((loss, cols), bf16), [vmem()] * 2)(keep, swapped(send))
    windows = nz.bit_length() - 1
    attention = [None] * heads
    for k in range(windows):
        got = crossed(half, 2**k)
        here = range(k, heads, windows)
        half, query_pos = lax.optimization_barrier((half, query_pos))
        made = [forward(j, query_pos) for j in here]
        half, made = lax.optimization_barrier((half, made))
        for j, result in zip(here, made):
            attention[j] = result
        half = call(sum_body, shape((loss, cols), bf16), [vmem()] * 2)(half, got)
    other = swapped(half)
    query_grad, key_grad, value_grad = call(
        functools.partial(backward_body, loss_per, heads, group),
        (
            shape((loss_per, query_width), bf16),
            shape((tokens, key_width), bf16),
            shape((tokens, key_width), bf16),
        ),
        [smem()] + [vmem()] * (3 + 3 * heads),
        [pltpu.VMEM((loss, query_width), f32)],
    )(place, half, other, packed_all, *jax.tree.leaves(attention))
    return (mean_loss.reshape(()), query_grad, key_grad, value_grad, resid_rows.T)


def solution(mesh):
    placed = (
        P("ctx", "vocab"),
        P(),
        P(("vocab", "ctx"), None),
        P(),
        P(),
        P(),
        P("ctx", "vocab"),
        P("ctx", "vocab"),
        P("ctx", "vocab"),
        P("vocab", "ctx"),
    )
    return jax.shard_map(
        per_device,
        mesh=mesh,
        in_specs=placed,
        out_specs=(P(), P("ctx", "vocab"), P("ctx", "vocab"), P("ctx", "vocab"), P("ctx", None)),
        check_vma=False,
    )
```

```python
import functools

import jax
import jax.numpy as jnp
from jax import lax
from jax.experimental import pallas as pl
from jax.experimental.pallas import tpu as pltpu
from jax.sharding import PartitionSpec as P

HEAD_SIZE = 128
CORES = 2
CHUNK = 768
SLOTS = 3
LANES = 128

norm_eps = 1e-06
grad_weight = 16.0
masked_fill = -1e30

f32 = jnp.float32
bf16 = jnp.bfloat16

NT = (((1,), (1,)), ((), ()))
NN = (((1,), (0,)), ((), ()))
TN = (((0,), (0,)), ((), ()))


def dot(a, b, dims):
    return lax.dot_general(a, b, dims, preferred_element_type=f32)


def smem():
    return pl.BlockSpec(memory_space=pltpu.SMEM)


def hbm():
    return pl.BlockSpec(memory_space=pltpu.HBM)


def vmem():
    return pl.BlockSpec(memory_space=pltpu.VMEM)


def shape(dims, dtype):
    return jax.ShapeDtypeStruct(dims, dtype)


def call(body, outs, ins, scratch=(), limit=16, flops=0, moved=0, exps=0):
    return pl.pallas_call(
        body,
        out_shape=outs,
        in_specs=ins,
        out_specs=jax.tree.map(lambda _: vmem(), outs),
        scratch_shapes=list(scratch),
        compiler_params=pltpu.CompilerParams(vmem_limit_bytes=limit * 2**20),
        cost_estimate=pl.CostEstimate(flops=flops, bytes_accessed=moved, transcendentals=exps),
    )


def shifted(value, axis, step, inner=1):
    size = lax.axis_size(axis)
    outer = size // inner
    pairs = [(i, ((i // inner + step) % outer) * inner + i % inner) for i in range(size)]
    return lax.ppermute(value, axis, pairs)


def crossed(value, bit):
    size = lax.axis_size("ctx")
    return lax.ppermute(value, "ctx", [(i, i ^ (bit * CORES)) for i in range(size)])


def swapped(value):
    size = lax.axis_size("ctx")
    return lax.ppermute(value, "ctx", [(i, i ^ 1) for i in range(size)])


def row_choice(loss_per, tokens, place, rows):
    base = place[3] * loss_per
    row_iota = lax.broadcasted_iota(jnp.int32, (loss_per, tokens), 0)
    col_iota = lax.broadcasted_iota(jnp.int32, (loss_per, tokens), 1)
    sel = jnp.zeros((loss_per, tokens), f32)
    for j in range(loss_per):
        sel = jnp.where((row_iota == j) & (col_iota == rows[base + j]), 1.0, sel)
    return sel.astype(bf16)


def pick_body(loss_per, place, rows, hidden, picked, here, sem):
    tokens, width = hidden.shape
    copy = pltpu.make_async_copy(hidden, here, sem)
    copy.start()
    choice = row_choice(loss_per, tokens, place, rows)
    copy.wait()
    mine = dot(choice, here[...], NN)
    half = width // 2
    picked[...] = jnp.concatenate([mine[:, :half], mine[:, half:]], axis=0).astype(bf16)


def pack_body(loss_per, place, rows, queries, keys, values, packed):
    tokens, key_width = keys.shape
    mine = dot(row_choice(loss_per, tokens, place, rows), queries[...], NN)
    packed[0:tokens, 0:key_width] = keys[...]
    packed[0:tokens, key_width : 2 * key_width] = values[...]
    parts = queries.shape[1] // (2 * key_width)
    stacked = [mine[:, b * 2 * key_width : (b + 1) * 2 * key_width] for b in range(parts)]
    packed[tokens : tokens + parts * loss_per, :] = jnp.concatenate(stacked, axis=0).astype(bf16)


def target_body(place, targets, weight, out, buf, spots, sems):
    blocks, loss, block_width = out.shape
    width = blocks * block_width
    total_rows = weight.shape[0]
    offset = targets[...] - place[4]
    local = (offset >= 0) & (offset < total_rows)
    offset = offset.astype(f32)
    index = lax.broadcasted_iota(jnp.int32, (1, loss), 1).astype(f32)
    none = float(loss)
    count = jnp.sum(jnp.where(local, 1.0, 0.0)).astype(jnp.int32)

    def copy(k, at):
        start = pl.multiple_of(lax.div(at, 16) * 16, 16)
        return pltpu.make_async_copy(weight.at[pl.ds(start, 16), :], buf.at[k], sems.at[k])

    def begin(k, left):
        spot = jnp.min(left)
        at = jnp.sum(jnp.where(index == spot, offset, 0.0)).astype(jnp.int32)
        spots[0, k] = spot.astype(jnp.int32)
        spots[1, k] = at
        copy(k, at).start()
        return jnp.where(index == spot, none, left)

    lax.fori_loop(0, count, begin, jnp.where(local, index, none))
    out[...] = jnp.zeros_like(out)
    line = lax.broadcasted_iota(jnp.int32, (16, block_width), 0)

    @pl.loop(0, count)
    def _(k):
        spot, at = spots[0, k], spots[1, k]
        copy(k, at).wait()
        group = pl.ds(pl.multiple_of(lax.div(spot, 16) * 16, 16), 16)
        for b in range(blocks):
            block = buf[k, :, b * block_width : (b + 1) * block_width].astype(f32)
            row = jnp.sum(jnp.where(line == lax.rem(at, 16), block, 0.0), axis=0, keepdims=True)
            before = out[b, group, :].astype(f32)
            out[b, group, :] = jnp.where(line == lax.rem(spot, 16), row, before).astype(bf16)


def flash_body(
    first,
    place,
    own,
    other,
    gain,
    targets,
    weight,
    keep,
    send,
    stats,
    unit,
    normed,
    raw,
    acc,
    probs,
    state,
    head_buf,
    buf,
    head_sem,
    sems,
):
    vocab_at, z_at, core_at, ctx_at, first_id = (place[k] for k in range(5))
    nv, nz = own.shape[0], own.shape[1]
    loss, width = normed.shape
    half = own.shape[3]
    total_rows = weight.shape[0]
    chunks = (total_rows - first) // CHUNK
    blocks = acc.shape[0]
    block_width = width // blocks

    def head_copy():
        return pltpu.make_async_copy(weight.at[pl.ds(0, first), :], head_buf, head_sem)

    def body_copy(c):
        slot = lax.rem(c, SLOTS)
        start = pl.multiple_of(first + c * CHUNK, 16)
        return pltpu.make_async_copy(
            weight.at[pl.ds(start, CHUNK), :], buf.at[slot], sems.at[slot]
        )

    head_copy().start()
    for c in range(min(SLOTS, chunks)):
        body_copy(c).start()

    is_even = core_at == 0
    for zr in range(nz):
        z_src = lax.rem(z_at - zr + nz, nz)
        square_own = jnp.zeros((8, 1), f32)
        square_other = jnp.zeros((8, 1), f32)
        for vr in range(nv):
            a = own[vr, zr].astype(f32)
            b = other[vr, zr].astype(f32)
            square_a = jnp.sum(a * a, axis=1, keepdims=True)
            square_b = jnp.sum(b * b, axis=1, keepdims=True)
            square_own += square_a[:8] + square_a[8:]
            square_other += square_b[:8] + square_b[8:]
        square = jnp.concatenate(
            [
                jnp.where(is_even, square_own, square_other),
                jnp.where(is_even, square_other, square_own),
            ],
            axis=0,
        )
        inv = lax.rsqrt(square / width + norm_eps)
        row_at = pl.multiple_of(z_src * 16, 16)
        state[pl.ds(row_at, 16), :] = jnp.broadcast_to(inv, (16, LANES))
        for vr in range(nv):
            v_src = lax.rem(vocab_at - vr + nv, nv)
            a = own[vr, zr].astype(f32)
            b = other[vr, zr].astype(f32)
            low = jnp.where(is_even, a, b)
            high = jnp.where(is_even, b, a)
            for k in range(2):
                x = jnp.concatenate([low[8 * k : 8 * k + 8], high[8 * k : 8 * k + 8]], axis=0)
                lane_at = pl.multiple_of((v_src * 2 + k) * half, half)
                raw[pl.ds(row_at, 16), pl.ds(lane_at, half)] = x.astype(bf16)
                normed[pl.ds(row_at, 16), pl.ds(lane_at, half)] = (
                    x * inv * gain[:, pl.ds(lane_at, half)]
                ).astype(bf16)

    per_vocab = loss // nv
    mine_at = pl.multiple_of(vocab_at * per_vocab, per_vocab)
    feature_at = pl.multiple_of(ctx_at * block_width, block_width)
    unit[...] = (
        raw[pl.ds(mine_at, per_vocab), pl.ds(feature_at, block_width)].astype(f32)
        * state[pl.ds(mine_at, per_vocab), 0:1]
    )

    target_col = targets[...]

    def softmax(scores, base, before):
        cols = scores.shape[1]
        ids = base + lax.broadcasted_iota(jnp.int32, (loss, cols), 1)
        hit = ids == target_col
        top = jnp.max(scores, axis=1, keepdims=True)
        if before is not None:
            top = jnp.maximum(top, before[0])
        shifted_scores = scores - top
        weights = jnp.exp(shifted_scores)
        total = jnp.sum(weights, axis=1, keepdims=True)
        moment = jnp.sum(weights * shifted_scores, axis=1, keepdims=True)
        logit = jnp.sum(jnp.where(hit, scores, 0.0), axis=1, keepdims=True)
        scale = None
        if before is not None:
            gap = before[0] - top
            scale = jnp.exp(gap)
            total = total + before[1] * scale
            moment = moment + scale * (before[2] + gap * before[1])
            logit = logit + before[3]
        masked = jnp.where(hit, 0.0, weights).astype(bf16)
        return masked, scale, (top, total, moment, logit)

    def scores_of(block):
        return dot(block, normed[...], NT).T

    def add_product(p, scale, read):
        for b in range(blocks):
            part = dot(p, read(b * block_width, block_width), NN)
            if scale is None:
                acc[b] = part
            else:
                acc[b] = acc[b] * scale + part

    def part(ref, slot):
        return lambda at, n: ref[slot, :, at : at + n]

    head_copy().wait()
    p, _, run = softmax(scores_of(head_buf[...]), first_id, None)
    if not chunks:
        add_product(p, None, lambda at, n: head_buf[:, at : at + n])
    else:
        def start_of(c):
            return first_id + first + c * CHUNK

        body_copy(0).wait()
        scores = scores_of(buf[0])
        add_product(p, None, lambda at, n: head_buf[:, at : at + n])
        p, scale, run = softmax(scores, start_of(0), run)
        probs[...] = p

        def step(c, carry):
            scale, run = carry
            body_copy(c).wait()
            scores = scores_of(buf[lax.rem(c, SLOTS)])
            add_product(probs[...], scale, part(buf, lax.rem(c - 1, SLOTS)))
            p, scale, run = softmax(scores, start_of(c), run)
            probs[...] = p

            @pl.when(c + 2 < chunks)
            def _():
                body_copy(c + 2).start()

            return scale, run

        scale, run = lax.fori_loop(1, chunks, step, (scale, run))
        add_product(probs[...], scale, part(buf, (chunks - 1) % SLOTS))

    for z in range(nz):
        keep[z] = acc[CORES * z + core_at]
        send[:, z * block_width : (z + 1) * block_width] = acc[CORES * z + 1 - core_at].astype(bf16)
    send[:, nz * block_width :] = split_columns(run)
    stats[...] = with_stats(state[...], run)


def split_columns(columns):
    rows = columns[0].shape[0]
    lane = lax.broadcasted_iota(jnp.int32, (rows, LANES), 1)
    table = jnp.zeros((rows, LANES), f32)
    for k, column in enumerate(columns):
        rest = column
        for j in range(3):
            term = rest.astype(bf16).astype(f32)
            table = jnp.where(lane == 3 * k + j, term, table)
            rest = rest - term
    return table.astype(bf16)


def joined_columns(block, count):
    block = block.astype(f32)
    return [
        block[:, 3 * k : 3 * k + 1] + block[:, 3 * k + 1 : 3 * k + 2] + block[:, 3 * k + 2 : 3 * k + 3]
        for k in range(count)
    ]


def stats_of(table):
    return [table[:, k : k + 1] for k in range(4)]


def merge_stats(columns):
    top = functools.reduce(jnp.maximum, [c[0] for c in columns])
    gaps = [c[0] - top for c in columns]
    scales = [jnp.exp(g) for g in gaps]
    total = sum(s * c[1] for s, c in zip(scales, columns))
    moment = sum(s * (c[2] + g * c[1]) for s, g, c in zip(scales, gaps, columns))
    logit = sum(c[3] for c in columns)
    return scales, (top, total, moment, logit)


def with_stats(table, merged):
    lane = lax.broadcasted_iota(jnp.int32, table.shape, 1)
    for k in range(4):
        table = jnp.where(lane == k, merged[k], table)
    return table


def core_body(count, place, keep, got, mine, target_rows, new_stats, new_keep, new_rows, *rest):
    sends, (total, table, message, rows_here, sem) = rest[:count], rest[count:]
    nz, loss, block = keep.shape
    rows_copy = pltpu.make_async_copy(target_rows, rows_here, sem)
    rows_copy.start()
    columns = [stats_of(mine[...]), joined_columns(got[:, nz * block :], 4)]
    scales, merged = merge_stats(columns)
    table[...] = with_stats(mine[...], merged)
    message[...] = split_columns(merged)
    per = loss // (count + 1)
    for z in range(nz):
        other = got[:, z * block : (z + 1) * block].astype(f32)
        total[z] = keep[z] * scales[0] + other * scales[1]
    at = pl.multiple_of(place[0] * per, per)
    new_stats[...] = table[pl.ds(at, per), :]
    new_keep[...] = total[:, pl.ds(at, per), :]
    for s in range(count):
        to = lax.rem(place[0] + s + 1, count + 1)
        rows = pl.ds(pl.multiple_of(to * per, per), per)
        for z in range(nz):
            sends[s][:, z * block : (z + 1) * block] = total[z, rows, :].astype(bf16)
        sends[s][:, (nz + 1) * block :] = message[rows, :]
    rows_copy.wait()
    for s in range(count):
        to = lax.rem(place[0] + s + 1, count + 1)
        rows = pl.ds(pl.multiple_of(to * per, per), per)
        sends[s][:, nz * block : (nz + 1) * block] = rows_here[rows, :]
    new_rows[...] = rows_here[pl.ds(at, per), :]


def plane_body(count, place, keep, mine, target_rows, *rest):
    got, rest = rest[:count], rest[count:]
    new_stats, new_keep, new_target = rest[:3]
    sends, (total,) = rest[3:-1], rest[-1:]
    nz, per, block = keep.shape
    columns = [stats_of(mine[...])] + [joined_columns(g[:, (nz + 1) * block :], 4) for g in got]
    scales, merged = merge_stats(columns)
    new_stats[...] = with_stats(mine[...], merged)
    message = split_columns(merged)
    for z in range(nz):
        value = keep[z] * scales[0]
        for k in range(count):
            value = value + got[k][:, z * block : (z + 1) * block].astype(f32) * scales[k + 1]
        total[z] = value
    new_keep[...] = total[place[1]]
    rows = target_rows[...].astype(f32)
    for k in range(count):
        rows = rows + got[k][:, nz * block : (nz + 1) * block].astype(f32)
    new_target[...] = rows.astype(bf16)
    for s in range(nz - 1):
        sends[s][:, :block] = total[lax.rem(place[1] + s + 1, nz)].astype(bf16)
        sends[s][:, block:] = message


def line_body(count, width, place, keep, mine, target_rows, unit, gain, *rest):
    got, (message,) = rest[:count], rest[count:]
    per, block = keep.shape
    columns = [stats_of(mine[...])] + [joined_columns(g[:, block:], 4) for g in got]
    scales, (top, total, moment, logit) = merge_stats(columns)
    log_total = top + jnp.log(total)
    value = keep[...] * (scales[0] / total)
    for k in range(count):
        value = value + got[k][:, :block].astype(f32) * (scales[k + 1] / total)
    inner = grad_weight * (moment / total + (top - logit)) / width
    short = jnp.exp(logit - log_total) - 1.0
    inv = mine[:, 4:5]
    grad = grad_weight * (value + short * target_rows[...].astype(f32))
    gain_at = pl.multiple_of(place[3] * block, block)
    scaled = grad * gain[:, pl.ds(gain_at, block)]
    message[:, :block] = (inv * (scaled - unit[...] * inner)).astype(bf16)
    message[:, block:] = split_columns([log_total - logit])


def project_body(nv, place, *refs):
    gathered, refs = refs[:nv], refs[nv:]
    weight, resid, loss_out, keep, send, whole, partial, here, sems = refs
    parts, part, _ = here.shape
    copies = [
        pltpu.make_async_copy(weight.at[pl.ds(k * part, part), :], here.at[k], sems.at[k])
        for k in range(parts)
    ]
    for copy in copies:
        copy.start()
    per = gathered[0].shape[0]
    block = whole.shape[1]
    loss_sum = jnp.zeros((1, 1), f32)
    for v in range(nv):
        src = lax.rem(place[0] - v + nv, nv)
        whole[pl.ds(pl.multiple_of(src * per, per), per), :] = gathered[v][:, :block]
        (column,) = joined_columns(gathered[v][:, block:], 1)
        loss_sum = loss_sum + jnp.sum(column, axis=0, keepdims=True)
    loss_out[...] = loss_sum / (nv * per)
    resid[...] = whole[...]
    for k in range(parts):
        copies[k].wait()
        partial[:, k * part : (k + 1) * part] = dot(whole[...], here[k], NT)
    cols = keep.shape[1]
    keep[...] = partial[:, pl.ds(pl.multiple_of(place[2] * cols, cols), cols)]
    send[...] = partial[:, pl.ds(pl.multiple_of((1 - place[2]) * cols, cols), cols)].astype(bf16)


def sum_body(keep, *refs):
    value = keep[...].astype(f32)
    for ref in refs[:-1]:
        value = value + ref[...].astype(f32)
    refs[-1][...] = value.astype(bf16)


def forward_body(
    loss_per, heads, group, heads_at_once, j, place, key_pos, query_pos, packed, p_own, p_rows, out, scratch
):
    nc = packed.shape[0]
    tokens = p_own.shape[1]
    loss = loss_per * nc
    key_width = heads * HEAD_SIZE
    score_scale = HEAD_SIZE ** (-0.5)
    ctx_at = place[3]
    own_at = pl.multiple_of(ctx_at * tokens, tokens)
    row_at = pl.multiple_of(ctx_at * loss_per, loss_per)
    key = jnp.concatenate(
        [packed[c, 0:tokens, j * HEAD_SIZE : (j + 1) * HEAD_SIZE] for c in range(nc)], axis=0
    )
    at = key_width + j * HEAD_SIZE
    value = jnp.concatenate(
        [packed[c, 0:tokens, at : at + HEAD_SIZE] for c in range(nc)], axis=0
    )
    for g0 in range(0, group, heads_at_once):
        stacked = []
        for g in range(g0, g0 + heads_at_once):
            stacked.append(query_of(packed, j * group + g, tokens, loss_per, key_width))
        query = jnp.concatenate(stacked, axis=0).astype(bf16)
        where_at = jnp.concatenate([query_pos[...]] * heads_at_once, axis=0)
        visible = key_pos[...] <= where_at
        scores = jnp.where(visible, dot(query, key, NT) * score_scale, masked_fill)
        top = jnp.max(scores, axis=1, keepdims=True)
        raw = jnp.where(visible, jnp.exp(scores - top), 0.0)
        prob = raw / jnp.sum(raw, axis=1, keepdims=True)
        scratch[...] = prob
        coarse = prob.astype(bf16)
        fine = (prob - coarse.astype(f32)).astype(bf16)
        first = g0 * loss
        n = heads_at_once * loss
        out[first : first + n, :] = dot(coarse, value, NN) + dot(fine, value, NN)
        p_own[first : first + n, :] = scratch[:, pl.ds(own_at, tokens)]
        for k in range(heads_at_once):
            p_rows[(g0 + k) * loss_per : (g0 + k + 1) * loss_per, :] = scratch[
                pl.ds(pl.multiple_of(k * loss + row_at, loss_per), loss_per), :
            ]


def query_of(packed, head, tokens, loss_per, key_width):
    lane = head * HEAD_SIZE
    b, at = lane // (2 * key_width), lane % (2 * key_width)
    parts = []
    for c in range(packed.shape[0]):
        block = packed[c, tokens:, at : at + HEAD_SIZE].astype(f32)
        parts.append(block[b * loss_per : (b + 1) * loss_per])
    return jnp.concatenate(parts, axis=0)


def backward_body(loss_per, heads, group, place, half, other, packed, *refs):
    attention = [refs[3 * j : 3 * j + 3] for j in range(heads)]
    query_grad, key_grad, value_grad, grad = refs[3 * heads :]
    nc = packed.shape[0]
    tokens = key_grad.shape[0]
    loss = loss_per * nc
    key_width = heads * HEAD_SIZE
    score_scale = HEAD_SIZE ** (-0.5)
    ctx_at = place[3]
    cols = half.shape[1]
    grad[:, pl.ds(pl.multiple_of(place[2] * cols, cols), cols)] = half[...].astype(f32)
    grad[:, pl.ds(pl.multiple_of((1 - place[2]) * cols, cols), cols)] = other[...].astype(f32)
    mine_at = pl.multiple_of(ctx_at * loss_per, loss_per)
    for j in range(heads):
        p_own, p_rows, out = attention[j]
        lanes = [slice((j * group + g) * HEAD_SIZE, (j * group + g + 1) * HEAD_SIZE) for g in range(group)]
        d_out = jnp.concatenate([grad[:, s] for s in lanes], axis=0)
        d_half = d_out.astype(bf16)
        delta = jnp.sum(d_out * out[...], axis=1, keepdims=True)
        query = jnp.concatenate(
            [query_of(packed, j * group + g, tokens, loss_per, key_width) for g in range(group)], axis=0
        ).astype(bf16)
        at = key_width + j * HEAD_SIZE
        own_value = packed[ctx_at, 0:tokens, at : at + HEAD_SIZE]
        prob = p_own[...]
        score_grad = (prob * (dot(d_half, own_value, NT) - delta)).astype(bf16)
        k_lanes = slice(j * HEAD_SIZE, (j + 1) * HEAD_SIZE)
        key_grad[:, k_lanes] = (dot(score_grad, query, TN) * score_scale).astype(bf16)
        value_grad[:, k_lanes] = dot(prob.astype(bf16), d_half, TN).astype(bf16)
        key = jnp.concatenate([packed[c, 0:tokens, k_lanes] for c in range(nc)], axis=0)
        value = jnp.concatenate([packed[c, 0:tokens, at : at + HEAD_SIZE] for c in range(nc)], axis=0)
        d_mine = jnp.concatenate([grad[pl.ds(mine_at, loss_per), s] for s in lanes], axis=0)
        out_mine = jnp.concatenate(
            [
                out[pl.ds(pl.multiple_of(g * loss + mine_at, loss_per), loss_per), :]
                for g in range(group)
            ],
            axis=0,
        )
        delta = jnp.sum(d_mine * out_mine, axis=1, keepdims=True)
        d_prob = dot(d_mine.astype(bf16), value, NT)
        score_grad = (p_rows[...] * (d_prob - delta)).astype(bf16)
        result = dot(score_grad, key, NN) * score_scale
        for g in range(group):
            query_grad[:, lanes[g]] = result[g * loss_per : (g + 1) * loss_per].astype(bf16)


def per_device(
    hidden,
    norm_gain,
    head_weight,
    targets,
    loss_rows,
    stretch_of_slot,
    queries,
    key_states,
    attention_values,
    output_weight,
):
    nc = lax.axis_size("ctx")
    nv = lax.axis_size("vocab")
    nz = nc // CORES
    ctx_at = lax.axis_index("ctx")
    vocab_at = lax.axis_index("vocab")
    tokens = hidden.shape[0]
    stretch_len = tokens // 2
    loss = loss_rows.shape[0]
    loss_per = loss // nc
    width = norm_gain.shape[0]
    voc_rows = head_weight.shape[0]
    part_width = hidden.shape[1]
    query_width = queries.shape[1]
    key_width = key_states.shape[1]
    heads = key_width // HEAD_SIZE
    group = query_width // key_width
    block_width = width // nc
    per_vocab = loss // nv
    all_tokens = tokens * nc

    first_id = (vocab_at * nc + ctx_at) * voc_rows
    place = jnp.stack([vocab_at, ctx_at // CORES, ctx_at % CORES, ctx_at, first_id]).astype(jnp.int32)

    slots = stretch_of_slot.shape[0]
    owner = lax.broadcasted_iota(jnp.int32, (loss, 1), 0) // loss_per
    slot = 2 * owner + loss_rows[:, None] // stretch_len
    slot_iota = lax.broadcasted_iota(jnp.int32, (1, slots), 1)
    stretch = jnp.sum(jnp.where(slot == slot_iota, stretch_of_slot[None, :], 0), axis=1, keepdims=True)
    query_pos = stretch * stretch_len + loss_rows[:, None] % stretch_len
    key_pos = (
        stretch_of_slot[:, None] * stretch_len
        + lax.broadcasted_iota(jnp.int32, (1, stretch_len), 1)
    ).reshape(1, all_tokens)
    picked = call(
        functools.partial(pick_body, loss_per),
        shape((2 * loss_per, part_width // 2), bf16),
        [smem(), smem(), hbm()],
        [pltpu.VMEM((tokens, part_width), bf16), pltpu.SemaphoreType.DMA],
    )(place, loss_rows, hidden)
    picked, queries, targets_late = lax.optimization_barrier((picked, queries, targets))
    extra = (query_width // (2 * key_width)) * loss_per
    packed = call(
        functools.partial(pack_body, loss_per),
        shape((tokens + extra, 2 * key_width), bf16),
        [smem(), smem()] + [vmem()] * 3,
        moved=2 * queries.size,
    )(place, loss_rows, queries, key_states, attention_values)
    by_z = jnp.stack([picked] + [shifted(picked, "ctx", s, CORES) for s in range(1, nz)])
    planes = [by_z] + [shifted(by_z, "vocab", s) for s in range(1, nv)]
    if voc_rows % 16:
        local = targets_late - first_id
        is_local = (local >= 0) & (local < voc_rows)
        target_rows = head_weight.at[jnp.clip(local, 0, voc_rows - 1)].get(mode="promise_in_bounds")
        target_rows = jnp.where(is_local[:, None], target_rows, jnp.zeros((), bf16))
        target_rows = target_rows.reshape(loss, nc, block_width).transpose(1, 0, 2)
    else:
        target_rows = pl.pallas_call(
            target_body,
            out_shape=shape((nc, loss, block_width), bf16),
            in_specs=[smem(), vmem(), pl.BlockSpec(memory_space=pl.ANY)],
            out_specs=vmem(),
            scratch_shapes=[
                pltpu.VMEM((loss, 16, width), bf16),
                pltpu.SMEM((2, loss), jnp.int32),
                pltpu.SemaphoreType.DMA((loss,)),
            ],
            compiler_params=pltpu.CompilerParams(vmem_limit_bytes=40 * 2**20),
            cost_estimate=pl.CostEstimate(
                flops=0, bytes_accessed=2 * 16 * loss * width, transcendentals=0
            ),
        )(place, targets_late.reshape(1, loss), head_weight)
    planes, target_rows = lax.optimization_barrier((planes, target_rows))
    by_plane = jnp.stack(planes)
    other = swapped(by_plane)
    target_rows = lax.psum_scatter(
        target_rows.reshape(nc * loss, block_width), "ctx", scatter_dimension=0, tiled=True
    )
    other, packed = lax.optimization_barrier((other, packed))
    packed_all = lax.all_gather(packed, "ctx")

    first = voc_rows % CHUNK
    if voc_rows < SLOTS * CHUNK or first % 16 or not first:
        first = voc_rows if voc_rows < SLOTS * CHUNK else CHUNK
    chunks = (voc_rows - first) // CHUNK
    gain = norm_gain.reshape(1, width)
    keep, send, stats, unit = pl.pallas_call(
        functools.partial(flash_body, first),
        out_shape=(
            shape((nz, loss, block_width), f32),
            shape((loss, nz * block_width + LANES), bf16),
            shape((loss, LANES), f32),
            shape((per_vocab, block_width), f32),
        ),
        in_specs=[smem()] + [vmem()] * 4 + [pl.BlockSpec(memory_space=pl.ANY)],
        out_specs=[vmem()] * 4,
        scratch_shapes=[
            pltpu.VMEM((loss, width), bf16),
            pltpu.VMEM((loss, width), bf16),
            pltpu.VMEM((nc, loss, block_width), f32),
            pltpu.VMEM((loss, CHUNK), bf16),
            pltpu.VMEM((loss, LANES), f32),
            pltpu.VMEM((first, width), bf16),
            pltpu.VMEM((SLOTS if chunks else 1, CHUNK if chunks else 16, width), bf16),
            pltpu.SemaphoreType.DMA,
            pltpu.SemaphoreType.DMA((SLOTS,)),
        ],
        compiler_params=pltpu.CompilerParams(vmem_limit_bytes=48 * 2**20),
        cost_estimate=pl.CostEstimate(
            flops=4 * max(loss, 256) * width * voc_rows,
            bytes_accessed=4 * width * voc_rows,
            transcendentals=loss * voc_rows,
        ),
    )(place, by_plane, other, gain, targets.reshape(loss, 1), head_weight)

    send, target_rows = lax.optimization_barrier((send, target_rows))
    got = swapped(send)
    stats, keep, target_rows, *sends = call(
        functools.partial(core_body, nv - 1),
        (
            shape((per_vocab, LANES), f32),
            shape((nz, per_vocab, block_width), f32),
            shape((per_vocab, block_width), bf16),
        )
        + (shape((per_vocab, (nz + 1) * block_width + LANES), bf16),) * (nv - 1),
        [smem()] + [vmem()] * 3 + [hbm()],
        [
            pltpu.VMEM((nz, loss, block_width), f32),
            pltpu.VMEM((loss, LANES), f32),
            pltpu.VMEM((loss, LANES), bf16),
            pltpu.VMEM((loss, block_width), bf16),
            pltpu.SemaphoreType.DMA,
        ],
    )(place, keep, got, stats, target_rows)
    got = [shifted(sends[s - 1], "vocab", s) for s in range(1, nv)]

    at_once = max(1, min(group, (4 * 2**20) // (loss * all_tokens * 4)))

    def forward(j, query_pos):
        return call(
            functools.partial(forward_body, loss_per, heads, group, at_once, j),
            (
                shape((group * loss, tokens), f32),
                shape((group * loss_per, all_tokens), f32),
                shape((group * loss, HEAD_SIZE), f32),
            ),
            [smem()] + [vmem()] * 3,
            [pltpu.VMEM((at_once * loss, all_tokens), f32)],
            limit=40,
            flops=24 * group * loss * all_tokens * HEAD_SIZE,
            moved=2 * packed_all.size,
            exps=group * loss * all_tokens,
        )(place, key_pos, query_pos, packed_all)

    stats, packed_all = lax.optimization_barrier((stats, packed_all))
    stats, keep, target_rows, *sends = call(
        functools.partial(plane_body, nv - 1),
        (
            shape((per_vocab, LANES), f32),
            shape((per_vocab, block_width), f32),
            shape((per_vocab, block_width), bf16),
        )
        + (shape((per_vocab, block_width + LANES), bf16),) * (nz - 1),
        [smem()] + [vmem()] * (3 + nv - 1),
        [pltpu.VMEM((nz, per_vocab, block_width), f32)],
    )(place, keep, stats, target_rows, *got)
    got = [shifted(sends[s - 1], "ctx", s, CORES) for s in range(1, nz)]
    message = call(
        functools.partial(line_body, nz - 1, width),
        shape((per_vocab, block_width + LANES), bf16),
        [smem()] + [vmem()] * (5 + nz - 1),
    )(place, keep, stats, target_rows, unit, gain, *got)

    gathered = [message] + [shifted(message, "vocab", s) for s in range(1, nv)]
    cols = query_width // CORES
    resid_rows, mean_loss, keep, send = call(
        functools.partial(project_body, nv),
        (
            shape((loss, block_width), bf16),
            shape((1, 1), f32),
            shape((loss, cols), f32),
            shape((loss, cols), bf16),
        ),
        [smem()] + [vmem()] * nv + [hbm()],
        [
            pltpu.VMEM((loss, block_width), bf16),
            pltpu.VMEM((loss, query_width), f32),
            pltpu.VMEM((4, query_width // 4, block_width), bf16),
            pltpu.SemaphoreType.DMA((4,)),
        ],
        limit=52,
    )(place, *gathered, output_weight)
    half = call(sum_body, shape((loss, cols), bf16), [vmem()] * 2)(keep, swapped(send))
    windows = nz.bit_length() - 1
    attention = [None] * heads
    for k in range(windows):
        got = crossed(half, 2**k)
        here = range(k, heads, windows)
        half, query_pos = lax.optimization_barrier((half, query_pos))
        made = [forward(j, query_pos) for j in here]
        half, made = lax.optimization_barrier((half, made))
        for j, result in zip(here, made):
            attention[j] = result
        half = call(sum_body, shape((loss, cols), bf16), [vmem()] * 2)(half, got)
    other = swapped(half)
    query_grad, key_grad, value_grad = call(
        functools.partial(backward_body, loss_per, heads, group),
        (
            shape((loss_per, query_width), bf16),
            shape((tokens, key_width), bf16),
            shape((tokens, key_width), bf16),
        ),
        [smem()] + [vmem()] * (3 + 3 * heads),
        [pltpu.VMEM((loss, query_width), f32)],
    )(place, half, other, packed_all, *jax.tree.leaves(attention))
    return (mean_loss.reshape(()), query_grad, key_grad, value_grad, resid_rows.T)


def solution(mesh):
    placed = (
        P("ctx", "vocab"),
        P(),
        P(("vocab", "ctx"), None),
        P(),
        P(),
        P(),
        P("ctx", "vocab"),
        P("ctx", "vocab"),
        P("ctx", "vocab"),
        P("vocab", "ctx"),
    )
    return jax.shard_map(
        per_device,
        mesh=mesh,
        in_specs=placed,
        out_specs=(P(), P("ctx", "vocab"), P("ctx", "vocab"), P("ctx", "vocab"), P("ctx", None)),
        check_vma=False,
    )
```

```python
import functools

import jax
import jax.numpy as jnp
from jax import lax
from jax.experimental import pallas as pl
from jax.experimental.pallas import tpu as pltpu
from jax.sharding import PartitionSpec as P

HEAD_SIZE = 128
CORES = 2
CHUNK = 512
SLOTS = 3
LANES = 128

norm_eps = 1e-06
grad_weight = 16.0
masked_fill = -1e30

f32 = jnp.float32
bf16 = jnp.bfloat16

NT = (((1,), (1,)), ((), ()))
NN = (((1,), (0,)), ((), ()))
TN = (((0,), (0,)), ((), ()))


def dot(a, b, dims):
    return lax.dot_general(a, b, dims, preferred_element_type=f32)


def smem():
    return pl.BlockSpec(memory_space=pltpu.SMEM)


def hbm():
    return pl.BlockSpec(memory_space=pltpu.HBM)


def vmem():
    return pl.BlockSpec(memory_space=pltpu.VMEM)


def shape(dims, dtype):
    return jax.ShapeDtypeStruct(dims, dtype)


def call(body, outs, ins, scratch=(), limit=16, flops=0, moved=0, exps=0):
    return pl.pallas_call(
        body,
        out_shape=outs,
        in_specs=ins,
        out_specs=jax.tree.map(lambda _: vmem(), outs),
        scratch_shapes=list(scratch),
        compiler_params=pltpu.CompilerParams(vmem_limit_bytes=limit * 2**20),
        cost_estimate=pl.CostEstimate(flops=flops, bytes_accessed=moved, transcendentals=exps),
    )


def shifted(value, axis, step, inner=1):
    size = lax.axis_size(axis)
    outer = size // inner
    pairs = [(i, ((i // inner + step) % outer) * inner + i % inner) for i in range(size)]
    return lax.ppermute(value, axis, pairs)


def crossed(value, bit):
    size = lax.axis_size("ctx")
    return lax.ppermute(value, "ctx", [(i, i ^ (bit * CORES)) for i in range(size)])


def swapped(value):
    size = lax.axis_size("ctx")
    return lax.ppermute(value, "ctx", [(i, i ^ 1) for i in range(size)])


def row_choice(loss_per, tokens, place, rows):
    base = place[3] * loss_per
    row_iota = lax.broadcasted_iota(jnp.int32, (loss_per, tokens), 0)
    col_iota = lax.broadcasted_iota(jnp.int32, (loss_per, tokens), 1)
    sel = jnp.zeros((loss_per, tokens), f32)
    for j in range(loss_per):
        sel = jnp.where((row_iota == j) & (col_iota == rows[base + j]), 1.0, sel)
    return sel.astype(bf16)


def pick_body(loss_per, place, rows, hidden, picked, here, sem):
    tokens, width = hidden.shape
    copy = pltpu.make_async_copy(hidden, here, sem)
    copy.start()
    choice = row_choice(loss_per, tokens, place, rows)
    copy.wait()
    mine = dot(choice, here[...], NN)
    half = width // 2
    picked[...] = jnp.concatenate([mine[:, :half], mine[:, half:]], axis=0).astype(bf16)


def pack_body(loss_per, place, rows, queries, keys, values, packed):
    tokens, key_width = keys.shape
    mine = dot(row_choice(loss_per, tokens, place, rows), queries[...], NN)
    packed[0:tokens, 0:key_width] = keys[...]
    packed[0:tokens, key_width : 2 * key_width] = values[...]
    parts = queries.shape[1] // (2 * key_width)
    stacked = [mine[:, b * 2 * key_width : (b + 1) * 2 * key_width] for b in range(parts)]
    packed[tokens : tokens + parts * loss_per, :] = jnp.concatenate(stacked, axis=0).astype(bf16)


def target_body(place, targets, weight, out, buf, spots, sems):
    blocks, loss, block_width = out.shape
    width = blocks * block_width
    total_rows = weight.shape[0]
    offset = targets[...] - place[4]
    local = (offset >= 0) & (offset < total_rows)
    offset = offset.astype(f32)
    index = lax.broadcasted_iota(jnp.int32, (1, loss), 1).astype(f32)
    none = float(loss)
    count = jnp.sum(jnp.where(local, 1.0, 0.0)).astype(jnp.int32)

    def copy(k, at):
        start = pl.multiple_of(lax.div(at, 16) * 16, 16)
        return pltpu.make_async_copy(weight.at[pl.ds(start, 16), :], buf.at[k], sems.at[k])

    def begin(k, left):
        spot = jnp.min(left)
        at = jnp.sum(jnp.where(index == spot, offset, 0.0)).astype(jnp.int32)
        spots[0, k] = spot.astype(jnp.int32)
        spots[1, k] = at
        copy(k, at).start()
        return jnp.where(index == spot, none, left)

    lax.fori_loop(0, count, begin, jnp.where(local, index, none))
    out[...] = jnp.zeros_like(out)
    line = lax.broadcasted_iota(jnp.int32, (16, block_width), 0)

    @pl.loop(0, count)
    def _(k):
        spot, at = spots[0, k], spots[1, k]
        copy(k, at).wait()
        group = pl.ds(pl.multiple_of(lax.div(spot, 16) * 16, 16), 16)
        for b in range(blocks):
            block = buf[k, :, b * block_width : (b + 1) * block_width].astype(f32)
            row = jnp.sum(jnp.where(line == lax.rem(at, 16), block, 0.0), axis=0, keepdims=True)
            before = out[b, group, :].astype(f32)
            out[b, group, :] = jnp.where(line == lax.rem(spot, 16), row, before).astype(bf16)


def flash_body(
    first,
    place,
    own,
    other,
    gain,
    targets,
    weight,
    keep,
    send,
    stats,
    unit,
    normed,
    raw,
    acc,
    probs,
    state,
    head_buf,
    buf,
    head_sem,
    sems,
):
    vocab_at, z_at, core_at, ctx_at, first_id = (place[k] for k in range(5))
    nv, nz = own.shape[0], own.shape[1]
    loss, width = normed.shape
    half = own.shape[3]
    total_rows = weight.shape[0]
    chunks = (total_rows - first) // CHUNK
    blocks = acc.shape[0]
    block_width = width // blocks

    def head_copy():
        return pltpu.make_async_copy(weight.at[pl.ds(0, first), :], head_buf, head_sem)

    def body_copy(c):
        slot = lax.rem(c, SLOTS)
        start = pl.multiple_of(first + c * CHUNK, 16)
        return pltpu.make_async_copy(
            weight.at[pl.ds(start, CHUNK), :], buf.at[slot], sems.at[slot]
        )

    head_copy().start()
    for c in range(min(SLOTS, chunks)):
        body_copy(c).start()

    is_even = core_at == 0
    for zr in range(nz):
        z_src = lax.rem(z_at - zr + nz, nz)
        square_own = jnp.zeros((8, 1), f32)
        square_other = jnp.zeros((8, 1), f32)
        for vr in range(nv):
            a = own[vr, zr].astype(f32)
            b = other[vr, zr].astype(f32)
            square_a = jnp.sum(a * a, axis=1, keepdims=True)
            square_b = jnp.sum(b * b, axis=1, keepdims=True)
            square_own += square_a[:8] + square_a[8:]
            square_other += square_b[:8] + square_b[8:]
        square = jnp.concatenate(
            [
                jnp.where(is_even, square_own, square_other),
                jnp.where(is_even, square_other, square_own),
            ],
            axis=0,
        )
        inv = lax.rsqrt(square / width + norm_eps)
        row_at = pl.multiple_of(z_src * 16, 16)
        state[pl.ds(row_at, 16), :] = jnp.broadcast_to(inv, (16, LANES))
        for vr in range(nv):
            v_src = lax.rem(vocab_at - vr + nv, nv)
            a = own[vr, zr].astype(f32)
            b = other[vr, zr].astype(f32)
            low = jnp.where(is_even, a, b)
            high = jnp.where(is_even, b, a)
            for k in range(2):
                x = jnp.concatenate([low[8 * k : 8 * k + 8], high[8 * k : 8 * k + 8]], axis=0)
                lane_at = pl.multiple_of((v_src * 2 + k) * half, half)
                raw[pl.ds(row_at, 16), pl.ds(lane_at, half)] = x.astype(bf16)
                normed[pl.ds(row_at, 16), pl.ds(lane_at, half)] = (
                    x * inv * gain[:, pl.ds(lane_at, half)]
                ).astype(bf16)

    per_vocab = loss // nv
    mine_at = pl.multiple_of(vocab_at * per_vocab, per_vocab)
    feature_at = pl.multiple_of(ctx_at * block_width, block_width)
    unit[...] = (
        raw[pl.ds(mine_at, per_vocab), pl.ds(feature_at, block_width)].astype(f32)
        * state[pl.ds(mine_at, per_vocab), 0:1]
    )

    target_col = targets[...]

    def softmax(scores, base, before):
        cols = scores.shape[1]
        ids = base + lax.broadcasted_iota(jnp.int32, (loss, cols), 1)
        hit = ids == target_col
        top = jnp.max(scores, axis=1, keepdims=True)
        if before is not None:
            top = jnp.maximum(top, before[0])
        shifted_scores = scores - top
        weights = jnp.exp(shifted_scores)
        total = jnp.sum(weights, axis=1, keepdims=True)
        moment = jnp.sum(weights * shifted_scores, axis=1, keepdims=True)
        logit = jnp.sum(jnp.where(hit, scores, 0.0), axis=1, keepdims=True)
        scale = None
        if before is not None:
            gap = before[0] - top
            scale = jnp.exp(gap)
            total = total + before[1] * scale
            moment = moment + scale * (before[2] + gap * before[1])
            logit = logit + before[3]
        masked = jnp.where(hit, 0.0, weights).astype(bf16)
        return masked, scale, (top, total, moment, logit)

    def scores_of(block):
        return dot(block, normed[...], NT).T

    def add_product(p, scale, read):
        for b in range(blocks):
            part = dot(p, read(b * block_width, block_width), NN)
            if scale is None:
                acc[b] = part
            else:
                acc[b] = acc[b] * scale + part

    def part(ref, slot):
        return lambda at, n: ref[slot, :, at : at + n]

    head_copy().wait()
    p, _, run = softmax(scores_of(head_buf[...]), first_id, None)
    if not chunks:
        add_product(p, None, lambda at, n: head_buf[:, at : at + n])
    else:
        def start_of(c):
            return first_id + first + c * CHUNK

        body_copy(0).wait()
        scores = scores_of(buf[0])
        add_product(p, None, lambda at, n: head_buf[:, at : at + n])
        p, scale, run = softmax(scores, start_of(0), run)
        probs[...] = p

        def step(c, carry):
            scale, run = carry
            body_copy(c).wait()
            scores = scores_of(buf[lax.rem(c, SLOTS)])
            add_product(probs[...], scale, part(buf, lax.rem(c - 1, SLOTS)))
            p, scale, run = softmax(scores, start_of(c), run)
            probs[...] = p

            @pl.when(c + 2 < chunks)
            def _():
                body_copy(c + 2).start()

            return scale, run

        scale, run = lax.fori_loop(1, chunks, step, (scale, run))
        add_product(probs[...], scale, part(buf, (chunks - 1) % SLOTS))

    for z in range(nz):
        keep[z] = acc[CORES * z + core_at]
        send[:, z * block_width : (z + 1) * block_width] = acc[CORES * z + 1 - core_at].astype(bf16)
    send[:, nz * block_width :] = split_columns(run)
    stats[...] = with_stats(state[...], run)


def split_columns(columns):
    rows = columns[0].shape[0]
    lane = lax.broadcasted_iota(jnp.int32, (rows, LANES), 1)
    table = jnp.zeros((rows, LANES), f32)
    for k, column in enumerate(columns):
        rest = column
        for j in range(3):
            term = rest.astype(bf16).astype(f32)
            table = jnp.where(lane == 3 * k + j, term, table)
            rest = rest - term
    return table.astype(bf16)


def joined_columns(block, count):
    block = block.astype(f32)
    return [
        block[:, 3 * k : 3 * k + 1] + block[:, 3 * k + 1 : 3 * k + 2] + block[:, 3 * k + 2 : 3 * k + 3]
        for k in range(count)
    ]


def stats_of(table):
    return [table[:, k : k + 1] for k in range(4)]


def merge_stats(columns):
    top = functools.reduce(jnp.maximum, [c[0] for c in columns])
    gaps = [c[0] - top for c in columns]
    scales = [jnp.exp(g) for g in gaps]
    total = sum(s * c[1] for s, c in zip(scales, columns))
    moment = sum(s * (c[2] + g * c[1]) for s, g, c in zip(scales, gaps, columns))
    logit = sum(c[3] for c in columns)
    return scales, (top, total, moment, logit)


def with_stats(table, merged):
    lane = lax.broadcasted_iota(jnp.int32, table.shape, 1)
    for k in range(4):
        table = jnp.where(lane == k, merged[k], table)
    return table


def core_body(count, place, keep, got, mine, target_rows, new_stats, new_keep, new_rows, *rest):
    sends, (total, table, message, rows_here, sem) = rest[:count], rest[count:]
    nz, loss, block = keep.shape
    rows_copy = pltpu.make_async_copy(target_rows, rows_here, sem)
    rows_copy.start()
    columns = [stats_of(mine[...]), joined_columns(got[:, nz * block :], 4)]
    scales, merged = merge_stats(columns)
    table[...] = with_stats(mine[...], merged)
    message[...] = split_columns(merged)
    per = loss // (count + 1)
    for z in range(nz):
        other = got[:, z * block : (z + 1) * block].astype(f32)
        total[z] = keep[z] * scales[0] + other * scales[1]
    at = pl.multiple_of(place[0] * per, per)
    new_stats[...] = table[pl.ds(at, per), :]
    new_keep[...] = total[:, pl.ds(at, per), :]
    for s in range(count):
        to = lax.rem(place[0] + s + 1, count + 1)
        rows = pl.ds(pl.multiple_of(to * per, per), per)
        for z in range(nz):
            sends[s][:, z * block : (z + 1) * block] = total[z, rows, :].astype(bf16)
        sends[s][:, (nz + 1) * block :] = message[rows, :]
    rows_copy.wait()
    for s in range(count):
        to = lax.rem(place[0] + s + 1, count + 1)
        rows = pl.ds(pl.multiple_of(to * per, per), per)
        sends[s][:, nz * block : (nz + 1) * block] = rows_here[rows, :]
    new_rows[...] = rows_here[pl.ds(at, per), :]


def plane_body(count, place, keep, mine, target_rows, *rest):
    got, rest = rest[:count], rest[count:]
    new_stats, new_keep, new_target = rest[:3]
    sends, (total,) = rest[3:-1], rest[-1:]
    nz, per, block = keep.shape
    columns = [stats_of(mine[...])] + [joined_columns(g[:, (nz + 1) * block :], 4) for g in got]
    scales, merged = merge_stats(columns)
    new_stats[...] = with_stats(mine[...], merged)
    message = split_columns(merged)
    for z in range(nz):
        value = keep[z] * scales[0]
        for k in range(count):
            value = value + got[k][:, z * block : (z + 1) * block].astype(f32) * scales[k + 1]
        total[z] = value
    new_keep[...] = total[place[1]]
    rows = target_rows[...].astype(f32)
    for k in range(count):
        rows = rows + got[k][:, nz * block : (nz + 1) * block].astype(f32)
    new_target[...] = rows.astype(bf16)
    for s in range(nz - 1):
        sends[s][:, :block] = total[lax.rem(place[1] + s + 1, nz)].astype(bf16)
        sends[s][:, block:] = message


def line_body(count, width, place, keep, mine, target_rows, unit, gain, *rest):
    got, (message,) = rest[:count], rest[count:]
    per, block = keep.shape
    columns = [stats_of(mine[...])] + [joined_columns(g[:, block:], 4) for g in got]
    scales, (top, total, moment, logit) = merge_stats(columns)
    log_total = top + jnp.log(total)
    value = keep[...] * (scales[0] / total)
    for k in range(count):
        value = value + got[k][:, :block].astype(f32) * (scales[k + 1] / total)
    inner = grad_weight * (moment / total + (top - logit)) / width
    short = jnp.exp(logit - log_total) - 1.0
    inv = mine[:, 4:5]
    grad = grad_weight * (value + short * target_rows[...].astype(f32))
    gain_at = pl.multiple_of(place[3] * block, block)
    scaled = grad * gain[:, pl.ds(gain_at, block)]
    message[:, :block] = (inv * (scaled - unit[...] * inner)).astype(bf16)
    message[:, block:] = split_columns([log_total - logit])


def project_body(nv, place, *refs):
    gathered, refs = refs[:nv], refs[nv:]
    weight, resid, loss_out, keep, send, whole, partial, here, sems = refs
    parts, part, _ = here.shape
    copies = [
        pltpu.make_async_copy(weight.at[pl.ds(k * part, part), :], here.at[k], sems.at[k])
        for k in range(parts)
    ]
    for copy in copies:
        copy.start()
    per = gathered[0].shape[0]
    block = whole.shape[1]
    loss_sum = jnp.zeros((1, 1), f32)
    for v in range(nv):
        src = lax.rem(place[0] - v + nv, nv)
        whole[pl.ds(pl.multiple_of(src * per, per), per), :] = gathered[v][:, :block]
        (column,) = joined_columns(gathered[v][:, block:], 1)
        loss_sum = loss_sum + jnp.sum(column, axis=0, keepdims=True)
    loss_out[...] = loss_sum / (nv * per)
    resid[...] = whole[...]
    for k in range(parts):
        copies[k].wait()
        partial[:, k * part : (k + 1) * part] = dot(whole[...], here[k], NT)
    cols = keep.shape[1]
    keep[...] = partial[:, pl.ds(pl.multiple_of(place[2] * cols, cols), cols)]
    send[...] = partial[:, pl.ds(pl.multiple_of((1 - place[2]) * cols, cols), cols)].astype(bf16)


def sum_body(keep, *refs):
    value = keep[...].astype(f32)
    for ref in refs[:-1]:
        value = value + ref[...].astype(f32)
    refs[-1][...] = value.astype(bf16)


def forward_body(
    loss_per, heads, group, heads_at_once, j, place, key_pos, query_pos, packed, p_own, p_rows, out, scratch
):
    nc = packed.shape[0]
    tokens = p_own.shape[1]
    loss = loss_per * nc
    key_width = heads * HEAD_SIZE
    score_scale = HEAD_SIZE ** (-0.5)
    ctx_at = place[3]
    own_at = pl.multiple_of(ctx_at * tokens, tokens)
    row_at = pl.multiple_of(ctx_at * loss_per, loss_per)
    key = jnp.concatenate(
        [packed[c, 0:tokens, j * HEAD_SIZE : (j + 1) * HEAD_SIZE] for c in range(nc)], axis=0
    )
    at = key_width + j * HEAD_SIZE
    value = jnp.concatenate(
        [packed[c, 0:tokens, at : at + HEAD_SIZE] for c in range(nc)], axis=0
    )
    for g0 in range(0, group, heads_at_once):
        stacked = []
        for g in range(g0, g0 + heads_at_once):
            stacked.append(query_of(packed, j * group + g, tokens, loss_per, key_width))
        query = jnp.concatenate(stacked, axis=0).astype(bf16)
        where_at = jnp.concatenate([query_pos[...]] * heads_at_once, axis=0)
        visible = key_pos[...] <= where_at
        scores = jnp.where(visible, dot(query, key, NT) * score_scale, masked_fill)
        top = jnp.max(scores, axis=1, keepdims=True)
        raw = jnp.where(visible, jnp.exp(scores - top), 0.0)
        prob = raw / jnp.sum(raw, axis=1, keepdims=True)
        scratch[...] = prob
        coarse = prob.astype(bf16)
        fine = (prob - coarse.astype(f32)).astype(bf16)
        first = g0 * loss
        n = heads_at_once * loss
        out[first : first + n, :] = dot(coarse, value, NN) + dot(fine, value, NN)
        p_own[first : first + n, :] = scratch[:, pl.ds(own_at, tokens)]
        for k in range(heads_at_once):
            p_rows[(g0 + k) * loss_per : (g0 + k + 1) * loss_per, :] = scratch[
                pl.ds(pl.multiple_of(k * loss + row_at, loss_per), loss_per), :
            ]


def query_of(packed, head, tokens, loss_per, key_width):
    lane = head * HEAD_SIZE
    b, at = lane // (2 * key_width), lane % (2 * key_width)
    parts = []
    for c in range(packed.shape[0]):
        block = packed[c, tokens:, at : at + HEAD_SIZE].astype(f32)
        parts.append(block[b * loss_per : (b + 1) * loss_per])
    return jnp.concatenate(parts, axis=0)


def backward_body(loss_per, heads, group, place, half, other, packed, *refs):
    attention = [refs[3 * j : 3 * j + 3] for j in range(heads)]
    query_grad, key_grad, value_grad, grad = refs[3 * heads :]
    nc = packed.shape[0]
    tokens = key_grad.shape[0]
    loss = loss_per * nc
    key_width = heads * HEAD_SIZE
    score_scale = HEAD_SIZE ** (-0.5)
    ctx_at = place[3]
    cols = half.shape[1]
    grad[:, pl.ds(pl.multiple_of(place[2] * cols, cols), cols)] = half[...].astype(f32)
    grad[:, pl.ds(pl.multiple_of((1 - place[2]) * cols, cols), cols)] = other[...].astype(f32)
    mine_at = pl.multiple_of(ctx_at * loss_per, loss_per)
    for j in range(heads):
        p_own, p_rows, out = attention[j]
        lanes = [slice((j * group + g) * HEAD_SIZE, (j * group + g + 1) * HEAD_SIZE) for g in range(group)]
        d_out = jnp.concatenate([grad[:, s] for s in lanes], axis=0)
        d_half = d_out.astype(bf16)
        delta = jnp.sum(d_out * out[...], axis=1, keepdims=True)
        query = jnp.concatenate(
            [query_of(packed, j * group + g, tokens, loss_per, key_width) for g in range(group)], axis=0
        ).astype(bf16)
        at = key_width + j * HEAD_SIZE
        own_value = packed[ctx_at, 0:tokens, at : at + HEAD_SIZE]
        prob = p_own[...]
        score_grad = (prob * (dot(d_half, own_value, NT) - delta)).astype(bf16)
        k_lanes = slice(j * HEAD_SIZE, (j + 1) * HEAD_SIZE)
        key_grad[:, k_lanes] = (dot(score_grad, query, TN) * score_scale).astype(bf16)
        value_grad[:, k_lanes] = dot(prob.astype(bf16), d_half, TN).astype(bf16)
        key = jnp.concatenate([packed[c, 0:tokens, k_lanes] for c in range(nc)], axis=0)
        value = jnp.concatenate([packed[c, 0:tokens, at : at + HEAD_SIZE] for c in range(nc)], axis=0)
        d_mine = jnp.concatenate([grad[pl.ds(mine_at, loss_per), s] for s in lanes], axis=0)
        out_mine = jnp.concatenate(
            [
                out[pl.ds(pl.multiple_of(g * loss + mine_at, loss_per), loss_per), :]
                for g in range(group)
            ],
            axis=0,
        )
        delta = jnp.sum(d_mine * out_mine, axis=1, keepdims=True)
        d_prob = dot(d_mine.astype(bf16), value, NT)
        score_grad = (p_rows[...] * (d_prob - delta)).astype(bf16)
        result = dot(score_grad, key, NN) * score_scale
        for g in range(group):
            query_grad[:, lanes[g]] = result[g * loss_per : (g + 1) * loss_per].astype(bf16)


def per_device(
    hidden,
    norm_gain,
    head_weight,
    targets,
    loss_rows,
    stretch_of_slot,
    queries,
    key_states,
    attention_values,
    output_weight,
):
    nc = lax.axis_size("ctx")
    nv = lax.axis_size("vocab")
    nz = nc // CORES
    ctx_at = lax.axis_index("ctx")
    vocab_at = lax.axis_index("vocab")
    tokens = hidden.shape[0]
    stretch_len = tokens // 2
    loss = loss_rows.shape[0]
    loss_per = loss // nc
    width = norm_gain.shape[0]
    voc_rows = head_weight.shape[0]
    part_width = hidden.shape[1]
    query_width = queries.shape[1]
    key_width = key_states.shape[1]
    heads = key_width // HEAD_SIZE
    group = query_width // key_width
    block_width = width // nc
    per_vocab = loss // nv
    all_tokens = tokens * nc

    first_id = (vocab_at * nc + ctx_at) * voc_rows
    place = jnp.stack([vocab_at, ctx_at // CORES, ctx_at % CORES, ctx_at, first_id]).astype(jnp.int32)

    slots = stretch_of_slot.shape[0]
    owner = lax.broadcasted_iota(jnp.int32, (loss, 1), 0) // loss_per
    slot = 2 * owner + loss_rows[:, None] // stretch_len
    slot_iota = lax.broadcasted_iota(jnp.int32, (1, slots), 1)
    stretch = jnp.sum(jnp.where(slot == slot_iota, stretch_of_slot[None, :], 0), axis=1, keepdims=True)
    query_pos = stretch * stretch_len + loss_rows[:, None] % stretch_len
    key_pos = (
        stretch_of_slot[:, None] * stretch_len
        + lax.broadcasted_iota(jnp.int32, (1, stretch_len), 1)
    ).reshape(1, all_tokens)
    picked = call(
        functools.partial(pick_body, loss_per),
        shape((2 * loss_per, part_width // 2), bf16),
        [smem(), smem(), hbm()],
        [pltpu.VMEM((tokens, part_width), bf16), pltpu.SemaphoreType.DMA],
    )(place, loss_rows, hidden)
    picked, queries, targets_late = lax.optimization_barrier((picked, queries, targets))
    extra = (query_width // (2 * key_width)) * loss_per
    packed = call(
        functools.partial(pack_body, loss_per),
        shape((tokens + extra, 2 * key_width), bf16),
        [smem(), smem()] + [vmem()] * 3,
        moved=2 * queries.size,
    )(place, loss_rows, queries, key_states, attention_values)
    by_z = jnp.stack([picked] + [shifted(picked, "ctx", s, CORES) for s in range(1, nz)])
    planes = [by_z] + [shifted(by_z, "vocab", s) for s in range(1, nv)]
    if voc_rows % 16:
        local = targets_late - first_id
        is_local = (local >= 0) & (local < voc_rows)
        target_rows = head_weight.at[jnp.clip(local, 0, voc_rows - 1)].get(mode="promise_in_bounds")
        target_rows = jnp.where(is_local[:, None], target_rows, jnp.zeros((), bf16))
        target_rows = target_rows.reshape(loss, nc, block_width).transpose(1, 0, 2)
    else:
        target_rows = pl.pallas_call(
            target_body,
            out_shape=shape((nc, loss, block_width), bf16),
            in_specs=[smem(), vmem(), pl.BlockSpec(memory_space=pl.ANY)],
            out_specs=vmem(),
            scratch_shapes=[
                pltpu.VMEM((loss, 16, width), bf16),
                pltpu.SMEM((2, loss), jnp.int32),
                pltpu.SemaphoreType.DMA((loss,)),
            ],
            compiler_params=pltpu.CompilerParams(vmem_limit_bytes=40 * 2**20),
            cost_estimate=pl.CostEstimate(
                flops=0, bytes_accessed=2 * 16 * loss * width, transcendentals=0
            ),
        )(place, targets_late.reshape(1, loss), head_weight)
    planes, target_rows = lax.optimization_barrier((planes, target_rows))
    by_plane = jnp.stack(planes)
    other = swapped(by_plane)
    target_rows = lax.psum_scatter(
        target_rows.reshape(nc * loss, block_width), "ctx", scatter_dimension=0, tiled=True
    )
    other, packed = lax.optimization_barrier((other, packed))
    packed_all = lax.all_gather(packed, "ctx")

    first = voc_rows % CHUNK
    if voc_rows < SLOTS * CHUNK or first % 16 or not first:
        first = voc_rows if voc_rows < SLOTS * CHUNK else CHUNK
    chunks = (voc_rows - first) // CHUNK
    gain = norm_gain.reshape(1, width)
    keep, send, stats, unit = pl.pallas_call(
        functools.partial(flash_body, first),
        out_shape=(
            shape((nz, loss, block_width), f32),
            shape((loss, nz * block_width + LANES), bf16),
            shape((loss, LANES), f32),
            shape((per_vocab, block_width), f32),
        ),
        in_specs=[smem()] + [vmem()] * 4 + [pl.BlockSpec(memory_space=pl.ANY)],
        out_specs=[vmem()] * 4,
        scratch_shapes=[
            pltpu.VMEM((loss, width), bf16),
            pltpu.VMEM((loss, width), bf16),
            pltpu.VMEM((nc, loss, block_width), f32),
            pltpu.VMEM((loss, CHUNK), bf16),
            pltpu.VMEM((loss, LANES), f32),
            pltpu.VMEM((first, width), bf16),
            pltpu.VMEM((SLOTS if chunks else 1, CHUNK if chunks else 16, width), bf16),
            pltpu.SemaphoreType.DMA,
            pltpu.SemaphoreType.DMA((SLOTS,)),
        ],
        compiler_params=pltpu.CompilerParams(vmem_limit_bytes=50 * 2**20),
        cost_estimate=pl.CostEstimate(
            flops=4 * max(loss, 256) * width * voc_rows,
            bytes_accessed=4 * width * voc_rows,
            transcendentals=loss * voc_rows,
        ),
    )(place, by_plane, other, gain, targets.reshape(loss, 1), head_weight)

    send, target_rows = lax.optimization_barrier((send, target_rows))
    got = swapped(send)
    stats, keep, target_rows, *sends = call(
        functools.partial(core_body, nv - 1),
        (
            shape((per_vocab, LANES), f32),
            shape((nz, per_vocab, block_width), f32),
            shape((per_vocab, block_width), bf16),
        )
        + (shape((per_vocab, (nz + 1) * block_width + LANES), bf16),) * (nv - 1),
        [smem()] + [vmem()] * 3 + [hbm()],
        [
            pltpu.VMEM((nz, loss, block_width), f32),
            pltpu.VMEM((loss, LANES), f32),
            pltpu.VMEM((loss, LANES), bf16),
            pltpu.VMEM((loss, block_width), bf16),
            pltpu.SemaphoreType.DMA,
        ],
    )(place, keep, got, stats, target_rows)
    got = [shifted(sends[s - 1], "vocab", s) for s in range(1, nv)]

    at_once = max(1, min(group, (4 * 2**20) // (loss * all_tokens * 4)))

    def forward(j, query_pos):
        return call(
            functools.partial(forward_body, loss_per, heads, group, at_once, j),
            (
                shape((group * loss, tokens), f32),
                shape((group * loss_per, all_tokens), f32),
                shape((group * loss, HEAD_SIZE), f32),
            ),
            [smem()] + [vmem()] * 3,
            [pltpu.VMEM((at_once * loss, all_tokens), f32)],
            limit=40,
            flops=24 * group * loss * all_tokens * HEAD_SIZE,
            moved=2 * packed_all.size,
            exps=group * loss * all_tokens,
        )(place, key_pos, query_pos, packed_all)

    stats, packed_all = lax.optimization_barrier((stats, packed_all))
    stats, keep, target_rows, *sends = call(
        functools.partial(plane_body, nv - 1),
        (
            shape((per_vocab, LANES), f32),
            shape((per_vocab, block_width), f32),
            shape((per_vocab, block_width), bf16),
        )
        + (shape((per_vocab, block_width + LANES), bf16),) * (nz - 1),
        [smem()] + [vmem()] * (3 + nv - 1),
        [pltpu.VMEM((nz, per_vocab, block_width), f32)],
    )(place, keep, stats, target_rows, *got)
    got = [shifted(sends[s - 1], "ctx", s, CORES) for s in range(1, nz)]
    message = call(
        functools.partial(line_body, nz - 1, width),
        shape((per_vocab, block_width + LANES), bf16),
        [smem()] + [vmem()] * (5 + nz - 1),
    )(place, keep, stats, target_rows, unit, gain, *got)

    gathered = [message] + [shifted(message, "vocab", s) for s in range(1, nv)]
    cols = query_width // CORES
    resid_rows, mean_loss, keep, send = call(
        functools.partial(project_body, nv),
        (
            shape((loss, block_width), bf16),
            shape((1, 1), f32),
            shape((loss, cols), f32),
            shape((loss, cols), bf16),
        ),
        [smem()] + [vmem()] * nv + [hbm()],
        [
            pltpu.VMEM((loss, block_width), bf16),
            pltpu.VMEM((loss, query_width), f32),
            pltpu.VMEM((4, query_width // 4, block_width), bf16),
            pltpu.SemaphoreType.DMA((4,)),
        ],
    )(place, *gathered, output_weight)
    half = call(sum_body, shape((loss, cols), bf16), [vmem()] * 2)(keep, swapped(send))
    windows = nz.bit_length() - 1
    attention = [None] * heads
    for k in range(windows):
        got = crossed(half, 2**k)
        here = range(k, heads, windows)
        half, query_pos = lax.optimization_barrier((half, query_pos))
        made = [forward(j, query_pos) for j in here]
        half, made = lax.optimization_barrier((half, made))
        for j, result in zip(here, made):
            attention[j] = result
        half = call(sum_body, shape((loss, cols), bf16), [vmem()] * 2)(half, got)
    other = swapped(half)
    query_grad, key_grad, value_grad = call(
        functools.partial(backward_body, loss_per, heads, group),
        (
            shape((loss_per, query_width), bf16),
            shape((tokens, key_width), bf16),
            shape((tokens, key_width), bf16),
        ),
        [smem()] + [vmem()] * (3 + 3 * heads),
        [pltpu.VMEM((loss, query_width), f32)],
    )(place, half, other, packed_all, *jax.tree.leaves(attention))
    return (mean_loss.reshape(()), query_grad, key_grad, value_grad, resid_rows.T)


def solution(mesh):
    placed = (
        P("ctx", "vocab"),
        P(),
        P(("vocab", "ctx"), None),
        P(),
        P(),
        P(),
        P("ctx", "vocab"),
        P("ctx", "vocab"),
        P("ctx", "vocab"),
        P("vocab", "ctx"),
    )
    return jax.shard_map(
        per_device,
        mesh=mesh,
        in_specs=placed,
        out_specs=(P(), P("ctx", "vocab"), P("ctx", "vocab"), P("ctx", "vocab"), P("ctx", None)),
        check_vma=False,
    )
```

```python
import functools

import jax
import jax.numpy as jnp
from jax import lax
from jax.experimental import pallas as pl
from jax.experimental.pallas import tpu as pltpu
from jax.sharding import PartitionSpec as P

HEAD_SIZE = 128
CORES = 2
CHUNK = 512
SLOTS = 3
LANES = 128

norm_eps = 1e-06
grad_weight = 16.0
masked_fill = -1e30

f32 = jnp.float32
bf16 = jnp.bfloat16

NT = (((1,), (1,)), ((), ()))
NN = (((1,), (0,)), ((), ()))
TN = (((0,), (0,)), ((), ()))


def dot(a, b, dims):
    return lax.dot_general(a, b, dims, preferred_element_type=f32)


def smem():
    return pl.BlockSpec(memory_space=pltpu.SMEM)


def hbm():
    return pl.BlockSpec(memory_space=pltpu.HBM)


def vmem():
    return pl.BlockSpec(memory_space=pltpu.VMEM)


def shape(dims, dtype):
    return jax.ShapeDtypeStruct(dims, dtype)


def call(body, outs, ins, scratch=(), limit=16, flops=0, moved=0, exps=0):
    return pl.pallas_call(
        body,
        out_shape=outs,
        in_specs=ins,
        out_specs=jax.tree.map(lambda _: vmem(), outs),
        scratch_shapes=list(scratch),
        compiler_params=pltpu.CompilerParams(vmem_limit_bytes=limit * 2**20),
        cost_estimate=pl.CostEstimate(flops=flops, bytes_accessed=moved, transcendentals=exps),
    )


def shifted(value, axis, step, inner=1):
    size = lax.axis_size(axis)
    outer = size // inner
    pairs = [(i, ((i // inner + step) % outer) * inner + i % inner) for i in range(size)]
    return lax.ppermute(value, axis, pairs)


def crossed(value, bit):
    size = lax.axis_size("ctx")
    return lax.ppermute(value, "ctx", [(i, i ^ (bit * CORES)) for i in range(size)])


def swapped(value):
    size = lax.axis_size("ctx")
    return lax.ppermute(value, "ctx", [(i, i ^ 1) for i in range(size)])


def row_choice(loss_per, tokens, place, rows):
    base = place[3] * loss_per
    row_iota = lax.broadcasted_iota(jnp.int32, (loss_per, tokens), 0)
    col_iota = lax.broadcasted_iota(jnp.int32, (loss_per, tokens), 1)
    sel = jnp.zeros((loss_per, tokens), f32)
    for j in range(loss_per):
        sel = jnp.where((row_iota == j) & (col_iota == rows[base + j]), 1.0, sel)
    return sel.astype(bf16)


def pick_body(loss_per, place, rows, hidden, picked, here, sem):
    tokens, width = hidden.shape
    copy = pltpu.make_async_copy(hidden, here, sem)
    copy.start()
    choice = row_choice(loss_per, tokens, place, rows)
    copy.wait()
    mine = dot(choice, here[...], NN)
    half = width // 2
    picked[...] = jnp.concatenate([mine[:, :half], mine[:, half:]], axis=0).astype(bf16)


def pack_body(loss_per, place, rows, queries, keys, values, packed):
    tokens, key_width = keys.shape
    mine = dot(row_choice(loss_per, tokens, place, rows), queries[...], NN)
    packed[0:tokens, 0:key_width] = keys[...]
    packed[0:tokens, key_width : 2 * key_width] = values[...]
    parts = queries.shape[1] // (2 * key_width)
    stacked = [mine[:, b * 2 * key_width : (b + 1) * 2 * key_width] for b in range(parts)]
    packed[tokens : tokens + parts * loss_per, :] = jnp.concatenate(stacked, axis=0).astype(bf16)


def target_body(place, targets, weight, out, buf, spots, sems):
    blocks, loss, block_width = out.shape
    width = blocks * block_width
    total_rows = weight.shape[0]
    offset = targets[...] - place[4]
    local = (offset >= 0) & (offset < total_rows)
    offset = offset.astype(f32)
    index = lax.broadcasted_iota(jnp.int32, (1, loss), 1).astype(f32)
    none = float(loss)
    count = jnp.sum(jnp.where(local, 1.0, 0.0)).astype(jnp.int32)

    def copy(k, at):
        start = pl.multiple_of(lax.div(at, 16) * 16, 16)
        return pltpu.make_async_copy(weight.at[pl.ds(start, 16), :], buf.at[k], sems.at[k])

    def begin(k, left):
        spot = jnp.min(left)
        at = jnp.sum(jnp.where(index == spot, offset, 0.0)).astype(jnp.int32)
        spots[0, k] = spot.astype(jnp.int32)
        spots[1, k] = at
        copy(k, at).start()
        return jnp.where(index == spot, none, left)

    lax.fori_loop(0, count, begin, jnp.where(local, index, none))
    out[...] = jnp.zeros_like(out)
    line = lax.broadcasted_iota(jnp.int32, (16, block_width), 0)

    @pl.loop(0, count)
    def _(k):
        spot, at = spots[0, k], spots[1, k]
        copy(k, at).wait()
        group = pl.ds(pl.multiple_of(lax.div(spot, 16) * 16, 16), 16)
        for b in range(blocks):
            block = buf[k, :, b * block_width : (b + 1) * block_width].astype(f32)
            row = jnp.sum(jnp.where(line == lax.rem(at, 16), block, 0.0), axis=0, keepdims=True)
            before = out[b, group, :].astype(f32)
            out[b, group, :] = jnp.where(line == lax.rem(spot, 16), row, before).astype(bf16)


def flash_body(
    first,
    place,
    own,
    other,
    gain,
    targets,
    weight,
    keep,
    send,
    stats,
    unit,
    normed,
    raw,
    acc,
    probs,
    state,
    head_buf,
    buf,
    head_sem,
    sems,
):
    vocab_at, z_at, core_at, ctx_at, first_id = (place[k] for k in range(5))
    nv, nz = own.shape[0], own.shape[1]
    loss, width = normed.shape
    half = own.shape[3]
    total_rows = weight.shape[0]
    chunks = (total_rows - first) // CHUNK
    blocks = acc.shape[0]
    block_width = width // blocks

    def head_copy():
        return pltpu.make_async_copy(weight.at[pl.ds(0, first), :], head_buf, head_sem)

    def body_copy(c):
        slot = lax.rem(c, SLOTS)
        start = pl.multiple_of(first + c * CHUNK, 16)
        return pltpu.make_async_copy(
            weight.at[pl.ds(start, CHUNK), :], buf.at[slot], sems.at[slot]
        )

    head_copy().start()
    for c in range(min(SLOTS, chunks)):
        body_copy(c).start()

    is_even = core_at == 0
    for zr in range(nz):
        z_src = lax.rem(z_at - zr + nz, nz)
        square_own = jnp.zeros((8, 1), f32)
        square_other = jnp.zeros((8, 1), f32)
        for vr in range(nv):
            a = own[vr, zr].astype(f32)
            b = other[vr, zr].astype(f32)
            square_a = jnp.sum(a * a, axis=1, keepdims=True)
            square_b = jnp.sum(b * b, axis=1, keepdims=True)
            square_own += square_a[:8] + square_a[8:]
            square_other += square_b[:8] + square_b[8:]
        square = jnp.concatenate(
            [
                jnp.where(is_even, square_own, square_other),
                jnp.where(is_even, square_other, square_own),
            ],
            axis=0,
        )
        inv = lax.rsqrt(square / width + norm_eps)
        row_at = pl.multiple_of(z_src * 16, 16)
        state[pl.ds(row_at, 16), :] = jnp.broadcast_to(inv, (16, LANES))
        for vr in range(nv):
            v_src = lax.rem(vocab_at - vr + nv, nv)
            a = own[vr, zr].astype(f32)
            b = other[vr, zr].astype(f32)
            low = jnp.where(is_even, a, b)
            high = jnp.where(is_even, b, a)
            for k in range(2):
                x = jnp.concatenate([low[8 * k : 8 * k + 8], high[8 * k : 8 * k + 8]], axis=0)
                lane_at = pl.multiple_of((v_src * 2 + k) * half, half)
                raw[pl.ds(row_at, 16), pl.ds(lane_at, half)] = x.astype(bf16)
                normed[pl.ds(row_at, 16), pl.ds(lane_at, half)] = (
                    x * inv * gain[:, pl.ds(lane_at, half)]
                ).astype(bf16)

    per_vocab = loss // nv
    mine_at = pl.multiple_of(vocab_at * per_vocab, per_vocab)
    feature_at = pl.multiple_of(ctx_at * block_width, block_width)
    unit[...] = (
        raw[pl.ds(mine_at, per_vocab), pl.ds(feature_at, block_width)].astype(f32)
        * state[pl.ds(mine_at, per_vocab), 0:1]
    )

    target_col = targets[...]

    def softmax(scores, base, before):
        cols = scores.shape[1]
        ids = base + lax.broadcasted_iota(jnp.int32, (loss, cols), 1)
        hit = ids == target_col
        top = jnp.max(scores, axis=1, keepdims=True)
        if before is not None:
            top = jnp.maximum(top, before[0])
        shifted_scores = scores - top
        weights = jnp.exp(shifted_scores)
        total = jnp.sum(weights, axis=1, keepdims=True)
        moment = jnp.sum(weights * shifted_scores, axis=1, keepdims=True)
        logit = jnp.sum(jnp.where(hit, scores, 0.0), axis=1, keepdims=True)
        scale = None
        if before is not None:
            gap = before[0] - top
            scale = jnp.exp(gap)
            total = total + before[1] * scale
            moment = moment + scale * (before[2] + gap * before[1])
            logit = logit + before[3]
        masked = jnp.where(hit, 0.0, weights).astype(bf16)
        return masked, scale, (top, total, moment, logit)

    def scores_of(block):
        return dot(block, normed[...], NT).T

    def add_product(p, scale, read):
        for b in range(blocks):
            part = dot(p, read(b * block_width, block_width), NN)
            if scale is None:
                acc[b] = part
            else:
                acc[b] = acc[b] * scale + part

    def part(ref, slot):
        return lambda at, n: ref[slot, :, at : at + n]

    head_copy().wait()
    p, _, run = softmax(scores_of(head_buf[...]), first_id, None)
    if not chunks:
        add_product(p, None, lambda at, n: head_buf[:, at : at + n])
    else:
        def start_of(c):
            return first_id + first + c * CHUNK

        body_copy(0).wait()
        scores = scores_of(buf[0])
        add_product(p, None, lambda at, n: head_buf[:, at : at + n])
        p, scale, run = softmax(scores, start_of(0), run)
        probs[...] = p

        def step(c, carry):
            scale, run = carry
            body_copy(c).wait()
            scores = scores_of(buf[lax.rem(c, SLOTS)])
            add_product(probs[...], scale, part(buf, lax.rem(c - 1, SLOTS)))
            p, scale, run = softmax(scores, start_of(c), run)
            probs[...] = p

            @pl.when(c + 2 < chunks)
            def _():
                body_copy(c + 2).start()

            return scale, run

        scale, run = lax.fori_loop(1, chunks, step, (scale, run))
        add_product(probs[...], scale, part(buf, (chunks - 1) % SLOTS))

    for z in range(nz):
        keep[z] = acc[CORES * z + core_at]
        send[:, z * block_width : (z + 1) * block_width] = acc[CORES * z + 1 - core_at].astype(bf16)
    send[:, nz * block_width :] = split_columns(run)
    stats[...] = with_stats(state[...], run)


def split_columns(columns):
    rows = columns[0].shape[0]
    lane = lax.broadcasted_iota(jnp.int32, (rows, LANES), 1)
    table = jnp.zeros((rows, LANES), f32)
    for k, column in enumerate(columns):
        rest = column
        for j in range(3):
            term = rest.astype(bf16).astype(f32)
            table = jnp.where(lane == 3 * k + j, term, table)
            rest = rest - term
    return table.astype(bf16)


def joined_columns(block, count):
    block = block.astype(f32)
    return [
        block[:, 3 * k : 3 * k + 1] + block[:, 3 * k + 1 : 3 * k + 2] + block[:, 3 * k + 2 : 3 * k + 3]
        for k in range(count)
    ]


def stats_of(table):
    return [table[:, k : k + 1] for k in range(4)]


def merge_stats(columns):
    top = functools.reduce(jnp.maximum, [c[0] for c in columns])
    gaps = [c[0] - top for c in columns]
    scales = [jnp.exp(g) for g in gaps]
    total = sum(s * c[1] for s, c in zip(scales, columns))
    moment = sum(s * (c[2] + g * c[1]) for s, g, c in zip(scales, gaps, columns))
    logit = sum(c[3] for c in columns)
    return scales, (top, total, moment, logit)


def with_stats(table, merged):
    lane = lax.broadcasted_iota(jnp.int32, table.shape, 1)
    for k in range(4):
        table = jnp.where(lane == k, merged[k], table)
    return table


def core_body(count, place, keep, got, mine, target_rows, new_stats, new_keep, new_rows, *rest):
    sends, (total, table, message) = rest[:count], rest[count:]
    nz, loss, block = keep.shape
    columns = [stats_of(mine[...]), joined_columns(got[:, nz * block :], 4)]
    scales, merged = merge_stats(columns)
    table[...] = with_stats(mine[...], merged)
    message[...] = split_columns(merged)
    per = loss // (count + 1)
    for z in range(nz):
        other = got[:, z * block : (z + 1) * block].astype(f32)
        total[z] = keep[z] * scales[0] + other * scales[1]
    at = pl.multiple_of(place[0] * per, per)
    new_stats[...] = table[pl.ds(at, per), :]
    new_keep[...] = total[:, pl.ds(at, per), :]
    for s in range(count):
        to = lax.rem(place[0] + s + 1, count + 1)
        rows = pl.ds(pl.multiple_of(to * per, per), per)
        for z in range(nz):
            sends[s][:, z * block : (z + 1) * block] = total[z, rows, :].astype(bf16)
        sends[s][:, (nz + 1) * block :] = message[rows, :]
    for s in range(count):
        to = lax.rem(place[0] + s + 1, count + 1)
        rows = pl.ds(pl.multiple_of(to * per, per), per)
        sends[s][:, nz * block : (nz + 1) * block] = target_rows[rows, :]
    new_rows[...] = target_rows[pl.ds(at, per), :]


def plane_body(count, place, keep, mine, target_rows, *rest):
    got, rest = rest[:count], rest[count:]
    new_stats, new_keep, new_target = rest[:3]
    sends, (total,) = rest[3:-1], rest[-1:]
    nz, per, block = keep.shape
    columns = [stats_of(mine[...])] + [joined_columns(g[:, (nz + 1) * block :], 4) for g in got]
    scales, merged = merge_stats(columns)
    new_stats[...] = with_stats(mine[...], merged)
    message = split_columns(merged)
    for z in range(nz):
        value = keep[z] * scales[0]
        for k in range(count):
            value = value + got[k][:, z * block : (z + 1) * block].astype(f32) * scales[k + 1]
        total[z] = value
    new_keep[...] = total[place[1]]
    rows = target_rows[...].astype(f32)
    for k in range(count):
        rows = rows + got[k][:, nz * block : (nz + 1) * block].astype(f32)
    new_target[...] = rows.astype(bf16)
    for s in range(nz - 1):
        sends[s][:, :block] = total[lax.rem(place[1] + s + 1, nz)].astype(bf16)
        sends[s][:, block:] = message


def line_body(count, width, place, keep, mine, target_rows, unit, gain, *rest):
    got, (message,) = rest[:count], rest[count:]
    per, block = keep.shape
    columns = [stats_of(mine[...])] + [joined_columns(g[:, block:], 4) for g in got]
    scales, (top, total, moment, logit) = merge_stats(columns)
    log_total = top + jnp.log(total)
    value = keep[...] * (scales[0] / total)
    for k in range(count):
        value = value + got[k][:, :block].astype(f32) * (scales[k + 1] / total)
    inner = grad_weight * (moment / total + (top - logit)) / width
    short = jnp.exp(logit - log_total) - 1.0
    inv = mine[:, 4:5]
    grad = grad_weight * (value + short * target_rows[...].astype(f32))
    gain_at = pl.multiple_of(place[3] * block, block)
    scaled = grad * gain[:, pl.ds(gain_at, block)]
    message[:, :block] = (inv * (scaled - unit[...] * inner)).astype(bf16)
    message[:, block:] = split_columns([log_total - logit])


def project_body(nv, place, *refs):
    gathered, refs = refs[:nv], refs[nv:]
    weight, resid, loss_out, keep, send, whole, partial = refs
    per = gathered[0].shape[0]
    block = whole.shape[1]
    loss_sum = jnp.zeros((1, 1), f32)
    for v in range(nv):
        src = lax.rem(place[0] - v + nv, nv)
        whole[pl.ds(pl.multiple_of(src * per, per), per), :] = gathered[v][:, :block]
        (column,) = joined_columns(gathered[v][:, block:], 1)
        loss_sum = loss_sum + jnp.sum(column, axis=0, keepdims=True)
    loss_out[...] = loss_sum / (nv * per)
    resid[...] = whole[...]
    partial[...] = dot(whole[...], weight[...], NT)
    cols = keep.shape[1]
    keep[...] = partial[:, pl.ds(pl.multiple_of(place[2] * cols, cols), cols)]
    send[...] = partial[:, pl.ds(pl.multiple_of((1 - place[2]) * cols, cols), cols)].astype(bf16)


def stage_body(source, staged, sem):
    copy = pltpu.make_async_copy(source, staged, sem)
    copy.start()
    copy.wait()


def staged(value):
    return call(
        stage_body,
        shape(value.shape, value.dtype),
        [hbm()],
        [pltpu.SemaphoreType.DMA],
        moved=2 * value.size * value.dtype.itemsize,
    )(value)


def sum_body(keep, *refs):
    value = keep[...].astype(f32)
    for ref in refs[:-1]:
        value = value + ref[...].astype(f32)
    refs[-1][...] = value.astype(bf16)


def forward_body(
    loss_per, heads, group, heads_at_once, j, place, key_pos, query_pos, packed, p_own, p_rows, out, scratch
):
    nc = packed.shape[0]
    tokens = p_own.shape[1]
    loss = loss_per * nc
    key_width = heads * HEAD_SIZE
    score_scale = HEAD_SIZE ** (-0.5)
    ctx_at = place[3]
    own_at = pl.multiple_of(ctx_at * tokens, tokens)
    row_at = pl.multiple_of(ctx_at * loss_per, loss_per)
    key = jnp.concatenate(
        [packed[c, 0:tokens, j * HEAD_SIZE : (j + 1) * HEAD_SIZE] for c in range(nc)], axis=0
    )
    at = key_width + j * HEAD_SIZE
    value = jnp.concatenate(
        [packed[c, 0:tokens, at : at + HEAD_SIZE] for c in range(nc)], axis=0
    )
    for g0 in range(0, group, heads_at_once):
        stacked = []
        for g in range(g0, g0 + heads_at_once):
            stacked.append(query_of(packed, j * group + g, tokens, loss_per, key_width))
        query = jnp.concatenate(stacked, axis=0).astype(bf16)
        where_at = jnp.concatenate([query_pos[...]] * heads_at_once, axis=0)
        visible = key_pos[...] <= where_at
        scores = jnp.where(visible, dot(query, key, NT) * score_scale, masked_fill)
        top = jnp.max(scores, axis=1, keepdims=True)
        raw = jnp.where(visible, jnp.exp(scores - top), 0.0)
        prob = raw / jnp.sum(raw, axis=1, keepdims=True)
        scratch[...] = prob
        coarse = prob.astype(bf16)
        fine = (prob - coarse.astype(f32)).astype(bf16)
        first = g0 * loss
        n = heads_at_once * loss
        out[first : first + n, :] = dot(coarse, value, NN) + dot(fine, value, NN)
        p_own[first : first + n, :] = scratch[:, pl.ds(own_at, tokens)]
        for k in range(heads_at_once):
            p_rows[(g0 + k) * loss_per : (g0 + k + 1) * loss_per, :] = scratch[
                pl.ds(pl.multiple_of(k * loss + row_at, loss_per), loss_per), :
            ]


def query_of(packed, head, tokens, loss_per, key_width):
    lane = head * HEAD_SIZE
    b, at = lane // (2 * key_width), lane % (2 * key_width)
    parts = []
    for c in range(packed.shape[0]):
        block = packed[c, tokens:, at : at + HEAD_SIZE].astype(f32)
        parts.append(block[b * loss_per : (b + 1) * loss_per])
    return jnp.concatenate(parts, axis=0)


def backward_body(loss_per, heads, group, place, half, other, packed, *refs):
    attention = [refs[3 * j : 3 * j + 3] for j in range(heads)]
    query_grad, key_grad, value_grad, grad = refs[3 * heads :]
    nc = packed.shape[0]
    tokens = key_grad.shape[0]
    loss = loss_per * nc
    key_width = heads * HEAD_SIZE
    score_scale = HEAD_SIZE ** (-0.5)
    ctx_at = place[3]
    cols = half.shape[1]
    grad[:, pl.ds(pl.multiple_of(place[2] * cols, cols), cols)] = half[...].astype(f32)
    grad[:, pl.ds(pl.multiple_of((1 - place[2]) * cols, cols), cols)] = other[...].astype(f32)
    mine_at = pl.multiple_of(ctx_at * loss_per, loss_per)
    for j in range(heads):
        p_own, p_rows, out = attention[j]
        lanes = [slice((j * group + g) * HEAD_SIZE, (j * group + g + 1) * HEAD_SIZE) for g in range(group)]
        d_out = jnp.concatenate([grad[:, s] for s in lanes], axis=0)
        d_half = d_out.astype(bf16)
        delta = jnp.sum(d_out * out[...], axis=1, keepdims=True)
        query = jnp.concatenate(
            [query_of(packed, j * group + g, tokens, loss_per, key_width) for g in range(group)], axis=0
        ).astype(bf16)
        at = key_width + j * HEAD_SIZE
        own_value = packed[ctx_at, 0:tokens, at : at + HEAD_SIZE]
        prob = p_own[...]
        score_grad = (prob * (dot(d_half, own_value, NT) - delta)).astype(bf16)
        k_lanes = slice(j * HEAD_SIZE, (j + 1) * HEAD_SIZE)
        key_grad[:, k_lanes] = (dot(score_grad, query, TN) * score_scale).astype(bf16)
        value_grad[:, k_lanes] = dot(prob.astype(bf16), d_half, TN).astype(bf16)
        key = jnp.concatenate([packed[c, 0:tokens, k_lanes] for c in range(nc)], axis=0)
        value = jnp.concatenate([packed[c, 0:tokens, at : at + HEAD_SIZE] for c in range(nc)], axis=0)
        d_mine = jnp.concatenate([grad[pl.ds(mine_at, loss_per), s] for s in lanes], axis=0)
        out_mine = jnp.concatenate(
            [
                out[pl.ds(pl.multiple_of(g * loss + mine_at, loss_per), loss_per), :]
                for g in range(group)
            ],
            axis=0,
        )
        delta = jnp.sum(d_mine * out_mine, axis=1, keepdims=True)
        d_prob = dot(d_mine.astype(bf16), value, NT)
        score_grad = (p_rows[...] * (d_prob - delta)).astype(bf16)
        result = dot(score_grad, key, NN) * score_scale
        for g in range(group):
            query_grad[:, lanes[g]] = result[g * loss_per : (g + 1) * loss_per].astype(bf16)


def per_device(
    hidden,
    norm_gain,
    head_weight,
    targets,
    loss_rows,
    stretch_of_slot,
    queries,
    key_states,
    attention_values,
    output_weight,
):
    nc = lax.axis_size("ctx")
    nv = lax.axis_size("vocab")
    nz = nc // CORES
    ctx_at = lax.axis_index("ctx")
    vocab_at = lax.axis_index("vocab")
    tokens = hidden.shape[0]
    stretch_len = tokens // 2
    loss = loss_rows.shape[0]
    loss_per = loss // nc
    width = norm_gain.shape[0]
    voc_rows = head_weight.shape[0]
    part_width = hidden.shape[1]
    query_width = queries.shape[1]
    key_width = key_states.shape[1]
    heads = key_width // HEAD_SIZE
    group = query_width // key_width
    block_width = width // nc
    per_vocab = loss // nv
    all_tokens = tokens * nc

    first_id = (vocab_at * nc + ctx_at) * voc_rows
    place = jnp.stack([vocab_at, ctx_at // CORES, ctx_at % CORES, ctx_at, first_id]).astype(jnp.int32)

    slots = stretch_of_slot.shape[0]
    owner = lax.broadcasted_iota(jnp.int32, (loss, 1), 0) // loss_per
    slot = 2 * owner + loss_rows[:, None] // stretch_len
    slot_iota = lax.broadcasted_iota(jnp.int32, (1, slots), 1)
    stretch = jnp.sum(jnp.where(slot == slot_iota, stretch_of_slot[None, :], 0), axis=1, keepdims=True)
    query_pos = stretch * stretch_len + loss_rows[:, None] % stretch_len
    key_pos = (
        stretch_of_slot[:, None] * stretch_len
        + lax.broadcasted_iota(jnp.int32, (1, stretch_len), 1)
    ).reshape(1, all_tokens)
    picked = call(
        functools.partial(pick_body, loss_per),
        shape((2 * loss_per, part_width // 2), bf16),
        [smem(), smem(), hbm()],
        [pltpu.VMEM((tokens, part_width), bf16), pltpu.SemaphoreType.DMA],
    )(place, loss_rows, hidden)
    picked, queries, targets_late = lax.optimization_barrier((picked, queries, targets))
    extra = (query_width // (2 * key_width)) * loss_per
    packed = call(
        functools.partial(pack_body, loss_per),
        shape((tokens + extra, 2 * key_width), bf16),
        [smem(), smem()] + [vmem()] * 3,
        moved=2 * queries.size,
    )(place, loss_rows, queries, key_states, attention_values)
    by_z = jnp.stack([picked] + [shifted(picked, "ctx", s, CORES) for s in range(1, nz)])
    planes = [by_z] + [shifted(by_z, "vocab", s) for s in range(1, nv)]
    if voc_rows % 16:
        local = targets_late - first_id
        is_local = (local >= 0) & (local < voc_rows)
        target_rows = head_weight.at[jnp.clip(local, 0, voc_rows - 1)].get(mode="promise_in_bounds")
        target_rows = jnp.where(is_local[:, None], target_rows, jnp.zeros((), bf16))
        target_rows = target_rows.reshape(loss, nc, block_width).transpose(1, 0, 2)
    else:
        target_rows = pl.pallas_call(
            target_body,
            out_shape=shape((nc, loss, block_width), bf16),
            in_specs=[smem(), vmem(), pl.BlockSpec(memory_space=pl.ANY)],
            out_specs=vmem(),
            scratch_shapes=[
                pltpu.VMEM((loss, 16, width), bf16),
                pltpu.SMEM((2, loss), jnp.int32),
                pltpu.SemaphoreType.DMA((loss,)),
            ],
            compiler_params=pltpu.CompilerParams(vmem_limit_bytes=40 * 2**20),
            cost_estimate=pl.CostEstimate(
                flops=0, bytes_accessed=2 * 16 * loss * width, transcendentals=0
            ),
        )(place, targets_late.reshape(1, loss), head_weight)
    planes, target_rows = lax.optimization_barrier((planes, target_rows))
    by_plane = jnp.stack(planes)
    other = swapped(by_plane)
    target_rows = lax.psum_scatter(
        target_rows.reshape(nc * loss, block_width), "ctx", scatter_dimension=0, tiled=True
    )
    other, packed = lax.optimization_barrier((other, packed))
    packed_all = lax.all_gather(packed, "ctx")

    first = voc_rows % CHUNK
    if voc_rows < SLOTS * CHUNK or first % 16 or not first:
        first = voc_rows if voc_rows < SLOTS * CHUNK else CHUNK
    chunks = (voc_rows - first) // CHUNK
    gain = norm_gain.reshape(1, width)
    keep, send, stats, unit = pl.pallas_call(
        functools.partial(flash_body, first),
        out_shape=(
            shape((nz, loss, block_width), f32),
            shape((loss, nz * block_width + LANES), bf16),
            shape((loss, LANES), f32),
            shape((per_vocab, block_width), f32),
        ),
        in_specs=[smem()] + [vmem()] * 4 + [pl.BlockSpec(memory_space=pl.ANY)],
        out_specs=[vmem()] * 4,
        scratch_shapes=[
            pltpu.VMEM((loss, width), bf16),
            pltpu.VMEM((loss, width), bf16),
            pltpu.VMEM((nc, loss, block_width), f32),
            pltpu.VMEM((loss, CHUNK), bf16),
            pltpu.VMEM((loss, LANES), f32),
            pltpu.VMEM((first, width), bf16),
            pltpu.VMEM((SLOTS if chunks else 1, CHUNK if chunks else 16, width), bf16),
            pltpu.SemaphoreType.DMA,
            pltpu.SemaphoreType.DMA((SLOTS,)),
        ],
        compiler_params=pltpu.CompilerParams(vmem_limit_bytes=45 * 2**20),
        cost_estimate=pl.CostEstimate(
            flops=4 * max(loss, 256) * width * voc_rows,
            bytes_accessed=4 * width * voc_rows,
            transcendentals=loss * voc_rows,
        ),
    )(place, by_plane, other, gain, targets.reshape(loss, 1), head_weight)

    send, target_rows = lax.optimization_barrier((send, target_rows))
    got = swapped(send)
    target_rows = staged(target_rows)
    stats, keep, target_rows, *sends = call(
        functools.partial(core_body, nv - 1),
        (
            shape((per_vocab, LANES), f32),
            shape((nz, per_vocab, block_width), f32),
            shape((per_vocab, block_width), bf16),
        )
        + (shape((per_vocab, (nz + 1) * block_width + LANES), bf16),) * (nv - 1),
        [smem()] + [vmem()] * 4,
        [
            pltpu.VMEM((nz, loss, block_width), f32),
            pltpu.VMEM((loss, LANES), f32),
            pltpu.VMEM((loss, LANES), bf16),
        ],
    )(place, keep, got, stats, target_rows)
    got = [shifted(sends[s - 1], "vocab", s) for s in range(1, nv)]

    at_once = max(1, min(group, (4 * 2**20) // (loss * all_tokens * 4)))

    def forward(j, query_pos):
        return call(
            functools.partial(forward_body, loss_per, heads, group, at_once, j),
            (
                shape((group * loss, tokens), f32),
                shape((group * loss_per, all_tokens), f32),
                shape((group * loss, HEAD_SIZE), f32),
            ),
            [smem()] + [vmem()] * 3,
            [pltpu.VMEM((at_once * loss, all_tokens), f32)],
            limit=40,
            flops=24 * group * loss * all_tokens * HEAD_SIZE,
            moved=2 * packed_all.size,
            exps=group * loss * all_tokens,
        )(place, key_pos, query_pos, packed_all)

    stats, output_weight = lax.optimization_barrier((stats, output_weight))
    weight_here = staged(output_weight)
    stats, packed_all, weight_here = lax.optimization_barrier((stats, packed_all, weight_here))
    stats, keep, target_rows, *sends = call(
        functools.partial(plane_body, nv - 1),
        (
            shape((per_vocab, LANES), f32),
            shape((per_vocab, block_width), f32),
            shape((per_vocab, block_width), bf16),
        )
        + (shape((per_vocab, block_width + LANES), bf16),) * (nz - 1),
        [smem()] + [vmem()] * (3 + nv - 1),
        [pltpu.VMEM((nz, per_vocab, block_width), f32)],
    )(place, keep, stats, target_rows, *got)
    got = [shifted(sends[s - 1], "ctx", s, CORES) for s in range(1, nz)]
    message = call(
        functools.partial(line_body, nz - 1, width),
        shape((per_vocab, block_width + LANES), bf16),
        [smem()] + [vmem()] * (5 + nz - 1),
    )(place, keep, stats, target_rows, unit, gain, *got)

    gathered = [message] + [shifted(message, "vocab", s) for s in range(1, nv)]
    cols = query_width // CORES
    resid_rows, mean_loss, keep, send = call(
        functools.partial(project_body, nv),
        (
            shape((loss, block_width), bf16),
            shape((1, 1), f32),
            shape((loss, cols), f32),
            shape((loss, cols), bf16),
        ),
        [smem()] + [vmem()] * (nv + 1),
        [pltpu.VMEM((loss, block_width), bf16), pltpu.VMEM((loss, query_width), f32)],
    )(place, *gathered, weight_here)
    half = call(sum_body, shape((loss, cols), bf16), [vmem()] * 2)(keep, swapped(send))
    windows = nz.bit_length() - 1
    attention = [None] * heads
    for k in range(windows):
        got = crossed(half, 2**k)
        here = range(k, heads, windows)
        half, query_pos = lax.optimization_barrier((half, query_pos))
        made = [forward(j, query_pos) for j in here]
        half, made = lax.optimization_barrier((half, made))
        for j, result in zip(here, made):
            attention[j] = result
        half = call(sum_body, shape((loss, cols), bf16), [vmem()] * 2)(half, got)
    other = swapped(half)
    query_grad, key_grad, value_grad = call(
        functools.partial(backward_body, loss_per, heads, group),
        (
            shape((loss_per, query_width), bf16),
            shape((tokens, key_width), bf16),
            shape((tokens, key_width), bf16),
        ),
        [smem()] + [vmem()] * (3 + 3 * heads),
        [pltpu.VMEM((loss, query_width), f32)],
    )(place, half, other, packed_all, *jax.tree.leaves(attention))
    return (mean_loss.reshape(()), query_grad, key_grad, value_grad, resid_rows.T)


def solution(mesh):
    placed = (
        P("ctx", "vocab"),
        P(),
        P(("vocab", "ctx"), None),
        P(),
        P(),
        P(),
        P("ctx", "vocab"),
        P("ctx", "vocab"),
        P("ctx", "vocab"),
        P("vocab", "ctx"),
    )
    return jax.shard_map(
        per_device,
        mesh=mesh,
        in_specs=placed,
        out_specs=(P(), P("ctx", "vocab"), P("ctx", "vocab"), P("ctx", "vocab"), P("ctx", None)),
        check_vma=False,
    )
```

```python
import functools

import jax
import jax.numpy as jnp
from jax import lax
from jax.experimental import pallas as pl
from jax.experimental.pallas import tpu as pltpu
from jax.sharding import PartitionSpec as P

HEAD_SIZE = 128
CORES = 2
CHUNK = 512
SLOTS = 3
LANES = 128

norm_eps = 1e-06
grad_weight = 16.0
masked_fill = -1e30

f32 = jnp.float32
bf16 = jnp.bfloat16

NT = (((1,), (1,)), ((), ()))
NN = (((1,), (0,)), ((), ()))
TN = (((0,), (0,)), ((), ()))


def dot(a, b, dims):
    return lax.dot_general(a, b, dims, preferred_element_type=f32)


def smem():
    return pl.BlockSpec(memory_space=pltpu.SMEM)


def hbm():
    return pl.BlockSpec(memory_space=pltpu.HBM)


def vmem():
    return pl.BlockSpec(memory_space=pltpu.VMEM)


def shape(dims, dtype):
    return jax.ShapeDtypeStruct(dims, dtype)


def call(body, outs, ins, scratch=(), limit=16, flops=0, moved=0, exps=0):
    return pl.pallas_call(
        body,
        out_shape=outs,
        in_specs=ins,
        out_specs=jax.tree.map(lambda _: vmem(), outs),
        scratch_shapes=list(scratch),
        compiler_params=pltpu.CompilerParams(vmem_limit_bytes=limit * 2**20),
        cost_estimate=pl.CostEstimate(flops=flops, bytes_accessed=moved, transcendentals=exps),
    )


def shifted(value, axis, step, inner=1):
    size = lax.axis_size(axis)
    outer = size // inner
    pairs = [(i, ((i // inner + step) % outer) * inner + i % inner) for i in range(size)]
    return lax.ppermute(value, axis, pairs)


def crossed(value, bit):
    size = lax.axis_size("ctx")
    return lax.ppermute(value, "ctx", [(i, i ^ (bit * CORES)) for i in range(size)])


def swapped(value):
    size = lax.axis_size("ctx")
    return lax.ppermute(value, "ctx", [(i, i ^ 1) for i in range(size)])


def row_choice(loss_per, tokens, place, rows):
    base = place[3] * loss_per
    row_iota = lax.broadcasted_iota(jnp.int32, (loss_per, tokens), 0)
    col_iota = lax.broadcasted_iota(jnp.int32, (loss_per, tokens), 1)
    sel = jnp.zeros((loss_per, tokens), f32)
    for j in range(loss_per):
        sel = jnp.where((row_iota == j) & (col_iota == rows[base + j]), 1.0, sel)
    return sel.astype(bf16)


def pick_body(loss_per, place, rows, hidden, picked, here, sem):
    tokens, width = hidden.shape
    copy = pltpu.make_async_copy(hidden, here, sem)
    copy.start()
    choice = row_choice(loss_per, tokens, place, rows)
    copy.wait()
    mine = dot(choice, here[...], NN)
    half = width // 2
    picked[...] = jnp.concatenate([mine[:, :half], mine[:, half:]], axis=0).astype(bf16)


def pack_body(loss_per, place, rows, queries, keys, values, packed):
    tokens, key_width = keys.shape
    mine = dot(row_choice(loss_per, tokens, place, rows), queries[...], NN)
    packed[0:tokens, 0:key_width] = keys[...]
    packed[0:tokens, key_width : 2 * key_width] = values[...]
    parts = queries.shape[1] // (2 * key_width)
    stacked = [mine[:, b * 2 * key_width : (b + 1) * 2 * key_width] for b in range(parts)]
    packed[tokens : tokens + parts * loss_per, :] = jnp.concatenate(stacked, axis=0).astype(bf16)


def target_body(place, targets, weight, out, buf, spots, sems):
    blocks, loss, block_width = out.shape
    width = blocks * block_width
    total_rows = weight.shape[0]
    offset = targets[...] - place[4]
    local = (offset >= 0) & (offset < total_rows)
    offset = offset.astype(f32)
    index = lax.broadcasted_iota(jnp.int32, (1, loss), 1).astype(f32)
    none = float(loss)
    count = jnp.sum(jnp.where(local, 1.0, 0.0)).astype(jnp.int32)

    def copy(k, at):
        start = pl.multiple_of(lax.div(at, 16) * 16, 16)
        return pltpu.make_async_copy(weight.at[pl.ds(start, 16), :], buf.at[k], sems.at[k])

    def begin(k, left):
        spot = jnp.min(left)
        at = jnp.sum(jnp.where(index == spot, offset, 0.0)).astype(jnp.int32)
        spots[0, k] = spot.astype(jnp.int32)
        spots[1, k] = at
        copy(k, at).start()
        return jnp.where(index == spot, none, left)

    lax.fori_loop(0, count, begin, jnp.where(local, index, none))
    out[...] = jnp.zeros_like(out)
    line = lax.broadcasted_iota(jnp.int32, (16, block_width), 0)

    @pl.loop(0, count)
    def _(k):
        spot, at = spots[0, k], spots[1, k]
        copy(k, at).wait()
        group = pl.ds(pl.multiple_of(lax.div(spot, 16) * 16, 16), 16)
        for b in range(blocks):
            block = buf[k, :, b * block_width : (b + 1) * block_width].astype(f32)
            row = jnp.sum(jnp.where(line == lax.rem(at, 16), block, 0.0), axis=0, keepdims=True)
            before = out[b, group, :].astype(f32)
            out[b, group, :] = jnp.where(line == lax.rem(spot, 16), row, before).astype(bf16)


def flash_body(
    first,
    place,
    own,
    other,
    gain,
    targets,
    weight,
    keep,
    send,
    stats,
    unit,
    normed,
    raw,
    acc,
    probs,
    state,
    head_buf,
    buf,
    head_sem,
    sems,
):
    vocab_at, z_at, core_at, ctx_at, first_id = (place[k] for k in range(5))
    nv, nz = own.shape[0], own.shape[1]
    loss, width = normed.shape
    half = own.shape[3]
    total_rows = weight.shape[0]
    chunks = (total_rows - first) // CHUNK
    blocks = acc.shape[0]
    block_width = width // blocks

    def head_copy():
        return pltpu.make_async_copy(weight.at[pl.ds(0, first), :], head_buf, head_sem)

    def body_copy(c):
        slot = lax.rem(c, SLOTS)
        start = pl.multiple_of(first + c * CHUNK, 16)
        return pltpu.make_async_copy(
            weight.at[pl.ds(start, CHUNK), :], buf.at[slot], sems.at[slot]
        )

    head_copy().start()
    for c in range(min(SLOTS, chunks)):
        body_copy(c).start()

    is_even = core_at == 0
    for zr in range(nz):
        z_src = lax.rem(z_at - zr + nz, nz)
        square_own = jnp.zeros((8, 1), f32)
        square_other = jnp.zeros((8, 1), f32)
        for vr in range(nv):
            a = own[vr, zr].astype(f32)
            b = other[vr, zr].astype(f32)
            square_a = jnp.sum(a * a, axis=1, keepdims=True)
            square_b = jnp.sum(b * b, axis=1, keepdims=True)
            square_own += square_a[:8] + square_a[8:]
            square_other += square_b[:8] + square_b[8:]
        square = jnp.concatenate(
            [
                jnp.where(is_even, square_own, square_other),
                jnp.where(is_even, square_other, square_own),
            ],
            axis=0,
        )
        inv = lax.rsqrt(square / width + norm_eps)
        row_at = pl.multiple_of(z_src * 16, 16)
        state[pl.ds(row_at, 16), :] = jnp.broadcast_to(inv, (16, LANES))
        for vr in range(nv):
            v_src = lax.rem(vocab_at - vr + nv, nv)
            a = own[vr, zr].astype(f32)
            b = other[vr, zr].astype(f32)
            low = jnp.where(is_even, a, b)
            high = jnp.where(is_even, b, a)
            for k in range(2):
                x = jnp.concatenate([low[8 * k : 8 * k + 8], high[8 * k : 8 * k + 8]], axis=0)
                lane_at = pl.multiple_of((v_src * 2 + k) * half, half)
                raw[pl.ds(row_at, 16), pl.ds(lane_at, half)] = x.astype(bf16)
                normed[pl.ds(row_at, 16), pl.ds(lane_at, half)] = (
                    x * inv * gain[:, pl.ds(lane_at, half)]
                ).astype(bf16)

    per_vocab = loss // nv
    mine_at = pl.multiple_of(vocab_at * per_vocab, per_vocab)
    feature_at = pl.multiple_of(ctx_at * block_width, block_width)
    unit[...] = (
        raw[pl.ds(mine_at, per_vocab), pl.ds(feature_at, block_width)].astype(f32)
        * state[pl.ds(mine_at, per_vocab), 0:1]
    )

    target_col = targets[...]

    def softmax(scores, base, before):
        cols = scores.shape[1]
        ids = base + lax.broadcasted_iota(jnp.int32, (loss, cols), 1)
        hit = ids == target_col
        top = jnp.max(scores, axis=1, keepdims=True)
        if before is not None:
            top = jnp.maximum(top, before[0])
        shifted_scores = scores - top
        weights = jnp.exp(shifted_scores)
        total = jnp.sum(weights, axis=1, keepdims=True)
        moment = jnp.sum(weights * shifted_scores, axis=1, keepdims=True)
        logit = jnp.sum(jnp.where(hit, scores, 0.0), axis=1, keepdims=True)
        scale = None
        if before is not None:
            gap = before[0] - top
            scale = jnp.exp(gap)
            total = total + before[1] * scale
            moment = moment + scale * (before[2] + gap * before[1])
            logit = logit + before[3]
        masked = jnp.where(hit, 0.0, weights).astype(bf16)
        return masked, scale, (top, total, moment, logit)

    def scores_of(block):
        return dot(block, normed[...], NT).T

    def add_product(p, scale, read):
        for b in range(blocks):
            part = dot(p, read(b * block_width, block_width), NN)
            if scale is None:
                acc[b] = part
            else:
                acc[b] = acc[b] * scale + part

    def part(ref, slot):
        return lambda at, n: ref[slot, :, at : at + n]

    head_copy().wait()
    p, _, run = softmax(scores_of(head_buf[...]), first_id, None)
    if not chunks:
        add_product(p, None, lambda at, n: head_buf[:, at : at + n])
    else:
        def start_of(c):
            return first_id + first + c * CHUNK

        body_copy(0).wait()
        scores = scores_of(buf[0])
        add_product(p, None, lambda at, n: head_buf[:, at : at + n])
        p, scale, run = softmax(scores, start_of(0), run)
        probs[...] = p

        def step(c, carry):
            scale, run = carry
            body_copy(c).wait()
            scores = scores_of(buf[lax.rem(c, SLOTS)])
            add_product(probs[...], scale, part(buf, lax.rem(c - 1, SLOTS)))
            p, scale, run = softmax(scores, start_of(c), run)
            probs[...] = p

            @pl.when(c + 2 < chunks)
            def _():
                body_copy(c + 2).start()

            return scale, run

        scale, run = lax.fori_loop(1, chunks, step, (scale, run))
        add_product(probs[...], scale, part(buf, (chunks - 1) % SLOTS))

    for z in range(nz):
        keep[z] = acc[CORES * z + core_at]
        send[:, z * block_width : (z + 1) * block_width] = acc[CORES * z + 1 - core_at].astype(bf16)
    send[:, nz * block_width :] = split_columns(run)
    stats[...] = with_stats(state[...], run)


def split_columns(columns):
    rows = columns[0].shape[0]
    lane = lax.broadcasted_iota(jnp.int32, (rows, LANES), 1)
    table = jnp.zeros((rows, LANES), f32)
    for k, column in enumerate(columns):
        rest = column
        for j in range(3):
            term = rest.astype(bf16).astype(f32)
            table = jnp.where(lane == 3 * k + j, term, table)
            rest = rest - term
    return table.astype(bf16)


def joined_columns(block, count):
    block = block.astype(f32)
    return [
        block[:, 3 * k : 3 * k + 1] + block[:, 3 * k + 1 : 3 * k + 2] + block[:, 3 * k + 2 : 3 * k + 3]
        for k in range(count)
    ]


def stats_of(table):
    return [table[:, k : k + 1] for k in range(4)]


def merge_stats(columns):
    top = functools.reduce(jnp.maximum, [c[0] for c in columns])
    gaps = [c[0] - top for c in columns]
    scales = [jnp.exp(g) for g in gaps]
    total = sum(s * c[1] for s, c in zip(scales, columns))
    moment = sum(s * (c[2] + g * c[1]) for s, g, c in zip(scales, gaps, columns))
    logit = sum(c[3] for c in columns)
    return scales, (top, total, moment, logit)


def with_stats(table, merged):
    lane = lax.broadcasted_iota(jnp.int32, table.shape, 1)
    for k in range(4):
        table = jnp.where(lane == k, merged[k], table)
    return table


def core_body(count, place, keep, got, mine, target_rows, new_stats, new_keep, new_rows, *rest):
    sends, (total, table, message) = rest[:count], rest[count:]
    nz, loss, block = keep.shape
    columns = [stats_of(mine[...]), joined_columns(got[:, nz * block :], 4)]
    scales, merged = merge_stats(columns)
    table[...] = with_stats(mine[...], merged)
    message[...] = split_columns(merged)
    per = loss // (count + 1)
    for z in range(nz):
        other = got[:, z * block : (z + 1) * block].astype(f32)
        total[z] = keep[z] * scales[0] + other * scales[1]
    at = pl.multiple_of(place[0] * per, per)
    new_stats[...] = table[pl.ds(at, per), :]
    new_keep[...] = total[:, pl.ds(at, per), :]
    for s in range(count):
        to = lax.rem(place[0] + s + 1, count + 1)
        rows = pl.ds(pl.multiple_of(to * per, per), per)
        for z in range(nz):
            sends[s][:, z * block : (z + 1) * block] = total[z, rows, :].astype(bf16)
        sends[s][:, (nz + 1) * block :] = message[rows, :]
    for s in range(count):
        to = lax.rem(place[0] + s + 1, count + 1)
        rows = pl.ds(pl.multiple_of(to * per, per), per)
        sends[s][:, nz * block : (nz + 1) * block] = target_rows[rows, :]
    new_rows[...] = target_rows[pl.ds(at, per), :]


def plane_body(count, place, keep, mine, target_rows, *rest):
    got, rest = rest[:count], rest[count:]
    new_stats, new_keep, new_target = rest[:3]
    sends, (total,) = rest[3:-1], rest[-1:]
    nz, per, block = keep.shape
    columns = [stats_of(mine[...])] + [joined_columns(g[:, (nz + 1) * block :], 4) for g in got]
    scales, merged = merge_stats(columns)
    new_stats[...] = with_stats(mine[...], merged)
    message = split_columns(merged)
    for z in range(nz):
        value = keep[z] * scales[0]
        for k in range(count):
            value = value + got[k][:, z * block : (z + 1) * block].astype(f32) * scales[k + 1]
        total[z] = value
    new_keep[...] = total[place[1]]
    rows = target_rows[...].astype(f32)
    for k in range(count):
        rows = rows + got[k][:, nz * block : (nz + 1) * block].astype(f32)
    new_target[...] = rows.astype(bf16)
    for s in range(nz - 1):
        sends[s][:, :block] = total[lax.rem(place[1] + s + 1, nz)].astype(bf16)
        sends[s][:, block:] = message


def line_body(count, width, place, keep, mine, target_rows, unit, gain, *rest):
    got, (message,) = rest[:count], rest[count:]
    per, block = keep.shape
    columns = [stats_of(mine[...])] + [joined_columns(g[:, block:], 4) for g in got]
    scales, (top, total, moment, logit) = merge_stats(columns)
    log_total = top + jnp.log(total)
    value = keep[...] * (scales[0] / total)
    for k in range(count):
        value = value + got[k][:, :block].astype(f32) * (scales[k + 1] / total)
    inner = grad_weight * (moment / total + (top - logit)) / width
    short = jnp.exp(logit - log_total) - 1.0
    inv = mine[:, 4:5]
    grad = grad_weight * (value + short * target_rows[...].astype(f32))
    gain_at = pl.multiple_of(place[3] * block, block)
    scaled = grad * gain[:, pl.ds(gain_at, block)]
    message[:, :block] = (inv * (scaled - unit[...] * inner)).astype(bf16)
    message[:, block:] = split_columns([log_total - logit])


def project_body(nv, place, *refs):
    gathered, refs = refs[:nv], refs[nv:]
    weight, resid, loss_out, keep, send, whole, partial = refs
    per = gathered[0].shape[0]
    block = whole.shape[1]
    loss_sum = jnp.zeros((1, 1), f32)
    for v in range(nv):
        src = lax.rem(place[0] - v + nv, nv)
        whole[pl.ds(pl.multiple_of(src * per, per), per), :] = gathered[v][:, :block]
        (column,) = joined_columns(gathered[v][:, block:], 1)
        loss_sum = loss_sum + jnp.sum(column, axis=0, keepdims=True)
    loss_out[...] = loss_sum / (nv * per)
    resid[...] = whole[...]
    partial[...] = dot(whole[...], weight[...], NT)
    cols = keep.shape[1]
    keep[...] = partial[:, pl.ds(pl.multiple_of(place[2] * cols, cols), cols)]
    send[...] = partial[:, pl.ds(pl.multiple_of((1 - place[2]) * cols, cols), cols)].astype(bf16)


def stage_body(source, staged, sem):
    copy = pltpu.make_async_copy(source, staged, sem)
    copy.start()
    copy.wait()


def staged(value):
    return call(
        stage_body,
        shape(value.shape, value.dtype),
        [hbm()],
        [pltpu.SemaphoreType.DMA],
        moved=2 * value.size * value.dtype.itemsize,
    )(value)


def sum_body(keep, *refs):
    value = keep[...].astype(f32)
    for ref in refs[:-1]:
        value = value + ref[...].astype(f32)
    refs[-1][...] = value.astype(bf16)


def forward_body(
    loss_per, heads, group, heads_at_once, j, place, key_pos, query_pos, packed, p_own, p_rows, out, scratch
):
    nc = packed.shape[0]
    tokens = p_own.shape[1]
    loss = loss_per * nc
    key_width = heads * HEAD_SIZE
    score_scale = HEAD_SIZE ** (-0.5)
    ctx_at = place[3]
    own_at = pl.multiple_of(ctx_at * tokens, tokens)
    row_at = pl.multiple_of(ctx_at * loss_per, loss_per)
    key = jnp.concatenate(
        [packed[c, 0:tokens, j * HEAD_SIZE : (j + 1) * HEAD_SIZE] for c in range(nc)], axis=0
    )
    at = key_width + j * HEAD_SIZE
    value = jnp.concatenate(
        [packed[c, 0:tokens, at : at + HEAD_SIZE] for c in range(nc)], axis=0
    )
    for g0 in range(0, group, heads_at_once):
        stacked = []
        for g in range(g0, g0 + heads_at_once):
            stacked.append(query_of(packed, j * group + g, tokens, loss_per, key_width))
        query = jnp.concatenate(stacked, axis=0).astype(bf16)
        where_at = jnp.concatenate([query_pos[...]] * heads_at_once, axis=0)
        visible = key_pos[...] <= where_at
        scores = jnp.where(visible, dot(query, key, NT) * score_scale, masked_fill)
        top = jnp.max(scores, axis=1, keepdims=True)
        raw = jnp.where(visible, jnp.exp(scores - top), 0.0)
        prob = raw / jnp.sum(raw, axis=1, keepdims=True)
        scratch[...] = prob
        coarse = prob.astype(bf16)
        fine = (prob - coarse.astype(f32)).astype(bf16)
        first = g0 * loss
        n = heads_at_once * loss
        out[first : first + n, :] = dot(coarse, value, NN) + dot(fine, value, NN)
        p_own[first : first + n, :] = scratch[:, pl.ds(own_at, tokens)]
        for k in range(heads_at_once):
            p_rows[(g0 + k) * loss_per : (g0 + k + 1) * loss_per, :] = scratch[
                pl.ds(pl.multiple_of(k * loss + row_at, loss_per), loss_per), :
            ]


def query_of(packed, head, tokens, loss_per, key_width):
    lane = head * HEAD_SIZE
    b, at = lane // (2 * key_width), lane % (2 * key_width)
    parts = []
    for c in range(packed.shape[0]):
        block = packed[c, tokens:, at : at + HEAD_SIZE].astype(f32)
        parts.append(block[b * loss_per : (b + 1) * loss_per])
    return jnp.concatenate(parts, axis=0)


def backward_body(loss_per, heads, group, place, half, other, packed, *refs):
    attention = [refs[3 * j : 3 * j + 3] for j in range(heads)]
    query_grad, key_grad, value_grad, grad = refs[3 * heads :]
    nc = packed.shape[0]
    tokens = key_grad.shape[0]
    loss = loss_per * nc
    key_width = heads * HEAD_SIZE
    score_scale = HEAD_SIZE ** (-0.5)
    ctx_at = place[3]
    cols = half.shape[1]
    grad[:, pl.ds(pl.multiple_of(place[2] * cols, cols), cols)] = half[...].astype(f32)
    grad[:, pl.ds(pl.multiple_of((1 - place[2]) * cols, cols), cols)] = other[...].astype(f32)
    mine_at = pl.multiple_of(ctx_at * loss_per, loss_per)
    for j in range(heads):
        p_own, p_rows, out = attention[j]
        lanes = [slice((j * group + g) * HEAD_SIZE, (j * group + g + 1) * HEAD_SIZE) for g in range(group)]
        d_out = jnp.concatenate([grad[:, s] for s in lanes], axis=0)
        d_half = d_out.astype(bf16)
        delta = jnp.sum(d_out * out[...], axis=1, keepdims=True)
        query = jnp.concatenate(
            [query_of(packed, j * group + g, tokens, loss_per, key_width) for g in range(group)], axis=0
        ).astype(bf16)
        at = key_width + j * HEAD_SIZE
        own_value = packed[ctx_at, 0:tokens, at : at + HEAD_SIZE]
        prob = p_own[...]
        score_grad = (prob * (dot(d_half, own_value, NT) - delta)).astype(bf16)
        k_lanes = slice(j * HEAD_SIZE, (j + 1) * HEAD_SIZE)
        key_grad[:, k_lanes] = (dot(score_grad, query, TN) * score_scale).astype(bf16)
        value_grad[:, k_lanes] = dot(prob.astype(bf16), d_half, TN).astype(bf16)
        key = jnp.concatenate([packed[c, 0:tokens, k_lanes] for c in range(nc)], axis=0)
        value = jnp.concatenate([packed[c, 0:tokens, at : at + HEAD_SIZE] for c in range(nc)], axis=0)
        d_mine = jnp.concatenate([grad[pl.ds(mine_at, loss_per), s] for s in lanes], axis=0)
        out_mine = jnp.concatenate(
            [
                out[pl.ds(pl.multiple_of(g * loss + mine_at, loss_per), loss_per), :]
                for g in range(group)
            ],
            axis=0,
        )
        delta = jnp.sum(d_mine * out_mine, axis=1, keepdims=True)
        d_prob = dot(d_mine.astype(bf16), value, NT)
        score_grad = (p_rows[...] * (d_prob - delta)).astype(bf16)
        result = dot(score_grad, key, NN) * score_scale
        for g in range(group):
            query_grad[:, lanes[g]] = result[g * loss_per : (g + 1) * loss_per].astype(bf16)


def per_device(
    hidden,
    norm_gain,
    head_weight,
    targets,
    loss_rows,
    stretch_of_slot,
    queries,
    key_states,
    attention_values,
    output_weight,
):
    nc = lax.axis_size("ctx")
    nv = lax.axis_size("vocab")
    nz = nc // CORES
    ctx_at = lax.axis_index("ctx")
    vocab_at = lax.axis_index("vocab")
    tokens = hidden.shape[0]
    stretch_len = tokens // 2
    loss = loss_rows.shape[0]
    loss_per = loss // nc
    width = norm_gain.shape[0]
    voc_rows = head_weight.shape[0]
    part_width = hidden.shape[1]
    query_width = queries.shape[1]
    key_width = key_states.shape[1]
    heads = key_width // HEAD_SIZE
    group = query_width // key_width
    block_width = width // nc
    per_vocab = loss // nv
    all_tokens = tokens * nc

    first_id = (vocab_at * nc + ctx_at) * voc_rows
    place = jnp.stack([vocab_at, ctx_at // CORES, ctx_at % CORES, ctx_at, first_id]).astype(jnp.int32)

    slots = stretch_of_slot.shape[0]
    owner = lax.broadcasted_iota(jnp.int32, (loss, 1), 0) // loss_per
    slot = 2 * owner + loss_rows[:, None] // stretch_len
    slot_iota = lax.broadcasted_iota(jnp.int32, (1, slots), 1)
    stretch = jnp.sum(jnp.where(slot == slot_iota, stretch_of_slot[None, :], 0), axis=1, keepdims=True)
    query_pos = stretch * stretch_len + loss_rows[:, None] % stretch_len
    key_pos = (
        stretch_of_slot[:, None] * stretch_len
        + lax.broadcasted_iota(jnp.int32, (1, stretch_len), 1)
    ).reshape(1, all_tokens)
    picked = call(
        functools.partial(pick_body, loss_per),
        shape((2 * loss_per, part_width // 2), bf16),
        [smem(), smem(), hbm()],
        [pltpu.VMEM((tokens, part_width), bf16), pltpu.SemaphoreType.DMA],
    )(place, loss_rows, hidden)
    picked, queries, targets_late = lax.optimization_barrier((picked, queries, targets))
    extra = (query_width // (2 * key_width)) * loss_per
    packed = call(
        functools.partial(pack_body, loss_per),
        shape((tokens + extra, 2 * key_width), bf16),
        [smem(), smem()] + [vmem()] * 3,
        moved=2 * queries.size,
    )(place, loss_rows, queries, key_states, attention_values)
    by_z = jnp.stack([picked] + [shifted(picked, "ctx", s, CORES) for s in range(1, nz)])
    planes = [by_z] + [shifted(by_z, "vocab", s) for s in range(1, nv)]
    if voc_rows % 16:
        local = targets_late - first_id
        is_local = (local >= 0) & (local < voc_rows)
        target_rows = head_weight.at[jnp.clip(local, 0, voc_rows - 1)].get(mode="promise_in_bounds")
        target_rows = jnp.where(is_local[:, None], target_rows, jnp.zeros((), bf16))
        target_rows = target_rows.reshape(loss, nc, block_width).transpose(1, 0, 2)
    else:
        target_rows = pl.pallas_call(
            target_body,
            out_shape=shape((nc, loss, block_width), bf16),
            in_specs=[smem(), vmem(), pl.BlockSpec(memory_space=pl.ANY)],
            out_specs=vmem(),
            scratch_shapes=[
                pltpu.VMEM((loss, 16, width), bf16),
                pltpu.SMEM((2, loss), jnp.int32),
                pltpu.SemaphoreType.DMA((loss,)),
            ],
            compiler_params=pltpu.CompilerParams(vmem_limit_bytes=40 * 2**20),
            cost_estimate=pl.CostEstimate(
                flops=0, bytes_accessed=2 * 16 * loss * width, transcendentals=0
            ),
        )(place, targets_late.reshape(1, loss), head_weight)
    planes, target_rows = lax.optimization_barrier((planes, target_rows))
    by_plane = jnp.stack(planes)
    other = swapped(by_plane)
    target_rows = lax.psum_scatter(
        target_rows.reshape(nc * loss, block_width), "ctx", scatter_dimension=0, tiled=True
    )
    other, packed = lax.optimization_barrier((other, packed))
    packed_all = lax.all_gather(packed, "ctx")

    first = voc_rows % CHUNK
    if voc_rows < SLOTS * CHUNK or first % 16 or not first:
        first = voc_rows if voc_rows < SLOTS * CHUNK else CHUNK
    chunks = (voc_rows - first) // CHUNK
    gain = norm_gain.reshape(1, width)
    keep, send, stats, unit = pl.pallas_call(
        functools.partial(flash_body, first),
        out_shape=(
            shape((nz, loss, block_width), f32),
            shape((loss, nz * block_width + LANES), bf16),
            shape((loss, LANES), f32),
            shape((per_vocab, block_width), f32),
        ),
        in_specs=[smem()] + [vmem()] * 4 + [pl.BlockSpec(memory_space=pl.ANY)],
        out_specs=[vmem()] * 4,
        scratch_shapes=[
            pltpu.VMEM((loss, width), bf16),
            pltpu.VMEM((loss, width), bf16),
            pltpu.VMEM((nc, loss, block_width), f32),
            pltpu.VMEM((loss, CHUNK), bf16),
            pltpu.VMEM((loss, LANES), f32),
            pltpu.VMEM((first, width), bf16),
            pltpu.VMEM((SLOTS if chunks else 1, CHUNK if chunks else 16, width), bf16),
            pltpu.SemaphoreType.DMA,
            pltpu.SemaphoreType.DMA((SLOTS,)),
        ],
        compiler_params=pltpu.CompilerParams(vmem_limit_bytes=45 * 2**20),
        cost_estimate=pl.CostEstimate(
            flops=4 * max(loss, 256) * width * voc_rows,
            bytes_accessed=4 * width * voc_rows,
            transcendentals=loss * voc_rows,
        ),
    )(place, by_plane, other, gain, targets.reshape(loss, 1), head_weight)

    send, target_rows = lax.optimization_barrier((send, target_rows))
    got = swapped(send)
    target_rows = staged(target_rows)
    stats, keep, target_rows, *sends = call(
        functools.partial(core_body, nv - 1),
        (
            shape((per_vocab, LANES), f32),
            shape((nz, per_vocab, block_width), f32),
            shape((per_vocab, block_width), bf16),
        )
        + (shape((per_vocab, (nz + 1) * block_width + LANES), bf16),) * (nv - 1),
        [smem()] + [vmem()] * 4,
        [
            pltpu.VMEM((nz, loss, block_width), f32),
            pltpu.VMEM((loss, LANES), f32),
            pltpu.VMEM((loss, LANES), bf16),
        ],
    )(place, keep, got, stats, target_rows)
    got = [shifted(sends[s - 1], "vocab", s) for s in range(1, nv)]

    at_once = max(1, min(group, (4 * 2**20) // (loss * all_tokens * 4)))

    def forward(j, query_pos):
        return call(
            functools.partial(forward_body, loss_per, heads, group, at_once, j),
            (
                shape((group * loss, tokens), f32),
                shape((group * loss_per, all_tokens), f32),
                shape((group * loss, HEAD_SIZE), f32),
            ),
            [smem()] + [vmem()] * 3,
            [pltpu.VMEM((at_once * loss, all_tokens), f32)],
            limit=40,
            flops=24 * group * loss * all_tokens * HEAD_SIZE,
            moved=2 * packed_all.size,
            exps=group * loss * all_tokens,
        )(place, key_pos, query_pos, packed_all)

    stats, packed_all = lax.optimization_barrier((stats, packed_all))
    stats, keep, target_rows, *sends = call(
        functools.partial(plane_body, nv - 1),
        (
            shape((per_vocab, LANES), f32),
            shape((per_vocab, block_width), f32),
            shape((per_vocab, block_width), bf16),
        )
        + (shape((per_vocab, block_width + LANES), bf16),) * (nz - 1),
        [smem()] + [vmem()] * (3 + nv - 1),
        [pltpu.VMEM((nz, per_vocab, block_width), f32)],
    )(place, keep, stats, target_rows, *got)
    got = [shifted(sends[s - 1], "ctx", s, CORES) for s in range(1, nz)]
    message = call(
        functools.partial(line_body, nz - 1, width),
        shape((per_vocab, block_width + LANES), bf16),
        [smem()] + [vmem()] * (5 + nz - 1),
    )(place, keep, stats, target_rows, unit, gain, *got)

    message, output_weight = lax.optimization_barrier((message, output_weight))
    weight_here = staged(output_weight)
    gathered = [message] + [shifted(message, "vocab", s) for s in range(1, nv)]
    cols = query_width // CORES
    resid_rows, mean_loss, keep, send = call(
        functools.partial(project_body, nv),
        (
            shape((loss, block_width), bf16),
            shape((1, 1), f32),
            shape((loss, cols), f32),
            shape((loss, cols), bf16),
        ),
        [smem()] + [vmem()] * (nv + 1),
        [pltpu.VMEM((loss, block_width), bf16), pltpu.VMEM((loss, query_width), f32)],
    )(place, *gathered, weight_here)
    half = call(sum_body, shape((loss, cols), bf16), [vmem()] * 2)(keep, swapped(send))
    windows = nz.bit_length() - 1
    attention = [None] * heads
    for k in range(windows):
        got = crossed(half, 2**k)
        here = range(k, heads, windows)
        half, query_pos = lax.optimization_barrier((half, query_pos))
        made = [forward(j, query_pos) for j in here]
        half, made = lax.optimization_barrier((half, made))
        for j, result in zip(here, made):
            attention[j] = result
        half = call(sum_body, shape((loss, cols), bf16), [vmem()] * 2)(half, got)
    other = swapped(half)
    query_grad, key_grad, value_grad = call(
        functools.partial(backward_body, loss_per, heads, group),
        (
            shape((loss_per, query_width), bf16),
            shape((tokens, key_width), bf16),
            shape((tokens, key_width), bf16),
        ),
        [smem()] + [vmem()] * (3 + 3 * heads),
        [pltpu.VMEM((loss, query_width), f32)],
    )(place, half, other, packed_all, *jax.tree.leaves(attention))
    return (mean_loss.reshape(()), query_grad, key_grad, value_grad, resid_rows.T)


def solution(mesh):
    placed = (
        P("ctx", "vocab"),
        P(),
        P(("vocab", "ctx"), None),
        P(),
        P(),
        P(),
        P("ctx", "vocab"),
        P("ctx", "vocab"),
        P("ctx", "vocab"),
        P("vocab", "ctx"),
    )
    return jax.shard_map(
        per_device,
        mesh=mesh,
        in_specs=placed,
        out_specs=(P(), P("ctx", "vocab"), P("ctx", "vocab"), P("ctx", "vocab"), P("ctx", None)),
        check_vma=False,
    )
```
